128 devices in a mesh: roll: 16 (over y_hi, z, core), tp: 8 (over y_lo, x).
Axes of the slice: x: 4, y: 4 (y_hi: 2, y_lo: 2; y = y_hi * 2 + y_lo), z: 4, core: 2. Of those that a mesh axis runs over, the one named last changes fastest.
Arguments:
- tokens: bfloat16 [64, 16, 4, 8192], P(None, 'roll', None, 'tp'), may hold values from -6 to 6
- query_weight: bfloat16 [8192, 8192], P('tp'), may hold values from -0.0625 to 0.0625
- query_bias: bfloat16 [8192], P('tp'), may hold values from -4 to 4
- pair_weight: bfloat16 [8192, 2048], P('tp'), may hold values from -0.0625 to 0.0625
- pair_bias: bfloat16 [2048], P('tp'), may hold values from -4 to 4
- cache_pairs: bfloat16 [64, 16, 64, 8, 256], P(None, 'roll', None, 'tp'), may hold values from -6 to 6
- prefix_pairs: bfloat16 [64, 512, 8, 256], P('roll', None, 'tp'), may hold values from -256 to 256
- owner_slot: int32 [64], replicated, may hold values from 0 to 63, each once
- prefix_blocks: int32 [64], replicated, may hold values from 1 to 4, as said below
- positions: int32 [64, 16], P(None, 'roll'), may hold values from 0 to 64, as said below
Outputs:
- attended: bfloat16 [64, 16, 4, 8192], P(None, 'roll', None, 'tp')
- new_pairs: bfloat16 [64, 16, 4, 8, 256], P(None, 'roll', None, 'tp')
The draws below stay inside these ranges and needn't reach their ends.
Inputs may be any that keep to these rules, and one draw needn't show every extreme that they name: owner_slot is a permutation of the prompts. `prefix_blocks`: some prompt has 4 blocks. The first positions[p, g] rows of cache_pairs[p, g] are filled; some sample has 64.
All inputs are finite; a program needn't handle non-finite values.
Results may differ from the reference program's by a relative error of at most 0.02.
Values may be sent and summed in bfloat16 or wider, within the bound.
No kernel may reach another device: no remote copies, remote signals or barrier semaphores. Data moves between devices by JAX's collectives and lax.ppermute only.
A program may use at most 128 MiB of HBM per device.

```python
import math
import jax
import jax.numpy as jnp
from jax import lax

D = 8192
H = 64
KVH = 8
HD = 128
GROUP = 16
NEW = 4
BLOCK = 128
PBLK = 4
CACHE = 64
PROMPTS = 64


def draw_prefix_pairs(key, part):
    key = jax.random.fold_in(key, 11)
    keys = jax.random.split(key, 1)
    shape = (PROMPTS, PBLK * BLOCK, KVH, 2 * HD)
    values = jnp.clip(jax.random.normal(keys[0], shape, jnp.float32), -6.0, 6.0)
    return values.astype(jnp.bfloat16)


def draw_prefix_blocks(key, part):
    key = jax.random.fold_in(key, 12)
    first_key, second_key = jax.random.split(key)
    counts = jax.random.randint(first_key, (PROMPTS,), 1, PBLK + 1)
    chosen = jax.random.randint(second_key, (), 0, PROMPTS)
    return jnp.where(jnp.arange(PROMPTS) == chosen, PBLK, counts).astype(jnp.int32)


def draw_positions(key, part):
    key = jax.random.fold_in(key, 13)
    first_key, second_key = jax.random.split(key)
    counts = jax.random.randint(first_key, (PROMPTS, GROUP), 0, CACHE + 1)
    chosen = jax.random.randint(second_key, (), 0, PROMPTS * GROUP)
    flat_index = jnp.arange(PROMPTS * GROUP).reshape(PROMPTS, GROUP)
    return jnp.where(flat_index == chosen, CACHE, counts).astype(jnp.int32)


def block_levels(stream_key, shape, cuts, smallest, largest):
    def one(position, blocks):
        draws = jax.random.uniform(jax.random.fold_in(jax.random.fold_in(stream_key, 6), position), (blocks,), jnp.float32, smallest / len(cuts), largest / len(cuts))
        return jnp.repeat(jnp.exp(draws), shape[position] // blocks).reshape((-1,) + (1,) * (len(shape) - position - 1))

    factor_of = one(*cuts[0])
    for cut in cuts[1:]:
        factor_of = factor_of * one(*cut)
    return factor_of


def normal_values(key, shape, deviation, bound, cuts=(), held_as=jnp.bfloat16):
    level = block_levels(key, shape, cuts, -0.22, 0.18) if cuts else 1.0
    values = jax.random.normal(key, shape, jnp.float32) * deviation * level
    return jnp.minimum(jnp.maximum(values, -bound), bound).astype(held_as)


def setup_inputs(seed: int = 0) -> dict:
    key_of = jax.random.split(jax.random.key(seed), 11)
    return {
        "tokens": normal_values(key_of[0], (PROMPTS, GROUP, NEW, D), 1.0, 6.0, ((1, 16), (3, 8))),
        "query_weight": normal_values(key_of[1], (D, H * HD), D ** -0.5, 0.0625, ((0, 8),)),
        "query_bias": normal_values(key_of[2], (H * HD,), 1.0, 4.0, ((0, 8),)),
        "pair_weight": normal_values(key_of[3], (D, 2 * KVH * HD), D ** -0.5, 0.0625, ((0, 8),)),
        "pair_bias": normal_values(key_of[4], (2 * KVH * HD,), 1.0, 4.0, ((0, 8),)),
        "cache_pairs": normal_values(key_of[5], (PROMPTS, GROUP, CACHE, KVH, 2 * HD), 1.0, 6.0, ((1, 16), (3, 8))),
        "prefix_pairs": draw_prefix_pairs(jax.random.fold_in(key_of[10], 71), 0),
        "owner_slot": jax.random.permutation(key_of[7], PROMPTS).astype(jnp.int32),
        "prefix_blocks": draw_prefix_blocks(jax.random.fold_in(key_of[10], 71), 0),
        "positions": draw_positions(jax.random.fold_in(key_of[10], 71), 0),
    }


rope_base = 1000000.0
neg_fill = -1.0e30


def rotate(values, where_at):
    half_dim = values.shape[-1] // 2
    frequency = jnp.exp(jnp.arange(half_dim, dtype=jnp.float32) * (-2.0 * math.log(rope_base) / values.shape[-1]))
    angles = where_at.astype(jnp.float32)[..., None] * frequency
    cosine = jnp.cos(angles)
    sine_part = jnp.sin(angles)
    leading = values[..., :half_dim]
    trailing = values[..., half_dim:]
    return jnp.concatenate([leading * cosine - trailing * sine_part, trailing * cosine + leading * sine_part], axis=-1)


def reference(tokens, query_weight, query_bias, pair_weight, pair_bias, cache_pairs, prefix_pairs, owner_slot, prefix_blocks, positions):
    per_group = H // KVH
    flat_rows = tokens.reshape(-1, D)
    query_full = jnp.dot(flat_rows, query_weight, preferred_element_type=jnp.float32) + query_bias.astype(jnp.float32)
    pair_full = jnp.dot(flat_rows, pair_weight, preferred_element_type=jnp.float32) + pair_bias.astype(jnp.float32)
    new_index = jnp.arange(NEW, dtype=jnp.int32)
    where_at = BLOCK * prefix_blocks[:, None, None] + positions[:, :, None] + new_index[None, None, :]
    queries = rotate(query_full.reshape(PROMPTS, GROUP, NEW, KVH, per_group, HD), where_at[..., None, None]).astype(jnp.bfloat16)
    pair_parts = pair_full.reshape(PROMPTS, GROUP, NEW, KVH, 2, HD)
    new_keys = rotate(pair_parts[..., 0, :], where_at[..., None])
    new_pairs = jnp.concatenate([new_keys, pair_parts[..., 1, :]], axis=-1).astype(jnp.bfloat16)
    prefix = jnp.take(prefix_pairs, owner_slot, axis=0)
    prefix_valid = jnp.arange(PBLK * BLOCK, dtype=jnp.int32)[None, :] < (BLOCK * prefix_blocks)[:, None]
    cache_valid = jnp.arange(CACHE, dtype=jnp.int32)[None, None, :] < positions[:, :, None]
    fresh_valid = new_index[:, None] >= new_index[None, :]
    scale_factor = HD ** -0.5

    def one_head(bundle):
        query_head, cache_head, fresh_head, prefix_head = bundle
        query_float = query_head.astype(jnp.float32)
        prefix_scores = jnp.einsum("pgnhd,pcd->pgnhc", query_float, prefix_head[..., :HD].astype(jnp.float32)) * scale_factor
        cache_scores = jnp.einsum("pgnhd,pgcd->pgnhc", query_float, cache_head[..., :HD].astype(jnp.float32)) * scale_factor
        fresh_scores = jnp.einsum("pgnhd,pgmd->pgnhm", query_float, fresh_head[..., :HD].astype(jnp.float32)) * scale_factor
        prefix_mask = prefix_valid[:, None, None, None, :]
        cache_mask = cache_valid[:, :, None, None, :]
        fresh_mask = fresh_valid[None, None, :, None, :]
        prefix_scores = jnp.where(prefix_mask, prefix_scores, neg_fill)
        cache_scores = jnp.where(cache_mask, cache_scores, neg_fill)
        fresh_scores = jnp.where(fresh_mask, fresh_scores, neg_fill)
        top = jnp.maximum(jnp.maximum(jnp.max(prefix_scores, -1), jnp.max(cache_scores, -1)), jnp.max(fresh_scores, -1))
        prefix_exp = jnp.where(prefix_mask, jnp.exp(prefix_scores - top[..., None]), 0.0)
        cache_exp = jnp.where(cache_mask, jnp.exp(cache_scores - top[..., None]), 0.0)
        fresh_exp = jnp.where(fresh_mask, jnp.exp(fresh_scores - top[..., None]), 0.0)
        total = jnp.sum(prefix_exp, -1) + jnp.sum(cache_exp, -1) + jnp.sum(fresh_exp, -1)
        prefix_probs = lax.optimization_barrier(prefix_exp.astype(jnp.bfloat16)).astype(jnp.float32)
        cache_probs = lax.optimization_barrier(cache_exp.astype(jnp.bfloat16)).astype(jnp.float32)
        fresh_probs = lax.optimization_barrier(fresh_exp.astype(jnp.bfloat16)).astype(jnp.float32)
        mixed = jnp.einsum("pgnhc,pcd->pgnhd", prefix_probs, prefix_head[..., HD:].astype(jnp.float32))
        mixed = mixed + jnp.einsum("pgnhc,pgcd->pgnhd", cache_probs, cache_head[..., HD:].astype(jnp.float32))
        mixed = mixed + jnp.einsum("pgnhm,pgmd->pgnhd", fresh_probs, fresh_head[..., HD:].astype(jnp.float32))
        return (mixed / total[..., None]).astype(jnp.bfloat16)

    stacked = lax.map(one_head, (jnp.moveaxis(queries, 3, 0), jnp.moveaxis(cache_pairs, 3, 0), jnp.moveaxis(new_pairs, 3, 0), jnp.moveaxis(prefix, 2, 0)))
    attended = jnp.moveaxis(stacked, 0, 3).reshape(PROMPTS, GROUP, NEW, H * HD)
    return attended, new_pairs
```

```python
import functools
import math

import jax
import jax.numpy as jnp
from jax import lax
from jax.experimental import pallas as pl
from jax.experimental.pallas import tpu as pltpu
from jax.sharding import PartitionSpec as P

BLOCK = 128
HD = 128
ROPE_BASE = 1000000.0
NEG = -1e30
SCALE = HD ** -0.5
F32 = jnp.float32
BF16 = jnp.bfloat16
VMEM = 48 * 1024 * 1024

X_GROUPS = [[0, 1, 2, 3], [4, 5, 6, 7]]
Y_SWAP = [(i, (i + 4) % 8) for i in range(8)]


def roll_index(y, z, c):
    return (y * 4 + z) * 2 + c


Z_GROUPS = [[roll_index(y, z, c) for z in range(4)] for y in range(2) for c in range(2)]
YH_SWAP = [(i, (i + 8) % 16) for i in range(16)]
CORE_SWAP = [(i, i ^ 1) for i in range(16)]


def dot(a, b, dims=((1,), (0,))):
    return lax.dot_general(a, b, (dims, ((), ())), preferred_element_type=F32)


def project_kernel(x_ref, wq_ref, wp_ref, o_ref):
    x = x_ref[...]
    width = wq_ref.shape[1]
    o_ref[0, :, :width] = dot(x, wq_ref[...]).astype(BF16)
    o_ref[0, :, width:] = dot(x, wp_ref[...]).astype(BF16)


def project(x, wq, wp):
    rows, depth = x.shape
    qw, pw = wq.shape[1] // 8, wp.shape[1] // 8
    dest = lambda g: (g % 2) * 4 + g // 2
    return pl.pallas_call(
        project_kernel,
        grid=(8,),
        in_specs=[
            pl.BlockSpec((rows, depth), lambda g: (0, 0)),
            pl.BlockSpec((depth, qw), lambda g: (0, dest(g))),
            pl.BlockSpec((depth, pw), lambda g: (0, dest(g))),
        ],
        out_specs=pl.BlockSpec((1, rows, qw + pw), lambda g: (g, 0, 0)),
        out_shape=jax.ShapeDtypeStruct((8, rows, qw + pw), BF16),
        compiler_params=pltpu.CompilerParams(vmem_limit_bytes=VMEM),
        cost_estimate=pl.CostEstimate(
            flops=2 * rows * depth * 8 * (qw + pw),
            bytes_accessed=2 * depth * 8 * (qw + pw),
            transcendentals=0,
        ),
        name="project",
    )(x, wq, wp)


def column_max_sum(scores):
    top = jnp.max(scores, -1, keepdims=True)
    weights = jnp.exp(scores - top)
    return top, weights, jnp.sum(weights, -1, keepdims=True)


def prefix_kernel(where_ref, limit_ref, q_ref, *refs):
    kvs, o_ref = refs[:-1], refs[-1]
    per = kvs[0].shape[0]
    slots = q_ref.shape[1]
    lane = lax.broadcasted_iota(jnp.int32, (128, 128), 1)
    stats = jnp.zeros((128, 128), F32)
    for b, kv in enumerate(kvs):

        def step(j, stats, b=b, kv=kv):
            at = where_ref[b] * per + j
            q = q_ref[:, at].reshape(128, HD)
            s = dot(q, kv[j, :, :HD], ((1,), (1,))) * SCALE
            col = lax.broadcasted_iota(jnp.int32, s.shape, 1)
            s = jnp.where(col < limit_ref[at], s, NEG)
            top, w, total = column_max_sum(s)
            o = dot(w.astype(BF16), kv[j, :, HD:]) / total
            o_ref[:, pl.ds(at, 1)] = o.astype(BF16).reshape(4, 1, 32, HD)
            rest = top + jnp.log(total)
            for part in range(3):
                piece = rest.astype(BF16).astype(F32)
                stats = jnp.where(lane == 3 * at + part, piece, stats)
                rest = rest - piece
            return stats

        stats = lax.fori_loop(0, per, step, stats, unroll=True)
    o_ref[:, slots] = stats.astype(BF16).reshape(4, 32, 128)


def prefix_attention(where, limits, q, kvs):
    slots = q.shape[1]
    return pl.pallas_call(
        prefix_kernel,
        in_specs=[pl.BlockSpec(memory_space=pltpu.SMEM)] * 2
        + [pl.BlockSpec(memory_space=pltpu.VMEM)] * (1 + len(kvs)),
        out_specs=pl.BlockSpec(memory_space=pltpu.VMEM),
        out_shape=jax.ShapeDtypeStruct((4, slots + 1, 32, 128), BF16),
        compiler_params=pltpu.CompilerParams(vmem_limit_bytes=VMEM),
        name="prefix_attention",
    )(where, limits, q, *kvs)


def cache_kernel(order_ref, pos_ref, q_ref, new_ref, c0, c1, c2, c3, o_ref, lse_ref):
    g = pl.program_id(0)
    caches = (c0, c1, c2, c3)
    q = q_ref[...].reshape(128, HD)
    keys = jnp.concatenate([c[0, :, :HD] for c in caches], 0)
    vals = jnp.concatenate([c[0, :, HD:] for c in caches], 0)
    s = dot(q, keys, ((1,), (1,))) * SCALE
    row = lax.broadcasted_iota(jnp.int32, s.shape, 0)
    col = lax.broadcasted_iota(jnp.int32, s.shape, 1)
    length = jnp.zeros(s.shape, jnp.int32)
    for i in range(4):
        length = jnp.where(row // 32 == i, pos_ref[order_ref[g * 4 + i]], length)
    s = jnp.where((row // 32 == col // 64) & (col % 64 < length), s, NEG)
    new = new_ref[...]
    f = dot(q, new[:, :HD], ((1,), (1,))) * SCALE
    row = lax.broadcasted_iota(jnp.int32, f.shape, 0)
    col = lax.broadcasted_iota(jnp.int32, f.shape, 1)
    f = jnp.where((row // 32 == col // 4) & (col % 4 <= row % 4), f, NEG)
    top = jnp.maximum(jnp.max(s, -1, keepdims=True), jnp.max(f, -1, keepdims=True))
    ws = jnp.exp(s - top)
    wf = jnp.exp(f - top)
    total = jnp.sum(ws, -1, keepdims=True) + jnp.sum(wf, -1, keepdims=True)
    o = dot(ws.astype(BF16), vals) + dot(wf.astype(BF16), new[:, HD:])
    o_ref[...] = o / total
    lse_ref[...] = jnp.broadcast_to(top + jnp.log(total), (128, HD))


def cache_attention(order, pos, q, new, cache):
    prompts = q.shape[0]
    spec = lambda i: pl.BlockSpec((1, 64, 2 * HD), lambda g, o, p, i=i: (o[g * 4 + i], 0, 0))
    flat = pl.BlockSpec((128, HD), lambda g, o, p: (g, 0))
    return pl.pallas_call(
        cache_kernel,
        grid_spec=pltpu.PrefetchScalarGridSpec(
            num_scalar_prefetch=2,
            grid=(prompts // 4,),
            in_specs=[
                pl.BlockSpec((4, 32, HD), lambda g, o, p: (g, 0, 0)),
                pl.BlockSpec((16, 2 * HD), lambda g, o, p: (g, 0)),
            ]
            + [spec(i) for i in range(4)],
            out_specs=[flat, flat],
        ),
        out_shape=[jax.ShapeDtypeStruct((prompts * 32, HD), F32)] * 2,
        compiler_params=pltpu.CompilerParams(vmem_limit_bytes=VMEM),
        name="cache_attention",
    )(order, pos, q, new, cache, cache, cache, cache)


def merge_kernel(order_ref, far_ref, o_ref, lse_ref, out_ref):
    z = pl.program_id(0)
    slots = far_ref.shape[1] - 1
    stats = far_ref[0, slots].astype(F32)
    for a in range(slots):
        far = jnp.sum(stats[:, 3 * a : 3 * a + 3], -1, keepdims=True)
        near = lse_ref[a * 32 : a * 32 + 32]
        top = jnp.maximum(far, near)
        wf, wn = jnp.exp(far - top), jnp.exp(near - top)
        o = (far_ref[0, a].astype(F32) * wf + o_ref[a * 32 : a * 32 + 32] * wn) / (wf + wn)
        o = jnp.concatenate([o[4 * h : 4 * h + 4] for h in range(8)], 1)
        out_ref[pl.ds(order_ref[z * slots + a], 1)] = o.astype(BF16)[None]


def merge(order, far, o, lse):
    slots = far.shape[1] - 1
    prompts = order.shape[0]
    flat = pl.BlockSpec((slots * 32, HD), lambda z, o: (z, 0))
    return pl.pallas_call(
        merge_kernel,
        grid_spec=pltpu.PrefetchScalarGridSpec(
            num_scalar_prefetch=1,
            grid=(4,),
            in_specs=[pl.BlockSpec((1, slots + 1, 32, HD), lambda z, o: (z, 0, 0, 0)), flat, flat],
            out_specs=pl.BlockSpec((prompts, 4, 8 * HD), lambda z, o: (0, 0, 0)),
        ),
        out_shape=jax.ShapeDtypeStruct((prompts, 4, 8 * HD), BF16),
        compiler_params=pltpu.CompilerParams(vmem_limit_bytes=VMEM),
        name="merge",
    )(order, far, o, lse)


def rotate(values, cosine, sine):
    half = values.shape[-1] // 2
    lead, trail = values[..., :half], values[..., half:]
    return jnp.concatenate([lead * cosine - trail * sine, trail * cosine + lead * sine], -1)


def on_device(
    tokens,
    query_weight,
    query_bias,
    pair_weight,
    pair_bias,
    cache_pairs,
    prefix_pairs,
    owner_slot,
    prefix_blocks,
    positions,
):
    prompts, _, new, width = tokens.shape
    rows = prompts * new
    me = lax.axis_index("roll")
    my_y, my_c = me // 8, me % 2
    my_tp_y = lax.axis_index("tp") // 4

    index = jnp.arange(prompts, dtype=jnp.int32)
    slot_prompt = jnp.sum(jnp.where(owner_slot[None, :] == index[:, None], index[None, :], 0), 1)
    order = slot_prompt.reshape(2, 4, 2, 4).transpose(1, 0, 2, 3).reshape(prompts)
    pos = positions.reshape(prompts)

    own = prefix_pairs.reshape(4, 512, 2 * HD)
    other = lax.ppermute(own, "roll", YH_SWAP)
    own_c = lax.ppermute(own, "roll", CORE_SWAP)
    other_c = lax.ppermute(other, "roll", CORE_SWAP)

    x = jnp.take(tokens.reshape(prompts, new * width), order, axis=0).reshape(rows, width)
    part = project(x, query_weight, pair_weight)
    cols = part.shape[-1]
    got = lax.all_to_all(
        part.reshape(4, 2 * rows, cols), "tp", 0, 0, tiled=True, axis_index_groups=X_GROUPS
    )
    half = jnp.sum(got.reshape(4, 2, rows, cols).astype(F32), 0)
    send = lax.dynamic_index_in_dim(half, 1 - my_tp_y, 0, keepdims=False).astype(BF16)
    keep = lax.dynamic_index_in_dim(half, my_tp_y, 0, keepdims=False)
    full = keep + lax.ppermute(send, "tp", Y_SWAP).astype(F32)

    at = (
        BLOCK * jnp.take(prefix_blocks, order)[:, None]
        + jnp.take(pos, order)[:, None]
        + jnp.arange(new, dtype=jnp.int32)[None, :]
    ).reshape(rows)
    frequency = jnp.exp(
        jnp.arange(HD // 2, dtype=F32) * (-2.0 * math.log(ROPE_BASE) / HD)
    )
    angles = at.astype(F32)[:, None] * frequency[None, :]
    cosine, sine = jnp.cos(angles), jnp.sin(angles)

    qw = 8 * HD
    q = (full[:, :qw] + query_bias.astype(F32)).reshape(rows, 8, HD)
    q = rotate(q, cosine[:, None], sine[:, None]).astype(BF16)
    q = q.reshape(prompts, new, 8, HD).transpose(0, 2, 1, 3).reshape(prompts, 32, HD)
    pair = full[:, qw:] + pair_bias.astype(F32)
    pair = jnp.concatenate([rotate(pair[:, :HD], cosine, sine), pair[:, HD:]], -1).astype(BF16)

    q_z = lax.all_to_all(
        q.reshape(4, 16, 32, HD), "roll", 0, 0, tiled=True, axis_index_groups=Z_GROUPS
    )
    where = jnp.stack(
        [(my_y ^ dy) * 2 + (my_c ^ dc) for dy, dc in ((0, 0), (1, 0), (0, 1), (1, 1))]
    ).astype(jnp.int32)
    limits = lax.dynamic_index_in_dim(
        (BLOCK * jnp.take(prefix_blocks, order)).reshape(4, 16), (me // 2) % 4, 0, keepdims=False
    )
    far = prefix_attention(where, limits, q_z, (own, other, own_c, other_c))
    far = lax.all_to_all(far, "roll", 0, 0, tiled=True, axis_index_groups=Z_GROUPS)

    near, near_lse = cache_attention(order, pos, q, pair, cache_pairs.reshape(prompts, 64, 2 * HD))
    attended = merge(order, far, near, near_lse)

    inverse = (
        owner_slot.reshape(-1) // 8 % 4 * 16
        + owner_slot // 32 * 8
        + owner_slot // 4 % 2 * 4
        + owner_slot % 4
    )
    new_pairs = jnp.take(pair.reshape(prompts, new, 2 * HD), inverse, axis=0)
    return (
        attended.reshape(prompts, 1, new, 8 * HD),
        new_pairs.reshape(prompts, 1, new, 1, 2 * HD),
    )


def solution(mesh):
    return jax.shard_map(
        on_device,
        mesh=mesh,
        in_specs=(
            P(None, "roll", None, "tp"),
            P("tp", None),
            P("tp"),
            P("tp", None),
            P("tp"),
            P(None, "roll", None, "tp", None),
            P("roll", None, "tp", None),
            P(),
            P(),
            P(None, "roll"),
        ),
        out_specs=(P(None, "roll", None, "tp"), P(None, "roll", None, "tp", None)),
        check_vma=False,
    )
```

```python
import math

import jax
import jax.numpy as jnp
from jax import lax
from jax.experimental import pallas as pl
from jax.experimental.pallas import tpu as pltpu
from jax.sharding import PartitionSpec as P

BLOCK = 128
HD = 128
HEADS = 8
QW = HEADS * HD
PW = 2 * HD
COLS = QW + PW
ROWS = 128
ROPE_BASE = 1000000.0
NEG = -1e30
SCALE = HD ** -0.5
F32 = jnp.float32
BF16 = jnp.bfloat16
VMEM = 50 * 1024 * 1024


def tp_shift(dy, dx):
    return [(y * 4 + x, (y + dy) % 2 * 4 + (x + dx) % 4) for y in range(2) for x in range(4)]


def roll_shift(dy, dz, dc):
    return [
        ((y * 4 + z) * 2 + c, ((y + dy) % 2 * 4 + (z + dz) % 4) * 2 + (c + dc) % 2)
        for y in range(2)
        for z in range(4)
        for c in range(2)
    ]


def over_tp(a, dy, dx):
    return lax.ppermute(a, "tp", tp_shift(dy, dx))


def over_roll(a, dy, dz, dc):
    return lax.ppermute(a, "roll", roll_shift(dy, dz, dc))


def dot(a, b, dims=((1,), (0,))):
    return lax.dot_general(a, b, (dims, ((), ())), preferred_element_type=F32)


ANY = pl.BlockSpec(memory_space=pl.ANY)
IN_VMEM = pl.BlockSpec(memory_space=pltpu.VMEM)
IN_SMEM = pl.BlockSpec(memory_space=pltpu.SMEM)


def project(heads, xs, wq, wp, groups):
    count = sum(len(g) for g in groups)
    depth = wq.shape[0]

    def kernel(heads_ref, *refs):
        x_refs, (wq_ref, wp_ref), rest = refs[: len(xs)], refs[len(xs) : len(xs) + 2], refs[len(xs) + 2 :]
        outs, (q_buf, p_buf, q_sem, p_sem) = rest[:-4], rest[-4:]
        copies = []
        for d in range(count):
            k = heads_ref[d]
            copies.append(
                (
                    pltpu.make_async_copy(
                        wq_ref.at[:, pl.ds(pl.multiple_of(k * QW, QW), QW)], q_buf.at[d], q_sem.at[d]
                    ),
                    pltpu.make_async_copy(
                        wp_ref.at[:, pl.ds(pl.multiple_of(k * PW, PW), PW)], p_buf.at[d], p_sem.at[d]
                    ),
                )
            )
        for pair in copies:
            for c in pair:
                c.start()
        x = jnp.concatenate([r[...] for r in x_refs], 0) if len(xs) > 1 else x_refs[0][...]
        d = 0
        for g, group in enumerate(groups):
            for i in range(len(group)):
                for c in copies[d]:
                    c.wait()
                for buf, low, high in ((q_buf, 0, QW), (p_buf, QW, COLS)):
                    y = dot(x, buf[d]).astype(BF16)
                    for b in range(len(xs)):
                        outs[b * len(groups) + g][i, :, low:high] = y[b * ROWS : (b + 1) * ROWS]
                d += 1

    return pl.pallas_call(
        kernel,
        in_specs=[IN_SMEM] + [IN_VMEM] * len(xs) + [ANY, ANY],
        out_specs=[IN_VMEM] * (len(xs) * len(groups)),
        out_shape=[jax.ShapeDtypeStruct((len(g), ROWS, COLS), BF16) for _ in xs for g in groups],
        scratch_shapes=[
            pltpu.VMEM((count, depth, QW), BF16),
            pltpu.VMEM((count, depth, PW), BF16),
            pltpu.SemaphoreType.DMA((count,)),
            pltpu.SemaphoreType.DMA((count,)),
        ],
        compiler_params=pltpu.CompilerParams(vmem_limit_bytes=VMEM),
        cost_estimate=pl.CostEstimate(
            flops=2 * len(xs) * ROWS * depth * count * COLS,
            bytes_accessed=2 * depth * count * COLS,
            transcendentals=0,
        ),
        name="project",
    )(heads, *xs, wq, wp)


def attend(limits, lengths, q, new, cache, kvs):
    flat = [a for group in kvs for a in group]

    def kernel(limit_ref, length_ref, q_ref, new_ref, cache_ref, *refs):
        kv_refs = refs[: len(flat)]
        o_ref, buf, cbuf, sem, csem = refs[len(flat) :]
        copies, at = [], 0
        for g, group in enumerate(kvs):
            mine, slot = [], 4 * g
            for a in group:
                n = a.shape[0]
                mine.append(pltpu.make_async_copy(kv_refs[at], buf.at[pl.ds(slot, n)], sem.at[at]))
                slot, at = slot + n, at + 1
            mine.append(
                pltpu.make_async_copy(cache_ref.at[pl.ds(4 * g, 4)], cbuf.at[pl.ds(4 * g, 4)], csem.at[g])
            )
            copies.append(mine)
        for mine in copies:
            for c in mine:
                c.start()
        for g in range(8):
            for c in copies[g]:
                c.wait()
            q = q_ref[4 * g : 4 * g + 4].reshape(128, HD)
            sp = []
            for i in range(4):
                p = 4 * g + i
                s = dot(q[32 * i : 32 * i + 32], buf[p, :, :HD], ((1,), (1,))) * SCALE
                col = lax.broadcasted_iota(jnp.int32, s.shape, 1)
                sp.append(jnp.where(col < limit_ref[p], s, NEG))
            sp = jnp.concatenate(sp, 0)
            sc = dot(q, cbuf[4 * g : 4 * g + 4, :, :HD].reshape(256, HD), ((1,), (1,))) * SCALE
            row = lax.broadcasted_iota(jnp.int32, sc.shape, 0)
            col = lax.broadcasted_iota(jnp.int32, sc.shape, 1)
            length = jnp.zeros(sc.shape, jnp.int32)
            for i in range(4):
                length = jnp.where(row // 32 == i, length_ref[4 * g + i], length)
            sc = jnp.where((row // 32 == col // 64) & (col % 64 < length), sc, NEG)
            new = new_ref[16 * g : 16 * g + 16]
            sn = dot(q, new[:, :HD], ((1,), (1,))) * SCALE
            row = lax.broadcasted_iota(jnp.int32, sn.shape, 0)
            col = lax.broadcasted_iota(jnp.int32, sn.shape, 1)
            sn = jnp.where((row // 32 == col // 4) & (col % 4 <= row % 4), sn, NEG)
            top = jnp.maximum(
                jnp.maximum(jnp.max(sp, -1, keepdims=True), jnp.max(sc, -1, keepdims=True)),
                jnp.max(sn, -1, keepdims=True),
            )
            wp, wc, wn = jnp.exp(sp - top), jnp.exp(sc - top), jnp.exp(sn - top)
            total = (
                jnp.sum(wp, -1, keepdims=True)
                + jnp.sum(wc, -1, keepdims=True)
                + jnp.sum(wn, -1, keepdims=True)
            )
            wp = wp.astype(BF16)
            o = jnp.concatenate(
                [dot(wp[32 * i : 32 * i + 32], buf[4 * g + i, :, HD:]) for i in range(4)], 0
            )
            o = o + dot(wc.astype(BF16), cbuf[4 * g : 4 * g + 4, :, HD:].reshape(256, HD))
            o = o + dot(wn.astype(BF16), new[:, HD:])
            o = o / total
            for i in range(4):
                o_ref[4 * g + i] = jnp.concatenate(
                    [o[32 * i + 4 * h : 32 * i + 4 * h + 4] for h in range(HEADS)], 1
                ).astype(BF16)

    return pl.pallas_call(
        kernel,
        in_specs=[IN_SMEM, IN_SMEM, IN_VMEM, IN_VMEM, ANY] + [ANY] * len(flat),
        out_specs=IN_VMEM,
        out_shape=jax.ShapeDtypeStruct((32, 4, QW), BF16),
        scratch_shapes=[
            pltpu.VMEM((32, 512, 2 * HD), BF16),
            pltpu.VMEM((32, 64, 2 * HD), BF16),
            pltpu.SemaphoreType.DMA((len(flat),)),
            pltpu.SemaphoreType.DMA((8,)),
        ],
        compiler_params=pltpu.CompilerParams(vmem_limit_bytes=VMEM),
        cost_estimate=pl.CostEstimate(
            flops=32 * 32 * 600 * 512, bytes_accessed=10 * 2**20, transcendentals=32 * 32 * 600
        ),
        name="attend",
    )(limits, lengths, q, new, cache, *flat)


def rotate(values, cosine, sine):
    half = values.shape[-1] // 2
    lead, trail = values[..., :half], values[..., half:]
    return jnp.concatenate([lead * cosine - trail * sine, trail * cosine + lead * sine], -1)


def finish(own, from_left, from_right):
    total = own.astype(F32) + from_left.astype(F32) + from_right.astype(F32)
    return total[0], total[1].astype(BF16)


def on_device(
    tokens,
    query_weight,
    query_bias,
    pair_weight,
    pair_bias,
    cache_pairs,
    prefix_pairs,
    owner_slot,
    prefix_blocks,
    positions,
):
    prompts, _, new, width = tokens.shape
    me = lax.axis_index("roll")
    my_y, my_z, my_c = me // 8, me // 2 % 4, me % 2
    tp = lax.axis_index("tp")
    tp_y, tp_x = tp // 4, tp % 4

    index = jnp.arange(prompts, dtype=jnp.int32)
    steps = jnp.array([0, 3, 1, 2], jnp.int32)
    half = jnp.arange(2, dtype=jnp.int32)
    y_of = (1 - half + my_y) % 2
    c_of = (half + my_c) % 2
    z_of = (steps + my_z) % 4
    slot = (
        ((y_of[:, None, None, None] * 4 + z_of[None, None, :, None]) * 2 + c_of[None, :, None, None]) * 4
        + jnp.arange(4, dtype=jnp.int32)[None, None, None, :]
    ).reshape(prompts)
    order = jnp.sum(jnp.where(owner_slot[None, :] == slot[:, None], index[None, :], 0), 1)
    inverse = jnp.sum(jnp.where(slot[None, :] == owner_slot[:, None], index[None, :], 0), 1)
    pos = positions.reshape(prompts)

    x = jnp.take(tokens.reshape(prompts, new * width), order, axis=0)
    pos_sorted = jnp.take(pos, order)
    blocks = jnp.take(prefix_blocks, order[32:])
    head_row = jnp.zeros((16, width), BF16).at[0, :32].set(pos_sorted[:32].astype(BF16))
    swapped = over_roll(
        jnp.concatenate([x[:32].reshape(ROWS, width), head_row], 0), 1, 0, 0
    )
    x_t, pos_t = swapped[:ROWS], swapped[ROWS, :32].astype(jnp.int32)
    x_g, pos_g = x[32:].reshape(ROWS, width), pos_sorted[32:]
    cache = cache_pairs.reshape(prompts, 64, 2 * HD)
    cache_t = over_roll(jnp.take(cache, order[:32], axis=0), 1, 0, 0)
    cache_g = jnp.take(cache, order[32:], axis=0)

    def heads(*pairs):
        return jnp.stack([(tp_y + dy) % 2 * 4 + (tp_x + dx) % 4 for dy, dx in pairs]).astype(jnp.int32)

    far = heads((0, 2), (1, 2))
    up_g, down_g = project(far, [x_g], query_weight, pair_weight, [[0], [1]])
    up_t, down_t = project(far, [x_t], query_weight, pair_weight, [[0], [1]])
    right_t, left_t, right_g, left_g = project(
        heads((0, 1), (1, 1), (0, 3), (1, 3)), [x_t, x_g], query_weight, pair_weight, [[0, 1], [2, 3]]
    )
    own_t, own_g = project(heads((0, 0), (1, 0)), [x_t, x_g], query_weight, pair_weight, [[0, 1]])

    def reduce(up, down, right, left, own):
        up, down = over_tp(up, 0, 1), over_tp(down, 0, 3)
        right = right.at[0].add(up[0])
        left = left.at[1].add(down[0])
        keep, send = finish(own, over_tp(right, 0, 1), over_tp(left, 0, 3))
        return keep + over_tp(send, 1, 0).astype(F32)

    full_t = reduce(up_t, down_t, right_t, left_t, own_t)
    full_g = reduce(up_g, down_g, right_g, left_g, own_g)

    own = prefix_pairs.reshape(4, 512, 2 * HD)
    below, above = over_roll(own, 0, 1, 0), over_roll(own, 0, 3, 0)
    far_a, far_b = over_roll(below[:2], 0, 1, 0), over_roll(above[2:], 0, 3, 0)
    kvs = [[own], [below], [above], [far_a, far_b]]
    kvs = kvs + [[over_roll(a, 0, 0, 1) for a in group] for group in kvs]

    frequency = jnp.exp(jnp.arange(HD // 2, dtype=F32) * (-2.0 * math.log(ROPE_BASE) / HD))
    limits = BLOCK * blocks

    def rows(full, where, cache):
        at = (limits[:, None] + where[:, None] + jnp.arange(new, dtype=jnp.int32)).reshape(ROWS)
        angles = at.astype(F32)[:, None] * frequency[None, :]
        cosine, sine = jnp.cos(angles), jnp.sin(angles)
        q = (full[:, :QW] + query_bias.astype(F32)).reshape(ROWS, HEADS, HD)
        q = rotate(q, cosine[:, None], sine[:, None]).astype(BF16)
        q = q.reshape(32, new, HEADS, HD).transpose(0, 2, 1, 3).reshape(32, 32, HD)
        pair = full[:, QW:] + pair_bias.astype(F32)
        pair = jnp.concatenate([rotate(pair[:, :HD], cosine, sine), pair[:, HD:]], -1).astype(BF16)
        return attend(limits, where, q, pair, cache, kvs), pair.reshape(32, new, PW)

    done_t, pair_t = rows(full_t, pos_t, cache_t)
    back = over_roll(jnp.concatenate([done_t, pair_t], -1), 1, 0, 0)
    done_g, pair_g = rows(full_g, pos_g, cache_g)

    attended = jnp.take(jnp.concatenate([back[..., :QW], done_g], 0), inverse, axis=0)
    new_pairs = jnp.take(jnp.concatenate([back[..., QW:], pair_g], 0), inverse, axis=0)
    return (
        attended.reshape(prompts, 1, new, QW),
        new_pairs.reshape(prompts, 1, new, 1, PW),
    )


def solution(mesh):
    return jax.shard_map(
        on_device,
        mesh=mesh,
        in_specs=(
            P(None, "roll", None, "tp"),
            P("tp", None),
            P("tp"),
            P("tp", None),
            P("tp"),
            P(None, "roll", None, "tp", None),
            P("roll", None, "tp", None),
            P(),
            P(),
            P(None, "roll"),
        ),
        out_specs=(P(None, "roll", None, "tp"), P(None, "roll", None, "tp", None)),
        check_vma=False,
    )
```

```python
import math

import jax
import jax.numpy as jnp
from jax import lax
from jax.experimental import pallas as pl
from jax.experimental.pallas import tpu as pltpu
from jax.sharding import PartitionSpec as P

BLOCK = 128
HD = 128
HEADS = 8
QW = HEADS * HD
PW = 2 * HD
COLS = QW + PW
ROWS = 128
ROPE_BASE = 1000000.0
NEG = -1e30
SCALE = HD ** -0.5
F32 = jnp.float32
BF16 = jnp.bfloat16
VMEM = 50 * 1024 * 1024


def tp_shift(dy, dx):
    return [(y * 4 + x, (y + dy) % 2 * 4 + (x + dx) % 4) for y in range(2) for x in range(4)]


def roll_shift(dy, dz, dc):
    return [
        ((y * 4 + z) * 2 + c, ((y + dy) % 2 * 4 + (z + dz) % 4) * 2 + (c + dc) % 2)
        for y in range(2)
        for z in range(4)
        for c in range(2)
    ]


def over_tp(a, dy, dx):
    return lax.ppermute(a, "tp", tp_shift(dy, dx))


def over_roll(a, dy, dz, dc):
    return lax.ppermute(a, "roll", roll_shift(dy, dz, dc))


def dot(a, b, dims=((1,), (0,))):
    return lax.dot_general(a, b, (dims, ((), ())), preferred_element_type=F32)


ANY = pl.BlockSpec(memory_space=pl.ANY)
IN_VMEM = pl.BlockSpec(memory_space=pltpu.VMEM)
IN_SMEM = pl.BlockSpec(memory_space=pltpu.SMEM)


def project(heads, xs, wq, wp, groups):
    count = sum(len(g) for g in groups)
    depth = wq.shape[0]

    def kernel(heads_ref, *refs):
        x_refs, (wq_ref, wp_ref), rest = refs[: len(xs)], refs[len(xs) : len(xs) + 2], refs[len(xs) + 2 :]
        outs, (q_buf, p_buf, q_sem, p_sem) = rest[:-4], rest[-4:]
        copies = []
        for d in range(count):
            k = heads_ref[d]
            copies.append(
                (
                    pltpu.make_async_copy(
                        wq_ref.at[:, pl.ds(pl.multiple_of(k * QW, QW), QW)], q_buf.at[d], q_sem.at[d]
                    ),
                    pltpu.make_async_copy(
                        wp_ref.at[:, pl.ds(pl.multiple_of(k * PW, PW), PW)], p_buf.at[d], p_sem.at[d]
                    ),
                )
            )
        for pair in copies:
            for c in pair:
                c.start()
        x = jnp.concatenate([r[:, :depth] for r in x_refs], 0)
        d = 0
        for g, group in enumerate(groups):
            for i in range(len(group)):
                for c in copies[d]:
                    c.wait()
                for buf, low, high in ((q_buf, 0, QW), (p_buf, QW, COLS)):
                    y = dot(x, buf[d]).astype(BF16)
                    for b in range(len(xs)):
                        outs[b * len(groups) + g][i, :, low:high] = y[b * ROWS : (b + 1) * ROWS]
                d += 1

    return pl.pallas_call(
        kernel,
        in_specs=[IN_SMEM] + [IN_VMEM] * len(xs) + [ANY, ANY],
        out_specs=[IN_VMEM] * (len(xs) * len(groups)),
        out_shape=[jax.ShapeDtypeStruct((len(g), ROWS, COLS), BF16) for _ in xs for g in groups],
        scratch_shapes=[
            pltpu.VMEM((count, depth, QW), BF16),
            pltpu.VMEM((count, depth, PW), BF16),
            pltpu.SemaphoreType.DMA((count,)),
            pltpu.SemaphoreType.DMA((count,)),
        ],
        compiler_params=pltpu.CompilerParams(vmem_limit_bytes=VMEM),
        cost_estimate=pl.CostEstimate(
            flops=2 * len(xs) * ROWS * depth * count * COLS,
            bytes_accessed=2 * depth * count * COLS,
            transcendentals=0,
        ),
        name="project",
    )(heads, *xs, wq, wp)


def sort_rows(place, owner, pos, tokens):
    rows, width = tokens.shape

    def kernel(place_ref, owner_ref, pos_ref, x_ref, *outs):
        x = x_ref[...]
        for b, out in enumerate(outs):
            row = lax.broadcasted_iota(jnp.int32, (ROWS, rows), 0)
            col = lax.broadcasted_iota(jnp.int32, (ROWS, rows), 1)
            i = row // 4
            y, c, step, j = (1 - b + place_ref[0]) % 2, i // 16, i // 4 % 4, i % 4
            c = jnp.where(c == 0, place_ref[2], 1 - place_ref[2])
            z = (step + place_ref[1]) % 4
            slot = ((y * 4 + z) * 2 + c) * 4 + j
            hit = (owner_ref[...] == slot) & (col % 4 == row % 4)
            at = jnp.sum(jnp.where(hit, pos_ref[...], 0.0), -1, keepdims=True)
            hit = jnp.where(hit, 1.0, 0.0).astype(BF16)
            out[:, :width] = dot(hit, x).astype(BF16)
            out[:, width:] = jnp.broadcast_to(at, (ROWS, 128)).astype(BF16)

    return pl.pallas_call(
        kernel,
        in_specs=[IN_SMEM, IN_VMEM, IN_VMEM, IN_VMEM],
        out_specs=[IN_VMEM] * 2,
        out_shape=[jax.ShapeDtypeStruct((ROWS, width + 128), BF16)] * 2,
        compiler_params=pltpu.CompilerParams(vmem_limit_bytes=VMEM),
        name="sort_rows",
    )(place, owner, pos, tokens)


def place_rows(order, first, second):
    def kernel(order_ref, a_ref, b_ref, o_ref, p_ref):
        for half, ref in enumerate((a_ref, b_ref)):

            def step(i, carry, half=half, ref=ref):
                at = order_ref[32 * half + i]
                o_ref[at] = ref[i, :, :QW]
                p_ref[at] = ref[i, :, QW:]
                return carry

            lax.fori_loop(0, 32, step, 0, unroll=8)

    return pl.pallas_call(
        kernel,
        in_specs=[IN_SMEM, IN_VMEM, IN_VMEM],
        out_specs=[IN_VMEM] * 2,
        out_shape=[jax.ShapeDtypeStruct((64, 4, QW), BF16), jax.ShapeDtypeStruct((64, 4, PW), BF16)],
        compiler_params=pltpu.CompilerParams(vmem_limit_bytes=VMEM),
        name="place_rows",
    )(order, first, second)


def sum_x(own, from_left, from_right):
    def kernel(a, b, c, keep, send):
        for i, out in enumerate((keep, send)):
            out[...] = (a[i].astype(F32) + b[i].astype(F32) + c[i].astype(F32)).astype(out.dtype)

    return pl.pallas_call(
        kernel,
        in_specs=[IN_VMEM] * 3,
        out_specs=[IN_VMEM] * 2,
        out_shape=[jax.ShapeDtypeStruct((ROWS, COLS), F32), jax.ShapeDtypeStruct((ROWS, COLS), BF16)],
        compiler_params=pltpu.CompilerParams(vmem_limit_bytes=VMEM),
        name="sum_x",
    )(own, from_left, from_right)


def attend(limits, lengths, cache_at, keep, more, bias, cosine, sine, cache, kvs):
    def kernel(
        limit_ref, length_ref, at_ref, keep_ref, more_ref, bias_ref, cos_ref, sin_ref, cache_ref, kv_a, kv_b,
        o_ref, buf, cbuf, qbuf, sem, csem,
    ):
        copies = []
        for g in range(8):
            kv = (kv_a, kv_b)[g // 4]
            mine = [pltpu.make_async_copy(kv.at[limit_ref[32 + g % 4]], buf.at[pl.ds(4 * g, 4)], sem.at[g])]
            for p in range(4 * g, 4 * g + 4):
                mine.append(pltpu.make_async_copy(cache_ref.at[at_ref[p]], cbuf.at[p], csem.at[p]))
            copies.append(mine)
        for mine in copies:
            for c in mine:
                c.start()
        cos, sin = cos_ref[...], sin_ref[...]

        def turn(v):
            return v * cos + pltpu.roll(v, HD // 2, 1) * sin

        for h in range(HEADS):
            low, high = h * HD, h * HD + HD
            v = keep_ref[:, low:high] + more_ref[:, low:high].astype(F32) + bias_ref[:, low:high]
            v = turn(v)
            for p in range(32):
                qbuf[32 * p + 4 * h : 32 * p + 4 * h + 4, :] = v[4 * p : 4 * p + 4]
        u = keep_ref[:, QW:] + more_ref[:, QW:].astype(F32) + bias_ref[:, QW:]
        new_all = jnp.concatenate([turn(u[:, :HD]), u[:, HD:]], 1)
        for p in range(32):
            o_ref[p, :, QW:] = new_all[4 * p : 4 * p + 4].astype(BF16)
        new_all = new_all.astype(BF16)
        for g in range(8):
            for c in copies[g]:
                c.wait()
            q = qbuf[128 * g : 128 * g + 128, :].astype(BF16)
            sp = []
            for i in range(4):
                p = 4 * g + i
                s = dot(q[32 * i : 32 * i + 32], buf[p, :, :HD], ((1,), (1,))) * SCALE
                col = lax.broadcasted_iota(jnp.int32, s.shape, 1)
                sp.append(jnp.where(col < limit_ref[p], s, NEG))
            sp = jnp.concatenate(sp, 0)
            sc = dot(q, cbuf[4 * g : 4 * g + 4, :, :HD].reshape(256, HD), ((1,), (1,))) * SCALE
            row = lax.broadcasted_iota(jnp.int32, sc.shape, 0)
            col = lax.broadcasted_iota(jnp.int32, sc.shape, 1)
            length = jnp.zeros(sc.shape, jnp.int32)
            for i in range(4):
                length = jnp.where(row // 32 == i, length_ref[4 * g + i], length)
            sc = jnp.where((row // 32 == col // 64) & (col % 64 < length), sc, NEG)
            new = new_all[16 * g : 16 * g + 16]
            sn = dot(q, new[:, :HD], ((1,), (1,))) * SCALE
            row = lax.broadcasted_iota(jnp.int32, sn.shape, 0)
            col = lax.broadcasted_iota(jnp.int32, sn.shape, 1)
            sn = jnp.where((row // 32 == col // 4) & (col % 4 <= row % 4), sn, NEG)
            top = jnp.maximum(
                jnp.maximum(jnp.max(sp, -1, keepdims=True), jnp.max(sc, -1, keepdims=True)),
                jnp.max(sn, -1, keepdims=True),
            )
            wp, wc, wn = jnp.exp(sp - top), jnp.exp(sc - top), jnp.exp(sn - top)
            total = (
                jnp.sum(wp, -1, keepdims=True)
                + jnp.sum(wc, -1, keepdims=True)
                + jnp.sum(wn, -1, keepdims=True)
            )
            wp = wp.astype(BF16)
            o = jnp.concatenate(
                [dot(wp[32 * i : 32 * i + 32], buf[4 * g + i, :, HD:]) for i in range(4)], 0
            )
            o = o + dot(wc.astype(BF16), cbuf[4 * g : 4 * g + 4, :, HD:].reshape(256, HD))
            o = o + dot(wn.astype(BF16), new[:, HD:])
            o = o / total
            for i in range(4):
                for h in range(HEADS):
                    o_ref[4 * g + i, :, h * HD : h * HD + HD] = o[
                        32 * i + 4 * h : 32 * i + 4 * h + 4
                    ].astype(BF16)

    return pl.pallas_call(
        kernel,
        in_specs=[IN_SMEM] * 3 + [IN_VMEM] * 5 + [ANY] * 3,
        out_specs=IN_VMEM,
        out_shape=jax.ShapeDtypeStruct((32, 4, COLS), BF16),
        scratch_shapes=[
            pltpu.VMEM((32, 512, 2 * HD), BF16),
            pltpu.VMEM((32, 64, 2 * HD), BF16),
            pltpu.VMEM((1024, HD), F32),
            pltpu.SemaphoreType.DMA((8,)),
            pltpu.SemaphoreType.DMA((32,)),
        ],
        compiler_params=pltpu.CompilerParams(vmem_limit_bytes=VMEM),
        cost_estimate=pl.CostEstimate(
            flops=32 * 32 * 600 * 512, bytes_accessed=10 * 2**20, transcendentals=32 * 32 * 600
        ),
        name="attend",
    )(limits, lengths, cache_at, keep, more, bias, cosine, sine, cache, *kvs)


def on_device(
    tokens,
    query_weight,
    query_bias,
    pair_weight,
    pair_bias,
    cache_pairs,
    prefix_pairs,
    owner_slot,
    prefix_blocks,
    positions,
):
    prompts, _, new, width = tokens.shape
    me = lax.axis_index("roll")
    my_y, my_z, my_c = me // 8, me // 2 % 4, me % 2
    tp = lax.axis_index("tp")
    tp_y, tp_x = tp // 4, tp % 4
    pos = positions.reshape(prompts)

    z_groups = [[(y * 4 + z) * 2 + c for z in range(4)] for y in range(2) for c in range(2)]
    own_core = lax.all_gather(
        prefix_pairs.reshape(4, 512, 2 * HD), "roll", axis=0, axis_index_groups=z_groups
    )
    other_core = over_roll(own_core, 0, 0, 1)

    sorted_t, sorted_g = sort_rows(
        jnp.stack([my_y, my_z, my_c]).astype(jnp.int32),
        jnp.repeat(owner_slot, new)[None],
        jnp.repeat(pos, new)[None].astype(F32),
        tokens.reshape(prompts * new, width),
    )
    swapped = over_roll(sorted_t, 1, 0, 0)

    index = jnp.arange(prompts, dtype=jnp.int32)
    half, quarter = jnp.arange(2, dtype=jnp.int32), jnp.arange(4, dtype=jnp.int32)
    y_of, c_of, z_of = (1 - half + my_y) % 2, (half + my_c) % 2, (quarter + my_z) % 4
    slot = (
        ((y_of[:, None, None, None] * 4 + z_of[None, None, :, None]) * 2 + c_of[None, :, None, None]) * 4
        + quarter[None, None, None, :]
    ).reshape(prompts)
    hit = owner_slot[None, :] == slot[:, None]
    order = jnp.sum(jnp.where(hit, index[None, :], 0), 1)
    limits = BLOCK * jnp.sum(jnp.where(hit[32:], prefix_blocks[None, :], 0), 1)
    limits = jnp.concatenate([limits, z_of])
    pos_g = jnp.sum(jnp.where(hit[32:], pos[None, :], 0), 1)
    pos_t = swapped[::4, width].astype(jnp.int32)

    cache = cache_pairs.reshape(prompts, 64, 2 * HD)
    cache_t = over_roll(cache.at[order[:32]].get(mode="promise_in_bounds"), 1, 0, 0)

    def heads(*pairs):
        return jnp.stack([(tp_y + dy) % 2 * 4 + (tp_x + dx) % 4 for dy, dx in pairs]).astype(jnp.int32)

    far = heads((0, 2), (1, 2))
    up_g, down_g = project(far, [sorted_g], query_weight, pair_weight, [[0], [1]])
    up_t, down_t = project(far, [swapped], query_weight, pair_weight, [[0], [1]])
    right_t, left_t, right_g, left_g = project(
        heads((0, 1), (1, 1), (0, 3), (1, 3)), [swapped, sorted_g], query_weight, pair_weight, [[0, 1], [2, 3]]
    )
    own_t, own_g = project(heads((0, 0), (1, 0)), [swapped, sorted_g], query_weight, pair_weight, [[0, 1]])

    def reduce(up, down, right, left, own):
        up, down = over_tp(up, 0, 1), over_tp(down, 0, 3)
        right = right.at[0].add(up[0])
        left = left.at[1].add(down[0])
        keep, send = sum_x(own, over_tp(right, 0, 1), over_tp(left, 0, 3))
        return keep, over_tp(send, 1, 0)

    full_t = reduce(up_t, down_t, right_t, left_t, own_t)
    full_g = reduce(up_g, down_g, right_g, left_g, own_g)

    frequency = jnp.exp(jnp.arange(HD // 2, dtype=F32) * (-2.0 * math.log(ROPE_BASE) / HD))
    bias = jnp.concatenate([query_bias, pair_bias]).astype(F32)[None]

    def rows(full, where, cache_at, cache):
        at = (limits[:32, None] + where[:, None] + jnp.arange(new, dtype=jnp.int32)).reshape(ROWS)
        angles = at.astype(F32)[:, None] * frequency[None, :]
        cosine, sine = jnp.cos(angles), jnp.sin(angles)
        cosine = jnp.concatenate([cosine, cosine], 1)
        sine = jnp.concatenate([-sine, sine], 1)
        return attend(
            limits, where, cache_at, *full, bias, cosine, sine, cache, (own_core, other_core)
        )

    back = over_roll(rows(full_t, pos_t, index[:32], cache_t), 1, 0, 0)
    done = rows(full_g, pos_g, order[32:], cache)
    attended, new_pairs = place_rows(order, back, done)
    return (
        attended.reshape(prompts, 1, new, QW),
        new_pairs.reshape(prompts, 1, new, 1, PW),
    )


def solution(mesh):
    return jax.shard_map(
        on_device,
        mesh=mesh,
        in_specs=(
            P(None, "roll", None, "tp"),
            P("tp", None),
            P("tp"),
            P("tp", None),
            P("tp"),
            P(None, "roll", None, "tp", None),
            P("roll", None, "tp", None),
            P(),
            P(),
            P(None, "roll"),
        ),
        out_specs=(P(None, "roll", None, "tp"), P(None, "roll", None, "tp", None)),
        check_vma=False,
    )
```

```python
import math

import jax
import jax.numpy as jnp
from jax import lax
from jax.experimental import pallas as pl
from jax.experimental.pallas import tpu as pltpu
from jax.sharding import PartitionSpec as P

BLOCK = 128
HD = 128
HEADS = 8
QW = HEADS * HD
PW = 2 * HD
COLS = QW + PW
ROWS = 128
ROPE_BASE = 1000000.0
NEG = -1e30
SCALE = HD ** -0.5
F32 = jnp.float32
BF16 = jnp.bfloat16
VMEM = 50 * 1024 * 1024


def tp_shift(dy, dx):
    return [(y * 4 + x, (y + dy) % 2 * 4 + (x + dx) % 4) for y in range(2) for x in range(4)]


def roll_shift(dy, dz, dc):
    return [
        ((y * 4 + z) * 2 + c, ((y + dy) % 2 * 4 + (z + dz) % 4) * 2 + (c + dc) % 2)
        for y in range(2)
        for z in range(4)
        for c in range(2)
    ]


def over_tp(a, dy, dx):
    return lax.ppermute(a, "tp", tp_shift(dy, dx))


def over_roll(a, dy, dz, dc):
    return lax.ppermute(a, "roll", roll_shift(dy, dz, dc))


def dot(a, b, dims=((1,), (0,))):
    return lax.dot_general(a, b, (dims, ((), ())), preferred_element_type=F32)


ANY = pl.BlockSpec(memory_space=pl.ANY)
IN_VMEM = pl.BlockSpec(memory_space=pltpu.VMEM)
SMALL = pl.CostEstimate(flops=10**6, bytes_accessed=10**5, transcendentals=0)
IN_SMEM = pl.BlockSpec(memory_space=pltpu.SMEM)


def project(heads, xs, wq, wp, groups):
    count = sum(len(g) for g in groups)
    depth = wq.shape[0]

    def kernel(heads_ref, *refs):
        x_refs, (wq_ref, wp_ref), rest = refs[: len(xs)], refs[len(xs) : len(xs) + 2], refs[len(xs) + 2 :]
        outs, (q_buf, p_buf, q_sem, p_sem) = rest[:-4], rest[-4:]
        copies = []
        for d in range(count):
            k = heads_ref[d]
            copies.append(
                (
                    pltpu.make_async_copy(
                        wq_ref.at[:, pl.ds(pl.multiple_of(k * QW, QW), QW)], q_buf.at[d], q_sem.at[d]
                    ),
                    pltpu.make_async_copy(
                        wp_ref.at[:, pl.ds(pl.multiple_of(k * PW, PW), PW)], p_buf.at[d], p_sem.at[d]
                    ),
                )
            )
        for pair in copies:
            for c in pair:
                c.start()
        x = jnp.concatenate([r[:, :depth] for r in x_refs], 0)
        d = 0
        for g, group in enumerate(groups):
            for i in range(len(group)):
                for c in copies[d]:
                    c.wait()
                for buf, low, high in ((q_buf, 0, QW), (p_buf, QW, COLS)):
                    y = dot(x, buf[d]).astype(BF16)
                    for b in range(len(xs)):
                        outs[b * len(groups) + g][i, :, low:high] = y[b * ROWS : (b + 1) * ROWS]
                d += 1

    return pl.pallas_call(
        kernel,
        in_specs=[IN_SMEM] + [IN_VMEM] * len(xs) + [ANY, ANY],
        out_specs=[IN_VMEM] * (len(xs) * len(groups)),
        out_shape=[jax.ShapeDtypeStruct((len(g), ROWS, COLS), BF16) for _ in xs for g in groups],
        scratch_shapes=[
            pltpu.VMEM((count, depth, QW), BF16),
            pltpu.VMEM((count, depth, PW), BF16),
            pltpu.SemaphoreType.DMA((count,)),
            pltpu.SemaphoreType.DMA((count,)),
        ],
        compiler_params=pltpu.CompilerParams(vmem_limit_bytes=VMEM),
        cost_estimate=SMALL,
        name="project",
    )(heads, *xs, wq, wp)


def sort_rows(place, owner, pos, tokens):
    rows, width = tokens.shape

    def kernel(place_ref, owner_ref, pos_ref, x_ref, *outs):
        x = x_ref[...]
        for b, out in enumerate(outs):
            row = lax.broadcasted_iota(jnp.int32, (ROWS, rows), 0)
            col = lax.broadcasted_iota(jnp.int32, (ROWS, rows), 1)
            i = row // 4
            y, c, step, j = (1 - b + place_ref[0]) % 2, i // 16, i // 4 % 4, i % 4
            c = jnp.where(c == 0, place_ref[2], 1 - place_ref[2])
            z = (jnp.where(step == 1, 3, jnp.where(step == 0, 0, step - 1)) + place_ref[1]) % 4
            slot = ((y * 4 + z) * 2 + c) * 4 + j
            hit = (owner_ref[...] == slot) & (col % 4 == row % 4)
            at = jnp.sum(jnp.where(hit, pos_ref[...], 0.0), -1, keepdims=True)
            hit = jnp.where(hit, 1.0, 0.0).astype(BF16)
            out[:, :width] = dot(hit, x).astype(BF16)
            out[:, width:] = jnp.broadcast_to(at, (ROWS, 128)).astype(BF16)

    return pl.pallas_call(
        kernel,
        in_specs=[IN_SMEM, IN_VMEM, IN_VMEM, IN_VMEM],
        out_specs=[IN_VMEM] * 2,
        out_shape=[jax.ShapeDtypeStruct((ROWS, width + 128), BF16)] * 2,
        compiler_params=pltpu.CompilerParams(vmem_limit_bytes=VMEM),
        cost_estimate=SMALL,
        name="sort_rows",
    )(place, owner, pos, tokens)


def place_rows(order, first, second):
    def kernel(order_ref, a_ref, b_ref, o_ref, p_ref):
        for half, ref in enumerate((a_ref, b_ref)):

            def step(i, carry, half=half, ref=ref):
                at = order_ref[32 * half + i]
                o_ref[at] = ref[i, :, :QW]
                p_ref[at] = ref[i, :, QW:]
                return carry

            lax.fori_loop(0, 32, step, 0, unroll=8)

    return pl.pallas_call(
        kernel,
        in_specs=[IN_SMEM, IN_VMEM, IN_VMEM],
        out_specs=[IN_VMEM] * 2,
        out_shape=[jax.ShapeDtypeStruct((64, 4, QW), BF16), jax.ShapeDtypeStruct((64, 4, PW), BF16)],
        compiler_params=pltpu.CompilerParams(vmem_limit_bytes=VMEM),
        cost_estimate=SMALL,
        name="place_rows",
    )(order, first, second)


def add_far(right, left, up, down):
    def kernel(r, l, u, d, r_out, l_out):
        r_out[...] = (r[...].astype(F32) + u[...].astype(F32)).astype(BF16)
        l_out[...] = (l[...].astype(F32) + d[...].astype(F32)).astype(BF16)

    block = [pl.BlockSpec((1, ROWS, COLS), lambda i, h=h: (h, 0, 0)) for h in (0, 1)]
    return pl.pallas_call(
        kernel,
        grid=(1,),
        in_specs=block + [block[0]] * 2,
        out_specs=block,
        out_shape=[jax.ShapeDtypeStruct(right.shape, BF16)] * 2,
        input_output_aliases={0: 0, 1: 1},
        compiler_params=pltpu.CompilerParams(vmem_limit_bytes=VMEM),
        cost_estimate=SMALL,
        name="add_far",
    )(right, left, up, down)


def pick_cache(order, cache, after):
    def kernel(order_ref, cache_ref, *refs):
        out, sem = refs[-2:]
        copies = [pltpu.make_async_copy(cache_ref.at[order_ref[i]], out.at[i], sem.at[i]) for i in range(32)]
        for c in copies:
            c.start()
        for c in copies:
            c.wait()

    return pl.pallas_call(
        kernel,
        in_specs=[IN_SMEM] + [ANY] * (1 + len(after)),
        out_specs=ANY,
        out_shape=jax.ShapeDtypeStruct((32,) + cache.shape[1:], BF16),
        scratch_shapes=[pltpu.SemaphoreType.DMA((32,))],
        cost_estimate=SMALL,
        name="pick_cache",
    )(order, cache, *after)


def sum_x(own, from_left, from_right):
    def kernel(a, b, c, keep, send):
        for i, out in enumerate((keep, send)):
            out[...] = (a[i].astype(F32) + b[i].astype(F32) + c[i].astype(F32)).astype(out.dtype)

    return pl.pallas_call(
        kernel,
        in_specs=[IN_VMEM] * 3,
        out_specs=[IN_VMEM] * 2,
        out_shape=[jax.ShapeDtypeStruct((ROWS, COLS), F32), jax.ShapeDtypeStruct((ROWS, COLS), BF16)],
        compiler_params=pltpu.CompilerParams(vmem_limit_bytes=VMEM),
        cost_estimate=SMALL,
        name="sum_x",
    )(own, from_left, from_right)


def attend(limits, lengths, cache_at, keep, more, bias, cosine, sine, cache, kvs):
    flat = [a for group in kvs for a in group]

    def kernel(
        limit_ref, length_ref, at_ref, keep_ref, more_ref, bias_ref, cos_ref, sin_ref, cache_ref, *refs
    ):
        o_ref, buf, cbuf, qbuf, sem, csem = refs[len(flat) :]
        copies, k = [], 0
        for g, group in enumerate(kvs):
            mine, slot = [], 4 * g
            for a in group:
                n = a.shape[0]
                mine.append(pltpu.make_async_copy(refs[k], buf.at[pl.ds(slot, n)], sem.at[k]))
                slot, k = slot + n, k + 1
            for p in range(4 * g, 4 * g + 4):
                mine.append(pltpu.make_async_copy(cache_ref.at[at_ref[p]], cbuf.at[p], csem.at[p]))
            copies.append(mine)
        for mine in copies:
            for c in mine:
                c.start()
        cos, sin = cos_ref[...], sin_ref[...]

        def turn(v):
            return v * cos + pltpu.roll(v, HD // 2, 1) * sin

        for h in range(HEADS):
            low, high = h * HD, h * HD + HD
            v = keep_ref[:, low:high] + more_ref[:, low:high].astype(F32) + bias_ref[:, low:high]
            v = turn(v)
            for p in range(32):
                qbuf[32 * p + 4 * h : 32 * p + 4 * h + 4, :] = v[4 * p : 4 * p + 4]
        u = keep_ref[:, QW:] + more_ref[:, QW:].astype(F32) + bias_ref[:, QW:]
        new_all = jnp.concatenate([turn(u[:, :HD]), u[:, HD:]], 1)
        for p in range(32):
            o_ref[p, :, QW:] = new_all[4 * p : 4 * p + 4].astype(BF16)
        new_all = new_all.astype(BF16)
        for g in range(8):
            for c in copies[g]:
                c.wait()
            q = qbuf[128 * g : 128 * g + 128, :].astype(BF16)
            sp = []
            for i in range(4):
                p = 4 * g + i
                s = dot(q[32 * i : 32 * i + 32], buf[p, :, :HD], ((1,), (1,))) * SCALE
                col = lax.broadcasted_iota(jnp.int32, s.shape, 1)
                sp.append(jnp.where(col < limit_ref[p], s, NEG))
            sp = jnp.concatenate(sp, 0)
            sc = dot(q, cbuf[4 * g : 4 * g + 4, :, :HD].reshape(256, HD), ((1,), (1,))) * SCALE
            row = lax.broadcasted_iota(jnp.int32, sc.shape, 0)
            col = lax.broadcasted_iota(jnp.int32, sc.shape, 1)
            length = jnp.zeros(sc.shape, jnp.int32)
            for i in range(4):
                length = jnp.where(row // 32 == i, length_ref[4 * g + i], length)
            sc = jnp.where((row // 32 == col // 64) & (col % 64 < length), sc, NEG)
            new = new_all[16 * g : 16 * g + 16]
            sn = dot(q, new[:, :HD], ((1,), (1,))) * SCALE
            row = lax.broadcasted_iota(jnp.int32, sn.shape, 0)
            col = lax.broadcasted_iota(jnp.int32, sn.shape, 1)
            sn = jnp.where((row // 32 == col // 4) & (col % 4 <= row % 4), sn, NEG)
            top = jnp.maximum(
                jnp.maximum(jnp.max(sp, -1, keepdims=True), jnp.max(sc, -1, keepdims=True)),
                jnp.max(sn, -1, keepdims=True),
            )
            wp, wc, wn = jnp.exp(sp - top), jnp.exp(sc - top), jnp.exp(sn - top)
            total = (
                jnp.sum(wp, -1, keepdims=True)
                + jnp.sum(wc, -1, keepdims=True)
                + jnp.sum(wn, -1, keepdims=True)
            )
            wp = wp.astype(BF16)
            o = jnp.concatenate(
                [dot(wp[32 * i : 32 * i + 32], buf[4 * g + i, :, HD:]) for i in range(4)], 0
            )
            o = o + dot(wc.astype(BF16), cbuf[4 * g : 4 * g + 4, :, HD:].reshape(256, HD))
            o = o + dot(wn.astype(BF16), new[:, HD:])
            o = o / total
            for i in range(4):
                for h in range(HEADS):
                    o_ref[4 * g + i, :, h * HD : h * HD + HD] = o[
                        32 * i + 4 * h : 32 * i + 4 * h + 4
                    ].astype(BF16)

    return pl.pallas_call(
        kernel,
        in_specs=[IN_SMEM] * 3 + [IN_VMEM] * 5 + [ANY] * (1 + len(flat)),
        out_specs=IN_VMEM,
        out_shape=jax.ShapeDtypeStruct((32, 4, COLS), BF16),
        scratch_shapes=[
            pltpu.VMEM((32, 512, 2 * HD), BF16),
            pltpu.VMEM((32, 64, 2 * HD), BF16),
            pltpu.VMEM((1024, HD), F32),
            pltpu.SemaphoreType.DMA((len(flat),)),
            pltpu.SemaphoreType.DMA((32,)),
        ],
        compiler_params=pltpu.CompilerParams(vmem_limit_bytes=VMEM),
        cost_estimate=SMALL,
        name="attend",
    )(limits, lengths, cache_at, keep, more, bias, cosine, sine, cache, *flat)


def on_device(
    tokens,
    query_weight,
    query_bias,
    pair_weight,
    pair_bias,
    cache_pairs,
    prefix_pairs,
    owner_slot,
    prefix_blocks,
    positions,
):
    prompts, _, new, width = tokens.shape
    me = lax.axis_index("roll")
    my_y, my_z, my_c = me // 8, me // 2 % 4, me % 2
    tp = lax.axis_index("tp")
    tp_y, tp_x = tp // 4, tp % 4
    pos = positions.reshape(prompts)

    own = prefix_pairs.reshape(4, 512, 2 * HD)
    below, above = over_roll(own, 0, 1, 0), over_roll(own, 0, 3, 0)
    far_a, far_b = over_roll(below[:2], 0, 1, 0), over_roll(above[2:], 0, 3, 0)
    kvs = [[own], [below], [above], [far_a, far_b]]
    kvs = kvs + [[over_roll(a, 0, 0, 1) for a in group] for group in kvs]

    sorted_t, sorted_g = sort_rows(
        jnp.stack([my_y, my_z, my_c]).astype(jnp.int32),
        jnp.repeat(owner_slot, new)[None],
        jnp.repeat(pos, new)[None].astype(F32),
        tokens.reshape(prompts * new, width),
    )
    swapped = over_roll(sorted_t, 1, 0, 0)

    index = jnp.arange(prompts, dtype=jnp.int32)
    half, quarter = jnp.arange(2, dtype=jnp.int32), jnp.arange(4, dtype=jnp.int32)
    y_of, c_of, z_of = (1 - half + my_y) % 2, (half + my_c) % 2, (jnp.array([0, 3, 1, 2], jnp.int32) + my_z) % 4
    slot = (
        ((y_of[:, None, None, None] * 4 + z_of[None, None, :, None]) * 2 + c_of[None, :, None, None]) * 4
        + quarter[None, None, None, :]
    ).reshape(prompts)
    hit = owner_slot[None, :] == slot[:, None]
    order = jnp.sum(jnp.where(hit, index[None, :], 0), 1)
    limits = BLOCK * jnp.sum(jnp.where(hit[32:], prefix_blocks[None, :], 0), 1)
    pos_g = jnp.sum(jnp.where(hit[32:], pos[None, :], 0), 1)
    pos_t = swapped[::4, width].astype(jnp.int32)

    cache = cache_pairs.reshape(prompts, 64, 2 * HD)
    cache_t = over_roll(pick_cache(order, cache, (below, above)), 1, 0, 0)

    def heads(*pairs):
        return jnp.stack([(tp_y + dy) % 2 * 4 + (tp_x + dx) % 4 for dy, dx in pairs]).astype(jnp.int32)

    far = heads((0, 2), (1, 2))
    up_g, down_g = project(far, [sorted_g], query_weight, pair_weight, [[0], [1]])
    up_t, down_t = project(far, [swapped], query_weight, pair_weight, [[0], [1]])
    right_t, left_t, right_g, left_g = project(
        heads((0, 1), (1, 1), (0, 3), (1, 3)), [swapped, sorted_g], query_weight, pair_weight, [[0, 1], [2, 3]]
    )
    own_t, own_g = project(heads((0, 0), (1, 0)), [swapped, sorted_g], query_weight, pair_weight, [[0, 1]])

    def reduce(up, down, right, left, own):
        up, down = over_tp(up, 0, 1), over_tp(down, 0, 3)
        right, left = add_far(right, left, up, down)
        keep, send = sum_x(own, over_tp(right, 0, 1), over_tp(left, 0, 3))
        return keep, over_tp(send, 1, 0)

    full_t = reduce(up_t, down_t, right_t, left_t, own_t)
    full_g = reduce(up_g, down_g, right_g, left_g, own_g)

    frequency = jnp.exp(jnp.arange(HD // 2, dtype=F32) * (-2.0 * math.log(ROPE_BASE) / HD))
    bias = jnp.concatenate([query_bias, pair_bias]).astype(F32)[None]

    def rows(full, where, cache_at, cache):
        at = (limits[:, None] + where[:, None] + jnp.arange(new, dtype=jnp.int32)).reshape(ROWS)
        angles = at.astype(F32)[:, None] * frequency[None, :]
        cosine, sine = jnp.cos(angles), jnp.sin(angles)
        cosine = jnp.concatenate([cosine, cosine], 1)
        sine = jnp.concatenate([-sine, sine], 1)
        return attend(
            limits, where, cache_at, *full, bias, cosine, sine, cache, kvs
        )

    back = over_roll(rows(full_t, pos_t, index[:32], cache_t), 1, 0, 0)
    done = rows(full_g, pos_g, order[32:], cache)
    attended, new_pairs = place_rows(order, back, done)
    return (
        attended.reshape(prompts, 1, new, QW),
        new_pairs.reshape(prompts, 1, new, 1, PW),
    )


def solution(mesh):
    return jax.shard_map(
        on_device,
        mesh=mesh,
        in_specs=(
            P(None, "roll", None, "tp"),
            P("tp", None),
            P("tp"),
            P("tp", None),
            P("tp"),
            P(None, "roll", None, "tp", None),
            P("roll", None, "tp", None),
            P(),
            P(),
            P(None, "roll"),
        ),
        out_specs=(P(None, "roll", None, "tp"), P(None, "roll", None, "tp", None)),
        check_vma=False,
    )
```

```python
import math

import jax
import jax.numpy as jnp
from jax import lax
from jax.experimental import pallas as pl
from jax.experimental.pallas import tpu as pltpu
from jax.sharding import PartitionSpec as P

BLOCK = 128
HD = 128
HEADS = 8
QW = HEADS * HD
PW = 2 * HD
COLS = QW + PW
ROWS = 128
ROPE_BASE = 1000000.0
NEG = -1e30
SCALE = HD ** -0.5
F32 = jnp.float32
BF16 = jnp.bfloat16
VMEM = 24 * 1024 * 1024


def tp_shift(dy, dx):
    return [(y * 4 + x, (y + dy) % 2 * 4 + (x + dx) % 4) for y in range(2) for x in range(4)]


def roll_shift(dy, dz, dc):
    return [
        ((y * 4 + z) * 2 + c, ((y + dy) % 2 * 4 + (z + dz) % 4) * 2 + (c + dc) % 2)
        for y in range(2)
        for z in range(4)
        for c in range(2)
    ]


def over_tp(a, dy, dx):
    return lax.ppermute(a, "tp", tp_shift(dy, dx))


def over_roll(a, dy, dz, dc):
    return lax.ppermute(a, "roll", roll_shift(dy, dz, dc))


def dot(a, b, dims=((1,), (0,))):
    return lax.dot_general(a, b, (dims, ((), ())), preferred_element_type=F32)


ANY = pl.BlockSpec(memory_space=pl.ANY)
IN_HBM = pl.BlockSpec(memory_space=pltpu.HBM)
IN_VMEM = pl.BlockSpec(memory_space=pltpu.VMEM)
SMALL = pl.CostEstimate(flops=10**6, bytes_accessed=10**5, transcendentals=0)
IN_SMEM = pl.BlockSpec(memory_space=pltpu.SMEM)


def project(heads, xs, wq, wp, groups):
    count = sum(len(g) for g in groups)
    depth = wq.shape[0]

    def kernel(heads_ref, *refs):
        x_refs, (wq_ref, wp_ref), rest = refs[: len(xs)], refs[len(xs) : len(xs) + 2], refs[len(xs) + 2 :]
        outs, (q_buf, p_buf, q_sem, p_sem) = rest[:-4], rest[-4:]
        copies = []
        for d in range(count):
            k = heads_ref[d]
            copies.append(
                (
                    pltpu.make_async_copy(
                        wq_ref.at[:, pl.ds(pl.multiple_of(k * QW, QW), QW)], q_buf.at[d], q_sem.at[d]
                    ),
                    pltpu.make_async_copy(
                        wp_ref.at[:, pl.ds(pl.multiple_of(k * PW, PW), PW)], p_buf.at[d], p_sem.at[d]
                    ),
                )
            )
        for pair in copies:
            for c in pair:
                c.start()
        x = jnp.concatenate([r[...] for r in x_refs], 0)
        d = 0
        for g, group in enumerate(groups):
            for i in range(len(group)):
                for c in copies[d]:
                    c.wait()
                for buf, low, high in ((q_buf, 0, QW), (p_buf, QW, COLS)):
                    y = dot(x, buf[d]).astype(BF16)
                    for b in range(len(xs)):
                        outs[b * len(groups) + g][i, :, low:high] = y[b * ROWS : (b + 1) * ROWS]
                d += 1

    return pl.pallas_call(
        kernel,
        in_specs=[IN_SMEM] + [IN_VMEM] * len(xs) + [IN_HBM, IN_HBM],
        out_specs=[IN_VMEM] * (len(xs) * len(groups)),
        out_shape=[jax.ShapeDtypeStruct((len(g), ROWS, COLS), BF16) for _ in xs for g in groups],
        scratch_shapes=[
            pltpu.VMEM((count, depth, QW), BF16),
            pltpu.VMEM((count, depth, PW), BF16),
            pltpu.SemaphoreType.DMA((count,)),
            pltpu.SemaphoreType.DMA((count,)),
        ],
        compiler_params=pltpu.CompilerParams(vmem_limit_bytes=VMEM),
        cost_estimate=SMALL,
        name="project",
    )(heads, *xs, wq, wp)


def sort_rows(place, owner, tokens):
    rows, width = tokens.shape

    def kernel(place_ref, owner_ref, x_ref, *outs):
        x = x_ref[...]
        for b, out in enumerate(outs):
            row = lax.broadcasted_iota(jnp.int32, (ROWS, rows), 0)
            col = lax.broadcasted_iota(jnp.int32, (ROWS, rows), 1)
            i = row // 4
            y, c, step, j = (1 - b + place_ref[0]) % 2, i // 16, i // 4 % 4, i % 4
            c = jnp.where(c == 0, place_ref[2], 1 - place_ref[2])
            z = (jnp.where(step == 1, 3, jnp.where(step == 0, 0, step - 1)) + place_ref[1]) % 4
            slot = ((y * 4 + z) * 2 + c) * 4 + j
            hit = (owner_ref[...] == slot) & (col % 4 == row % 4)
            out[...] = dot(jnp.where(hit, 1.0, 0.0).astype(BF16), x).astype(BF16)

    return pl.pallas_call(
        kernel,
        in_specs=[IN_SMEM, IN_VMEM, IN_VMEM],
        out_specs=[IN_VMEM] * 2,
        out_shape=[jax.ShapeDtypeStruct((ROWS, width), BF16)] * 2,
        compiler_params=pltpu.CompilerParams(vmem_limit_bytes=VMEM),
        cost_estimate=SMALL,
        name="sort_rows",
    )(place, owner, tokens)


def add_far(right, left, up, down):
    def kernel(r, l, u, d, r_out, l_out):
        r_out[...] = (r[...].astype(F32) + u[...].astype(F32)).astype(BF16)
        l_out[...] = (l[...].astype(F32) + d[...].astype(F32)).astype(BF16)

    block = [pl.BlockSpec((1, ROWS, COLS), lambda i, h=h: (h, 0, 0)) for h in (0, 1)]
    return pl.pallas_call(
        kernel,
        grid=(1,),
        in_specs=block + [block[0]] * 2,
        out_specs=block,
        out_shape=[jax.ShapeDtypeStruct(right.shape, BF16)] * 2,
        input_output_aliases={0: 0, 1: 1},
        compiler_params=pltpu.CompilerParams(vmem_limit_bytes=VMEM),
        cost_estimate=SMALL,
        name="add_far",
    )(right, left, up, down)


def sum_x(own, from_left, from_right):
    def kernel(a, b, c, keep, send):
        for i, out in enumerate((keep, send)):
            out[...] = (a[i].astype(F32) + b[i].astype(F32) + c[i].astype(F32)).astype(out.dtype)

    return pl.pallas_call(
        kernel,
        in_specs=[IN_VMEM] * 3,
        out_specs=[IN_VMEM] * 2,
        out_shape=[jax.ShapeDtypeStruct((ROWS, COLS), F32), jax.ShapeDtypeStruct((ROWS, COLS), BF16)],
        compiler_params=pltpu.CompilerParams(vmem_limit_bytes=VMEM),
        cost_estimate=SMALL,
        name="sum_x",
    )(own, from_left, from_right)


def rotated(keep_ref, more_ref, bias_ref, cos_ref, sin_ref, first, q_buf):
    cos, sin = cos_ref[first : first + ROWS, :], sin_ref[first : first + ROWS, :]

    def turn(v):
        return v * cos + pltpu.roll(v, HD // 2, 1) * sin

    for h in range(HEADS):
        low, high = h * HD, h * HD + HD
        v = turn(keep_ref[:, low:high] + more_ref[:, low:high].astype(F32) + bias_ref[:, low:high])
        for p in range(32):
            q_buf[32 * p + 4 * h : 32 * p + 4 * h + 4, :] = v[4 * p : 4 * p + 4]
    u = keep_ref[:, QW:] + more_ref[:, QW:].astype(F32) + bias_ref[:, QW:]
    return jnp.concatenate([turn(u[:, :HD]), u[:, HD:]], 1)


def prefix_scores(q, buf, limit_ref, g):
    parts = []
    for i in range(4):
        p = 4 * g + i
        s = dot(q[32 * i : 32 * i + 32], buf[p, :, :HD], ((1,), (1,))) * SCALE
        col = lax.broadcasted_iota(jnp.int32, s.shape, 1)
        parts.append(jnp.where(col < limit_ref[p], s, NEG))
    return jnp.concatenate(parts, 0)


def prefix_values(w, buf, g):
    w = w.astype(BF16)
    return jnp.concatenate([dot(w[32 * i : 32 * i + 32], buf[4 * g + i, :, HD:]) for i in range(4)], 0)


def near_scores(q, cbuf, new, length_ref, g):
    sc = dot(q, cbuf[4 * g : 4 * g + 4, :, :HD].reshape(256, HD), ((1,), (1,))) * SCALE
    row = lax.broadcasted_iota(jnp.int32, sc.shape, 0)
    col = lax.broadcasted_iota(jnp.int32, sc.shape, 1)
    length = jnp.zeros(sc.shape, jnp.int32)
    for i in range(4):
        length = jnp.where(row // 32 == i, length_ref[4 * g + i], length)
    sc = jnp.where((row // 32 == col // 64) & (col % 64 < length), sc, NEG)
    sn = dot(q, new[:, :HD], ((1,), (1,))) * SCALE
    row = lax.broadcasted_iota(jnp.int32, sn.shape, 0)
    col = lax.broadcasted_iota(jnp.int32, sn.shape, 1)
    sn = jnp.where((row // 32 == col // 4) & (col % 4 <= row % 4), sn, NEG)
    return sc, sn


def near_values(wc, wn, cbuf, new, g):
    o = dot(wc.astype(BF16), cbuf[4 * g : 4 * g + 4, :, HD:].reshape(256, HD))
    return o + dot(wn.astype(BF16), new[:, HD:])


def softmax(*scores):
    top = jnp.max(scores[0], -1, keepdims=True)
    for s in scores[1:]:
        top = jnp.maximum(top, jnp.max(s, -1, keepdims=True))
    weights = [jnp.exp(s - top) for s in scores]
    total = jnp.sum(weights[0], -1, keepdims=True)
    for w in weights[1:]:
        total = total + jnp.sum(w, -1, keepdims=True)
    return top, weights, total


def prefix_copies(kvs, refs, buf, sem):
    copies, k = [], 0
    for g, group in enumerate(kvs):
        mine, slot = [], 4 * g
        for a in group:
            n = a.shape[0]
            mine.append(pltpu.make_async_copy(refs[k], buf.at[pl.ds(slot, n)], sem.at[k]))
            slot, k = slot + n, k + 1
        copies.append(mine)
    return copies


def cache_copies(cache_ref, at_ref, first, cbuf, sem):
    return [
        pltpu.make_async_copy(cache_ref.at[at_ref[first + p]], cbuf.at[p], sem.at[p]) for p in range(32)
    ]


CACHE_SCRATCH = [pltpu.VMEM((32, 64, 2 * HD), BF16), pltpu.SemaphoreType.DMA((32,))]


def attend(limits, lengths, order, keep, more, bias, cosine, sine, cache, kvs):
    flat = [a for group in kvs for a in group]

    def kernel(limit_ref, length_ref, at_ref, keep_ref, more_ref, bias_ref, cos_ref, sin_ref, cache_ref, *refs):
        o_ref, buf, sem, qbuf, cbuf, csem = refs[len(flat) :]
        prefix = prefix_copies(kvs, refs, buf, sem)
        caches = cache_copies(cache_ref, at_ref, 32, cbuf, csem)
        for g in range(8):
            for c in prefix[g] + caches[4 * g : 4 * g + 4]:
                c.start()
        new_all = rotated(keep_ref, more_ref, bias_ref, cos_ref, sin_ref, ROWS, qbuf)
        for p in range(32):
            o_ref[p, :, QW:] = new_all[4 * p : 4 * p + 4].astype(BF16)
        new_all = new_all.astype(BF16)
        for g in range(8):
            for c in prefix[g] + caches[4 * g : 4 * g + 4]:
                c.wait()
            q = qbuf[128 * g : 128 * g + 128, :].astype(BF16)
            new = new_all[16 * g : 16 * g + 16]
            sp = prefix_scores(q, buf, limit_ref, g)
            sc, sn = near_scores(q, cbuf, new, length_ref.at[pl.ds(32, 32)], g)
            _, (wp, wc, wn), total = softmax(sp, sc, sn)
            o = (prefix_values(wp, buf, g) + near_values(wc, wn, cbuf, new, g)) / total
            for i in range(4):
                for h in range(HEADS):
                    o_ref[4 * g + i, :, h * HD : h * HD + HD] = o[
                        32 * i + 4 * h : 32 * i + 4 * h + 4
                    ].astype(BF16)

    return pl.pallas_call(
        kernel,
        in_specs=[IN_SMEM] * 3 + [IN_VMEM] * 5 + [ANY] * (1 + len(flat)),
        out_specs=IN_VMEM,
        out_shape=jax.ShapeDtypeStruct((32, 4, COLS), BF16),
        scratch_shapes=[
            pltpu.VMEM((32, 512, 2 * HD), BF16),
            pltpu.SemaphoreType.DMA((len(flat),)),
            pltpu.VMEM((1024, HD), F32),
        ]
        + CACHE_SCRATCH,
        compiler_params=pltpu.CompilerParams(vmem_limit_bytes=VMEM),
        cost_estimate=SMALL,
        name="attend",
    )(limits, lengths, order, keep, more, bias, cosine, sine, cache, *flat)


def make_queries(keep, more, bias, cosine, sine):
    def kernel(keep_ref, more_ref, bias_ref, cos_ref, sin_ref, q_ref, new_ref, qbuf):
        new_ref[...] = rotated(keep_ref, more_ref, bias_ref, cos_ref, sin_ref, 0, qbuf).astype(BF16)
        q_ref[...] = qbuf[...].astype(BF16).reshape(32, 32, HD)

    return pl.pallas_call(
        kernel,
        in_specs=[IN_VMEM] * 5,
        out_specs=[IN_VMEM] * 2,
        out_shape=[jax.ShapeDtypeStruct((32, 32, HD), BF16), jax.ShapeDtypeStruct((ROWS, PW), BF16)],
        scratch_shapes=[pltpu.VMEM((1024, HD), F32)],
        compiler_params=pltpu.CompilerParams(vmem_limit_bytes=VMEM),
        cost_estimate=SMALL,
        name="make_queries",
    )(keep, more, bias, cosine, sine)


def attend_prefix(limits, q, kvs):
    flat = [a for group in kvs for a in group]

    def kernel(limit_ref, q_ref, *refs):
        o_ref, buf, sem = refs[len(flat) :]
        prefix = prefix_copies(kvs, refs, buf, sem)
        for mine in prefix:
            for c in mine:
                c.start()
        lane = lax.broadcasted_iota(jnp.int32, (32, 128), 1)
        stats = jnp.zeros((32, 128), F32)
        for g in range(8):
            for c in prefix[g]:
                c.wait()
            q = q_ref[4 * g : 4 * g + 4].reshape(128, HD)
            top, (w,), total = softmax(prefix_scores(q, buf, limit_ref, g))
            o = prefix_values(w, buf, g) / total
            o_ref[4 * g : 4 * g + 4] = o.astype(BF16).reshape(4, 32, HD)
            rest = top + jnp.log(total)
            for part in range(3):
                piece = rest.astype(BF16).astype(F32)
                for i in range(4):
                    stats = jnp.where(lane == 3 * (4 * g + i) + part, piece[32 * i : 32 * i + 32], stats)
                rest = rest - piece
        o_ref[32] = stats.astype(BF16)

    return pl.pallas_call(
        kernel,
        in_specs=[IN_SMEM, IN_VMEM] + [ANY] * len(flat),
        out_specs=IN_VMEM,
        out_shape=jax.ShapeDtypeStruct((33, 32, HD), BF16),
        scratch_shapes=[pltpu.VMEM((32, 512, 2 * HD), BF16), pltpu.SemaphoreType.DMA((len(flat),))],
        compiler_params=pltpu.CompilerParams(vmem_limit_bytes=VMEM),
        cost_estimate=SMALL,
        name="attend_prefix",
    )(limits, q, *flat)


def attend_near(lengths, order, q, new, cache):
    def kernel(length_ref, at_ref, q_ref, new_ref, cache_ref, o_ref, l_ref, cbuf, csem):
        caches = cache_copies(cache_ref, at_ref, 0, cbuf, csem)
        for c in caches:
            c.start()
        for g in range(8):
            for c in caches[4 * g : 4 * g + 4]:
                c.wait()
            q = q_ref[4 * g : 4 * g + 4].reshape(128, HD)
            new = new_ref[16 * g : 16 * g + 16]
            top, (wc, wn), total = softmax(*near_scores(q, cbuf, new, length_ref, g))
            o_ref[128 * g : 128 * g + 128] = near_values(wc, wn, cbuf, new, g) / total
            l_ref[128 * g : 128 * g + 128] = jnp.broadcast_to(top + jnp.log(total), (128, HD))

    return pl.pallas_call(
        kernel,
        in_specs=[IN_SMEM] * 2 + [IN_VMEM] * 2 + [ANY],
        out_specs=[IN_VMEM] * 2,
        out_shape=[jax.ShapeDtypeStruct((1024, HD), F32)] * 2,
        scratch_shapes=CACHE_SCRATCH,
        compiler_params=pltpu.CompilerParams(vmem_limit_bytes=VMEM),
        cost_estimate=SMALL,
        name="attend_near",
    )(lengths, order, q, new, cache)


def merge_rows(order, far, near, near_log, new, done):
    def kernel(order_ref, far_ref, o_ref, l_ref, new_ref, done_ref, out_ref, pair_ref):
        stats = far_ref[32].astype(F32)
        for p in range(32):
            at = order_ref[p]
            theirs = jnp.sum(stats[:, 3 * p : 3 * p + 3], -1, keepdims=True)
            ours = l_ref[32 * p : 32 * p + 32]
            top = jnp.maximum(theirs, ours)
            wt, wo = jnp.exp(theirs - top), jnp.exp(ours - top)
            o = (far_ref[p].astype(F32) * wt + o_ref[32 * p : 32 * p + 32] * wo) / (wt + wo)
            for h in range(HEADS):
                out_ref[at, :, h * HD : h * HD + HD] = o[4 * h : 4 * h + 4].astype(BF16)
            pair_ref[at] = new_ref[p]
            at = order_ref[32 + p]
            out_ref[at] = done_ref[p, :, :QW]
            pair_ref[at] = done_ref[p, :, QW:]

    return pl.pallas_call(
        kernel,
        in_specs=[IN_SMEM] + [IN_VMEM] * 5,
        out_specs=[IN_VMEM] * 2,
        out_shape=[jax.ShapeDtypeStruct((64, 4, QW), BF16), jax.ShapeDtypeStruct((64, 4, PW), BF16)],
        compiler_params=pltpu.CompilerParams(vmem_limit_bytes=VMEM),
        cost_estimate=SMALL,
        name="merge_rows",
    )(order, far, near, near_log, new, done)


def on_device(
    tokens,
    query_weight,
    query_bias,
    pair_weight,
    pair_bias,
    cache_pairs,
    prefix_pairs,
    owner_slot,
    prefix_blocks,
    positions,
):
    prompts, _, new, width = tokens.shape
    me = lax.axis_index("roll")
    my_y, my_z, my_c = me // 8, me // 2 % 4, me % 2
    tp = lax.axis_index("tp")
    tp_y, tp_x = tp // 4, tp % 4
    pos = positions.reshape(prompts)

    own = prefix_pairs.reshape(4, 512, 2 * HD)
    below, above = over_roll(own, 0, 1, 0), over_roll(own, 0, 3, 0)
    far_a, far_b = over_roll(below[:2], 0, 1, 0), over_roll(above[2:], 0, 3, 0)
    kvs = [[own], [below], [above], [far_a, far_b]]
    kvs = kvs + [[over_roll(a, 0, 0, 1) for a in group] for group in kvs]

    x_o, x_m = sort_rows(
        jnp.stack([my_y, my_z, my_c]).astype(jnp.int32),
        jnp.broadcast_to(owner_slot[:, None], (prompts, new)).reshape(1, prompts * new),
        tokens.reshape(prompts * new, width),
    )

    def heads(*pairs):
        return jnp.stack([(tp_y + dy) % 2 * 4 + (tp_x + dx) % 4 for dy, dx in pairs]).astype(jnp.int32)

    weights = (query_weight, pair_weight)
    up_o, down_o, up_m, down_m = project(heads((0, 2), (1, 2)), [x_o, x_m], *weights, [[0], [1]])
    right_o, left_o, right_m, left_m = project(
        heads((0, 1), (1, 1), (0, 3), (1, 3)), [x_o, x_m], *weights, [[0, 1], [2, 3]]
    )
    own_o, own_m = project(heads((0, 0), (1, 0)), [x_o, x_m], *weights, [[0, 1]])

    def reduce(up, down, right, left, own):
        up, down = over_tp(up, 0, 1), over_tp(down, 0, 3)
        right, left = add_far(right, left, up, down)
        keep, send = sum_x(own, over_tp(right, 0, 1), over_tp(left, 0, 3))
        return keep, over_tp(send, 1, 0)

    full_o = reduce(up_o, down_o, right_o, left_o, own_o)
    full_m = reduce(up_m, down_m, right_m, left_m, own_m)

    index = jnp.arange(prompts, dtype=jnp.int32)
    half, quarter = jnp.arange(2, dtype=jnp.int32), jnp.arange(4, dtype=jnp.int32)
    y_of, c_of = (1 - half + my_y) % 2, (half + my_c) % 2
    z_of = (jnp.array([0, 3, 1, 2], jnp.int32) + my_z) % 4
    slot = (
        ((y_of[:, None, None, None] * 4 + z_of[None, None, :, None]) * 2 + c_of[None, :, None, None]) * 4
        + quarter[None, None, None, :]
    ).reshape(prompts)
    hit = owner_slot[None, :] == slot[:, None]
    order = jnp.sum(jnp.where(hit, index[None, :], 0), 1)
    limits = BLOCK * jnp.sum(jnp.where(hit, prefix_blocks[None, :], 0), 1)
    lengths = jnp.sum(jnp.where(hit, pos[None, :], 0), 1)
    my_limits = limits[32:]
    at = (limits[:, None] + lengths[:, None] + quarter[None, :]).reshape(prompts * new)
    frequency = jnp.exp(jnp.arange(HD // 2, dtype=F32) * (-2.0 * math.log(ROPE_BASE) / HD))
    angles = at.astype(F32)[:, None] * frequency[None, :]
    cosine, sine = jnp.cos(angles), jnp.sin(angles)
    tables = (
        jnp.concatenate([query_bias, pair_bias]).astype(F32)[None],
        jnp.concatenate([cosine, cosine], 1),
        jnp.concatenate([-sine, sine], 1),
    )
    cache = cache_pairs.reshape(prompts, 64, 2 * HD)

    q_o, new_o = make_queries(*full_o, *tables)
    far = over_roll(attend_prefix(my_limits, over_roll(q_o, 1, 0, 0), kvs), 1, 0, 0)
    near, near_log = attend_near(lengths, order, q_o, new_o, cache)
    done = attend(my_limits, lengths, order, *full_m, *tables, cache, kvs)
    attended, new_pairs = merge_rows(order, far, near, near_log, new_o.reshape(32, new, PW), done)
    return (
        attended.reshape(prompts, 1, new, QW),
        new_pairs.reshape(prompts, 1, new, 1, PW),
    )


def solution(mesh):
    return jax.shard_map(
        on_device,
        mesh=mesh,
        in_specs=(
            P(None, "roll", None, "tp"),
            P("tp", None),
            P("tp"),
            P("tp", None),
            P("tp"),
            P(None, "roll", None, "tp", None),
            P("roll", None, "tp", None),
            P(),
            P(),
            P(None, "roll"),
        ),
        out_specs=(P(None, "roll", None, "tp"), P(None, "roll", None, "tp", None)),
        check_vma=False,
    )
```

```python
import math

import jax
import jax.numpy as jnp
from jax import lax
from jax.experimental import pallas as pl
from jax.experimental.pallas import tpu as pltpu
from jax.sharding import PartitionSpec as P

BLOCK = 128
HD = 128
HEADS = 8
QW = HEADS * HD
PW = 2 * HD
COLS = QW + PW
ROWS = 128
ROPE_BASE = 1000000.0
NEG = -1e30
SCALE = HD ** -0.5
F32 = jnp.float32
BF16 = jnp.bfloat16
VMEM = 20 * 1024 * 1024
VMEM_PROJECT = 50 * 1024 * 1024


def tp_shift(dy, dx):
    return [(y * 4 + x, (y + dy) % 2 * 4 + (x + dx) % 4) for y in range(2) for x in range(4)]


def roll_shift(dy, dz, dc):
    return [
        ((y * 4 + z) * 2 + c, ((y + dy) % 2 * 4 + (z + dz) % 4) * 2 + (c + dc) % 2)
        for y in range(2)
        for z in range(4)
        for c in range(2)
    ]


def over_tp(a, dy, dx):
    return lax.ppermute(a, "tp", tp_shift(dy, dx))


def over_roll(a, dy, dz, dc):
    return lax.ppermute(a, "roll", roll_shift(dy, dz, dc))


def dot(a, b, dims=((1,), (0,))):
    return lax.dot_general(a, b, (dims, ((), ())), preferred_element_type=F32)


ANY = pl.BlockSpec(memory_space=pl.ANY)
IN_HBM = pl.BlockSpec(memory_space=pltpu.HBM)
IN_VMEM = pl.BlockSpec(memory_space=pltpu.VMEM)
SMALL = pl.CostEstimate(flops=10**6, bytes_accessed=10**5, transcendentals=0)
IN_SMEM = pl.BlockSpec(memory_space=pltpu.SMEM)


def project(heads, xs, wq, wp, groups):
    count = sum(len(g) for g in groups)
    depth = wq.shape[0]

    def kernel(heads_ref, *refs):
        x_refs, (wq_ref, wp_ref), rest = refs[: len(xs)], refs[len(xs) : len(xs) + 2], refs[len(xs) + 2 :]
        outs, (q_buf, p_buf, q_sem, p_sem) = rest[:-4], rest[-4:]
        copies = []
        for d in range(count):
            k = heads_ref[d]
            copies.append(
                (
                    pltpu.make_async_copy(
                        wq_ref.at[:, pl.ds(pl.multiple_of(k * QW, QW), QW)], q_buf.at[d], q_sem.at[d]
                    ),
                    pltpu.make_async_copy(
                        wp_ref.at[:, pl.ds(pl.multiple_of(k * PW, PW), PW)], p_buf.at[d], p_sem.at[d]
                    ),
                )
            )
        for pair in copies:
            for c in pair:
                c.start()
        x = jnp.concatenate([r[...] for r in x_refs], 0)
        d = 0
        for g, group in enumerate(groups):
            for i in range(len(group)):
                for c in copies[d]:
                    c.wait()
                for buf, low, high in ((q_buf, 0, QW), (p_buf, QW, COLS)):
                    y = dot(x, buf[d]).astype(BF16)
                    for b in range(len(xs)):
                        outs[b * len(groups) + g][i, :, low:high] = y[b * ROWS : (b + 1) * ROWS]
                d += 1

    return pl.pallas_call(
        kernel,
        in_specs=[IN_SMEM] + [IN_VMEM] * len(xs) + [IN_HBM, IN_HBM],
        out_specs=[IN_VMEM] * (len(xs) * len(groups)),
        out_shape=[jax.ShapeDtypeStruct((len(g), ROWS, COLS), BF16) for _ in xs for g in groups],
        scratch_shapes=[
            pltpu.VMEM((count, depth, QW), BF16),
            pltpu.VMEM((count, depth, PW), BF16),
            pltpu.SemaphoreType.DMA((count,)),
            pltpu.SemaphoreType.DMA((count,)),
        ],
        compiler_params=pltpu.CompilerParams(vmem_limit_bytes=VMEM_PROJECT),
        cost_estimate=SMALL,
        name="project",
    )(heads, *xs, wq, wp)


def sort_rows(place, owner, tokens):
    rows, width = tokens.shape

    def kernel(place_ref, owner_ref, x_ref, *outs):
        x = x_ref[...]
        for b, out in enumerate(outs):
            row = lax.broadcasted_iota(jnp.int32, (ROWS, rows), 0)
            col = lax.broadcasted_iota(jnp.int32, (ROWS, rows), 1)
            i = row // 4
            y, c, step, j = (1 - b + place_ref[0]) % 2, i // 16, i // 4 % 4, i % 4
            c = jnp.where(c == 0, place_ref[2], 1 - place_ref[2])
            z = (jnp.where(step == 1, 3, jnp.where(step == 0, 0, step - 1)) + place_ref[1]) % 4
            slot = ((y * 4 + z) * 2 + c) * 4 + j
            hit = (owner_ref[...] == slot) & (col % 4 == row % 4)
            out[...] = dot(jnp.where(hit, 1.0, 0.0).astype(BF16), x).astype(BF16)

    return pl.pallas_call(
        kernel,
        in_specs=[IN_SMEM, IN_VMEM, IN_VMEM],
        out_specs=[IN_VMEM] * 2,
        out_shape=[jax.ShapeDtypeStruct((ROWS, width), BF16)] * 2,
        compiler_params=pltpu.CompilerParams(vmem_limit_bytes=VMEM),
        cost_estimate=SMALL,
        name="sort_rows",
    )(place, owner, tokens)


def add_far(right, left, up, down):
    def kernel(r, l, u, d, r_out, l_out):
        r_out[...] = (r[...].astype(F32) + u[...].astype(F32)).astype(BF16)
        l_out[...] = (l[...].astype(F32) + d[...].astype(F32)).astype(BF16)

    block = [pl.BlockSpec((1, ROWS, COLS), lambda i, h=h: (h, 0, 0)) for h in (0, 1)]
    return pl.pallas_call(
        kernel,
        grid=(1,),
        in_specs=block + [block[0]] * 2,
        out_specs=block,
        out_shape=[jax.ShapeDtypeStruct(right.shape, BF16)] * 2,
        input_output_aliases={0: 0, 1: 1},
        compiler_params=pltpu.CompilerParams(vmem_limit_bytes=VMEM),
        cost_estimate=SMALL,
        name="add_far",
    )(right, left, up, down)


def sum_x(own, from_left, from_right):
    def kernel(a, b, c, keep, send):
        for i, out in enumerate((keep, send)):
            out[...] = (a[i].astype(F32) + b[i].astype(F32) + c[i].astype(F32)).astype(out.dtype)

    return pl.pallas_call(
        kernel,
        in_specs=[IN_VMEM] * 3,
        out_specs=[IN_VMEM] * 2,
        out_shape=[jax.ShapeDtypeStruct((ROWS, COLS), F32), jax.ShapeDtypeStruct((ROWS, COLS), BF16)],
        compiler_params=pltpu.CompilerParams(vmem_limit_bytes=VMEM),
        cost_estimate=SMALL,
        name="sum_x",
    )(own, from_left, from_right)


def rotated(keep_ref, more_ref, bias_ref, cos_ref, sin_ref, first, q_buf):
    cos, sin = cos_ref[first : first + ROWS, :], sin_ref[first : first + ROWS, :]

    def turn(v):
        return v * cos + pltpu.roll(v, HD // 2, 1) * sin

    for h in range(HEADS):
        low, high = h * HD, h * HD + HD
        v = turn(keep_ref[:, low:high] + more_ref[:, low:high].astype(F32) + bias_ref[:, low:high])
        for p in range(32):
            q_buf[32 * p + 4 * h : 32 * p + 4 * h + 4, :] = v[4 * p : 4 * p + 4]
    u = keep_ref[:, QW:] + more_ref[:, QW:].astype(F32) + bias_ref[:, QW:]
    return jnp.concatenate([turn(u[:, :HD]), u[:, HD:]], 1)


def prefix_scores(q, buf, limit_ref, g):
    parts = []
    for i in range(4):
        p = 4 * g + i
        s = dot(q[32 * i : 32 * i + 32], buf[p, :, :HD], ((1,), (1,))) * SCALE
        col = lax.broadcasted_iota(jnp.int32, s.shape, 1)
        parts.append(jnp.where(col < limit_ref[p], s, NEG))
    return jnp.concatenate(parts, 0)


def prefix_values(w, buf, g):
    w = w.astype(BF16)
    return jnp.concatenate([dot(w[32 * i : 32 * i + 32], buf[4 * g + i, :, HD:]) for i in range(4)], 0)


def near_scores(q, cbuf, new, length_ref, g):
    sc = dot(q, cbuf[4 * g : 4 * g + 4, :, :HD].reshape(256, HD), ((1,), (1,))) * SCALE
    row = lax.broadcasted_iota(jnp.int32, sc.shape, 0)
    col = lax.broadcasted_iota(jnp.int32, sc.shape, 1)
    length = jnp.zeros(sc.shape, jnp.int32)
    for i in range(4):
        length = jnp.where(row // 32 == i, length_ref[4 * g + i], length)
    sc = jnp.where((row // 32 == col // 64) & (col % 64 < length), sc, NEG)
    sn = dot(q, new[:, :HD], ((1,), (1,))) * SCALE
    row = lax.broadcasted_iota(jnp.int32, sn.shape, 0)
    col = lax.broadcasted_iota(jnp.int32, sn.shape, 1)
    sn = jnp.where((row // 32 == col // 4) & (col % 4 <= row % 4), sn, NEG)
    return sc, sn


def near_values(wc, wn, cbuf, new, g):
    o = dot(wc.astype(BF16), cbuf[4 * g : 4 * g + 4, :, HD:].reshape(256, HD))
    return o + dot(wn.astype(BF16), new[:, HD:])


def softmax(*scores):
    top = jnp.max(scores[0], -1, keepdims=True)
    for s in scores[1:]:
        top = jnp.maximum(top, jnp.max(s, -1, keepdims=True))
    weights = [jnp.exp(s - top) for s in scores]
    total = jnp.sum(weights[0], -1, keepdims=True)
    for w in weights[1:]:
        total = total + jnp.sum(w, -1, keepdims=True)
    return top, weights, total


def prefix_copies(refs, buf, sem):
    return [pltpu.make_async_copy(refs[g], buf.at[pl.ds(4 * g, 4)], sem.at[g]) for g in range(8)]


def cache_copies(cache_ref, at_ref, first, cbuf, sem):
    return [
        pltpu.make_async_copy(cache_ref.at[at_ref[first + p]], cbuf.at[p], sem.at[p]) for p in range(32)
    ]


CACHE_SCRATCH = [pltpu.VMEM((32, 64, 2 * HD), BF16), pltpu.SemaphoreType.DMA((32,))]


def attend(limits, lengths, order, keep, more, bias, cosine, sine, cache, kvs):
    def kernel(limit_ref, length_ref, at_ref, keep_ref, more_ref, bias_ref, cos_ref, sin_ref, cache_ref, *refs):
        o_ref, buf, sem, qbuf, cbuf, csem = refs[len(kvs) :]
        prefix = prefix_copies(refs, buf, sem)
        caches = cache_copies(cache_ref, at_ref, 32, cbuf, csem)
        for g in range(8):
            for c in [prefix[g]] + caches[4 * g : 4 * g + 4]:
                c.start()
        new_all = rotated(keep_ref, more_ref, bias_ref, cos_ref, sin_ref, ROWS, qbuf)
        for p in range(32):
            o_ref[p, :, QW:] = new_all[4 * p : 4 * p + 4].astype(BF16)
        new_all = new_all.astype(BF16)
        for g in range(8):
            for c in [prefix[g]] + caches[4 * g : 4 * g + 4]:
                c.wait()
            q = qbuf[128 * g : 128 * g + 128, :].astype(BF16)
            new = new_all[16 * g : 16 * g + 16]
            sp = prefix_scores(q, buf, limit_ref, g)
            sc, sn = near_scores(q, cbuf, new, length_ref.at[pl.ds(32, 32)], g)
            _, (wp, wc, wn), total = softmax(sp, sc, sn)
            o = (prefix_values(wp, buf, g) + near_values(wc, wn, cbuf, new, g)) / total
            for i in range(4):
                for h in range(HEADS):
                    o_ref[4 * g + i, :, h * HD : h * HD + HD] = o[
                        32 * i + 4 * h : 32 * i + 4 * h + 4
                    ].astype(BF16)

    return pl.pallas_call(
        kernel,
        in_specs=[IN_SMEM] * 3 + [IN_VMEM] * 5 + [ANY] * (1 + len(kvs)),
        out_specs=IN_VMEM,
        out_shape=jax.ShapeDtypeStruct((32, 4, COLS), BF16),
        scratch_shapes=[
            pltpu.VMEM((32, 512, 2 * HD), BF16),
            pltpu.SemaphoreType.DMA((len(kvs),)),
            pltpu.VMEM((1024, HD), F32),
        ]
        + CACHE_SCRATCH,
        compiler_params=pltpu.CompilerParams(vmem_limit_bytes=VMEM),
        cost_estimate=SMALL,
        name="attend",
    )(limits, lengths, order, keep, more, bias, cosine, sine, cache, *kvs)


def make_queries(keep, more, bias, cosine, sine):
    def kernel(keep_ref, more_ref, bias_ref, cos_ref, sin_ref, q_ref, new_ref, qbuf):
        new_ref[...] = rotated(keep_ref, more_ref, bias_ref, cos_ref, sin_ref, 0, qbuf).astype(BF16)
        q_ref[...] = qbuf[...].astype(BF16).reshape(32, 32, HD)

    return pl.pallas_call(
        kernel,
        in_specs=[IN_VMEM] * 5,
        out_specs=[IN_VMEM] * 2,
        out_shape=[jax.ShapeDtypeStruct((32, 32, HD), BF16), jax.ShapeDtypeStruct((ROWS, PW), BF16)],
        scratch_shapes=[pltpu.VMEM((1024, HD), F32)],
        compiler_params=pltpu.CompilerParams(vmem_limit_bytes=VMEM),
        cost_estimate=SMALL,
        name="make_queries",
    )(keep, more, bias, cosine, sine)


def attend_prefix(limits, q, kvs):
    def kernel(limit_ref, q_ref, *refs):
        o_ref, buf, sem = refs[len(kvs) :]
        prefix = prefix_copies(refs, buf, sem)
        for c in prefix:
            c.start()
        lane = lax.broadcasted_iota(jnp.int32, (32, 128), 1)
        stats = jnp.zeros((32, 128), F32)
        for g in range(8):
            prefix[g].wait()
            q = q_ref[4 * g : 4 * g + 4].reshape(128, HD)
            top, (w,), total = softmax(prefix_scores(q, buf, limit_ref, g))
            o = prefix_values(w, buf, g) / total
            o_ref[4 * g : 4 * g + 4] = o.astype(BF16).reshape(4, 32, HD)
            rest = top + jnp.log(total)
            for part in range(3):
                piece = rest.astype(BF16).astype(F32)
                for i in range(4):
                    stats = jnp.where(lane == 3 * (4 * g + i) + part, piece[32 * i : 32 * i + 32], stats)
                rest = rest - piece
        o_ref[32] = stats.astype(BF16)

    return pl.pallas_call(
        kernel,
        in_specs=[IN_SMEM, IN_VMEM] + [ANY] * len(kvs),
        out_specs=IN_VMEM,
        out_shape=jax.ShapeDtypeStruct((33, 32, HD), BF16),
        scratch_shapes=[pltpu.VMEM((32, 512, 2 * HD), BF16), pltpu.SemaphoreType.DMA((len(kvs),))],
        compiler_params=pltpu.CompilerParams(vmem_limit_bytes=VMEM),
        cost_estimate=SMALL,
        name="attend_prefix",
    )(limits, q, *kvs)


def attend_near(lengths, order, q, new, cache):
    def kernel(length_ref, at_ref, q_ref, new_ref, cache_ref, o_ref, l_ref, cbuf, csem):
        caches = cache_copies(cache_ref, at_ref, 0, cbuf, csem)
        for c in caches:
            c.start()
        for g in range(8):
            for c in caches[4 * g : 4 * g + 4]:
                c.wait()
            q = q_ref[4 * g : 4 * g + 4].reshape(128, HD)
            new = new_ref[16 * g : 16 * g + 16]
            top, (wc, wn), total = softmax(*near_scores(q, cbuf, new, length_ref, g))
            o_ref[128 * g : 128 * g + 128] = near_values(wc, wn, cbuf, new, g) / total
            l_ref[128 * g : 128 * g + 128] = jnp.broadcast_to(top + jnp.log(total), (128, HD))

    return pl.pallas_call(
        kernel,
        in_specs=[IN_SMEM] * 2 + [IN_VMEM] * 2 + [ANY],
        out_specs=[IN_VMEM] * 2,
        out_shape=[jax.ShapeDtypeStruct((1024, HD), F32)] * 2,
        scratch_shapes=CACHE_SCRATCH,
        compiler_params=pltpu.CompilerParams(vmem_limit_bytes=VMEM),
        cost_estimate=SMALL,
        name="attend_near",
    )(lengths, order, q, new, cache)


def merge_rows(order, far, near, near_log, new, done):
    def kernel(order_ref, far_ref, o_ref, l_ref, new_ref, done_ref, out_ref, pair_ref):
        stats = far_ref[32].astype(F32)
        for p in range(32):
            at = order_ref[p]
            theirs = jnp.sum(stats[:, 3 * p : 3 * p + 3], -1, keepdims=True)
            ours = l_ref[32 * p : 32 * p + 32]
            top = jnp.maximum(theirs, ours)
            wt, wo = jnp.exp(theirs - top), jnp.exp(ours - top)
            o = (far_ref[p].astype(F32) * wt + o_ref[32 * p : 32 * p + 32] * wo) / (wt + wo)
            for h in range(HEADS):
                out_ref[at, :, h * HD : h * HD + HD] = o[4 * h : 4 * h + 4].astype(BF16)
            pair_ref[at] = new_ref[p]
            at = order_ref[32 + p]
            out_ref[at] = done_ref[p, :, :QW]
            pair_ref[at] = done_ref[p, :, QW:]

    return pl.pallas_call(
        kernel,
        in_specs=[IN_SMEM] + [IN_VMEM] * 5,
        out_specs=[IN_VMEM] * 2,
        out_shape=[jax.ShapeDtypeStruct((64, 4, QW), BF16), jax.ShapeDtypeStruct((64, 4, PW), BF16)],
        compiler_params=pltpu.CompilerParams(vmem_limit_bytes=VMEM),
        cost_estimate=SMALL,
        name="merge_rows",
    )(order, far, near, near_log, new, done)


def on_device(
    tokens,
    query_weight,
    query_bias,
    pair_weight,
    pair_bias,
    cache_pairs,
    prefix_pairs,
    owner_slot,
    prefix_blocks,
    positions,
):
    prompts, _, new, width = tokens.shape
    me = lax.axis_index("roll")
    my_y, my_z, my_c = me // 8, me // 2 % 4, me % 2
    tp = lax.axis_index("tp")
    tp_y, tp_x = tp // 4, tp % 4
    pos = positions.reshape(prompts)

    own = prefix_pairs.reshape(4, 512, 2 * HD)
    below, above = over_roll(own, 0, 1, 0), over_roll(own, 0, 3, 0)
    kvs = [own, below, above, over_roll(below, 0, 1, 0)]
    kvs = kvs + [over_roll(a, 0, 0, 1) for a in kvs]

    x_o, x_m = sort_rows(
        jnp.stack([my_y, my_z, my_c]).astype(jnp.int32),
        jnp.broadcast_to(owner_slot[:, None], (prompts, new)).reshape(1, prompts * new),
        tokens.reshape(prompts * new, width),
    )

    def heads(*pairs):
        return jnp.stack([(tp_y + dy) % 2 * 4 + (tp_x + dx) % 4 for dy, dx in pairs]).astype(jnp.int32)

    weights = (query_weight, pair_weight)
    up_o, down_o, up_m, down_m = project(heads((0, 2), (1, 2)), [x_o, x_m], *weights, [[0], [1]])
    right_o, left_o, right_m, left_m = project(
        heads((0, 1), (1, 1), (0, 3), (1, 3)), [x_o, x_m], *weights, [[0, 1], [2, 3]]
    )
    own_o, own_m = project(heads((0, 0), (1, 0)), [x_o, x_m], *weights, [[0, 1]])

    def reduce(up, down, right, left, own):
        up, down = over_tp(up, 0, 1), over_tp(down, 0, 3)
        right, left = add_far(right, left, up, down)
        keep, send = sum_x(own, over_tp(right, 0, 1), over_tp(left, 0, 3))
        return keep, over_tp(send, 1, 0)

    full_o = reduce(up_o, down_o, right_o, left_o, own_o)
    full_m = reduce(up_m, down_m, right_m, left_m, own_m)

    index = jnp.arange(prompts, dtype=jnp.int32)
    half, quarter = jnp.arange(2, dtype=jnp.int32), jnp.arange(4, dtype=jnp.int32)
    y_of, c_of = (1 - half + my_y) % 2, (half + my_c) % 2
    z_of = (jnp.array([0, 3, 1, 2], jnp.int32) + my_z) % 4
    slot = (
        ((y_of[:, None, None, None] * 4 + z_of[None, None, :, None]) * 2 + c_of[None, :, None, None]) * 4
        + quarter[None, None, None, :]
    ).reshape(prompts)
    hit = owner_slot[None, :] == slot[:, None]
    order = jnp.sum(jnp.where(hit, index[None, :], 0), 1)
    limits = BLOCK * jnp.sum(jnp.where(hit, prefix_blocks[None, :], 0), 1)
    lengths = jnp.sum(jnp.where(hit, pos[None, :], 0), 1)
    my_limits = limits[32:]
    at = (limits[:, None] + lengths[:, None] + quarter[None, :]).reshape(prompts * new)
    frequency = jnp.exp(jnp.arange(HD // 2, dtype=F32) * (-2.0 * math.log(ROPE_BASE) / HD))
    angles = at.astype(F32)[:, None] * frequency[None, :]
    cosine, sine = jnp.cos(angles), jnp.sin(angles)
    tables = (
        jnp.concatenate([query_bias, pair_bias]).astype(F32)[None],
        jnp.concatenate([cosine, cosine], 1),
        jnp.concatenate([-sine, sine], 1),
    )
    cache = cache_pairs.reshape(prompts, 64, 2 * HD)

    q_o, new_o = make_queries(*full_o, *tables)
    far = over_roll(attend_prefix(my_limits, over_roll(q_o, 1, 0, 0), kvs), 1, 0, 0)
    near, near_log = attend_near(lengths, order, q_o, new_o, cache)
    done = attend(my_limits, lengths, order, *full_m, *tables, cache, kvs)
    attended, new_pairs = merge_rows(order, far, near, near_log, new_o.reshape(32, new, PW), done)
    return (
        attended.reshape(prompts, 1, new, QW),
        new_pairs.reshape(prompts, 1, new, 1, PW),
    )


def solution(mesh):
    return jax.shard_map(
        on_device,
        mesh=mesh,
        in_specs=(
            P(None, "roll", None, "tp"),
            P("tp", None),
            P("tp"),
            P("tp", None),
            P("tp"),
            P(None, "roll", None, "tp", None),
            P("roll", None, "tp", None),
            P(),
            P(),
            P(None, "roll"),
        ),
        out_specs=(P(None, "roll", None, "tp"), P(None, "roll", None, "tp", None)),
        check_vma=False,
    )
```

```python
import math

import jax
import jax.numpy as jnp
from jax import lax
from jax.experimental import pallas as pl
from jax.experimental.pallas import tpu as pltpu
from jax.sharding import PartitionSpec as P

BLOCK = 128
HD = 128
HEADS = 8
QW = HEADS * HD
PW = 2 * HD
COLS = QW + PW
ROWS = 128
ROPE_BASE = 1000000.0
NEG = -1e30
LOG2_SCALE = HD ** -0.5 / math.log(2.0)
F32 = jnp.float32
BF16 = jnp.bfloat16
VMEM = 20 * 1024 * 1024
VMEM_PROJECT = 50 * 1024 * 1024


def tp_shift(dy, dx):
    return [(y * 4 + x, (y + dy) % 2 * 4 + (x + dx) % 4) for y in range(2) for x in range(4)]


def roll_shift(dy, dz, dc):
    return [
        ((y * 4 + z) * 2 + c, ((y + dy) % 2 * 4 + (z + dz) % 4) * 2 + (c + dc) % 2)
        for y in range(2)
        for z in range(4)
        for c in range(2)
    ]


def over_tp(a, dy, dx):
    return lax.ppermute(a, "tp", tp_shift(dy, dx))


def over_roll(a, dy, dz, dc):
    return lax.ppermute(a, "roll", roll_shift(dy, dz, dc))


def dot(a, b, dims=((1,), (0,))):
    return lax.dot_general(a, b, (dims, ((), ())), preferred_element_type=F32)


ANY = pl.BlockSpec(memory_space=pl.ANY)
IN_HBM = pl.BlockSpec(memory_space=pltpu.HBM)
IN_VMEM = pl.BlockSpec(memory_space=pltpu.VMEM)


def cost(us):
    return pl.CostEstimate(flops=10**6, bytes_accessed=int(us * 2_500_000), transcendentals=0)


SMALL = cost(0.04)
IN_SMEM = pl.BlockSpec(memory_space=pltpu.SMEM)


def project(heads, xs, wq, wp, groups, after=()):
    count = sum(len(g) for g in groups)
    depth = wq.shape[0]

    def kernel(heads_ref, *refs):
        x_refs, (wq_ref, wp_ref) = refs[: len(xs)], refs[len(xs) : len(xs) + 2]
        rest = refs[len(xs) + 2 + len(after) :]
        outs, (q_buf, p_buf, q_sem, p_sem) = rest[:-4], rest[-4:]
        copies = []
        for d in range(count):
            k = heads_ref[d]
            copies.append(
                (
                    pltpu.make_async_copy(
                        wq_ref.at[:, pl.ds(pl.multiple_of(k * QW, QW), QW)], q_buf.at[d], q_sem.at[d]
                    ),
                    pltpu.make_async_copy(
                        wp_ref.at[:, pl.ds(pl.multiple_of(k * PW, PW), PW)], p_buf.at[d], p_sem.at[d]
                    ),
                )
            )
        for pair in copies:
            for c in pair:
                c.start()
        x = jnp.concatenate([r[...] for r in x_refs], 0)
        d = 0
        for g, group in enumerate(groups):
            for i in range(len(group)):
                for c in copies[d]:
                    c.wait()
                for buf, low, high in ((q_buf, 0, QW), (p_buf, QW, COLS)):
                    y = dot(x, buf[d]).astype(BF16)
                    for b in range(len(xs)):
                        outs[b * len(groups) + g][i, :, low:high] = y[b * ROWS : (b + 1) * ROWS]
                d += 1

    return pl.pallas_call(
        kernel,
        in_specs=[IN_SMEM] + [IN_VMEM] * len(xs) + [IN_HBM, IN_HBM] + [ANY] * len(after),
        out_specs=[IN_VMEM] * (len(xs) * len(groups)),
        out_shape=[jax.ShapeDtypeStruct((len(g), ROWS, COLS), BF16) for _ in xs for g in groups],
        scratch_shapes=[
            pltpu.VMEM((count, depth, QW), BF16),
            pltpu.VMEM((count, depth, PW), BF16),
            pltpu.SemaphoreType.DMA((count,)),
            pltpu.SemaphoreType.DMA((count,)),
        ],
        compiler_params=pltpu.CompilerParams(vmem_limit_bytes=VMEM_PROJECT),
        cost_estimate=SMALL,
        name="project",
    )(heads, *xs, wq, wp, *after)


def sort_rows(place, owner, tokens):
    rows, width = tokens.shape

    def kernel(place_ref, owner_ref, x_ref, *outs):
        x = x_ref[...]
        for b, out in enumerate(outs):
            row = lax.broadcasted_iota(jnp.int32, (ROWS, rows), 0)
            col = lax.broadcasted_iota(jnp.int32, (ROWS, rows), 1)
            i = row // 4
            y, c, step, j = (1 - b + place_ref[0]) % 2, i // 16, i // 4 % 4, i % 4
            c = jnp.where(c == 0, place_ref[2], 1 - place_ref[2])
            z = (jnp.where(step == 1, 3, jnp.where(step == 0, 0, step - 1)) + place_ref[1]) % 4
            slot = ((y * 4 + z) * 2 + c) * 4 + j
            hit = (owner_ref[...] == slot) & (col % 4 == row % 4)
            out[...] = dot(jnp.where(hit, 1.0, 0.0).astype(BF16), x).astype(BF16)

    return pl.pallas_call(
        kernel,
        in_specs=[IN_SMEM, IN_VMEM, IN_VMEM],
        out_specs=[IN_VMEM] * 2,
        out_shape=[jax.ShapeDtypeStruct((ROWS, width), BF16)] * 2,
        compiler_params=pltpu.CompilerParams(vmem_limit_bytes=VMEM),
        cost_estimate=SMALL,
        name="sort_rows",
    )(place, owner, tokens)


def add_far(right, left, up, down, after):
    def kernel(r, l, u, d, *refs):
        r_out, l_out = refs[len(after) :]
        r_out[...] = (r[...].astype(F32) + u[...].astype(F32)).astype(BF16)
        l_out[...] = (l[...].astype(F32) + d[...].astype(F32)).astype(BF16)

    block = [pl.BlockSpec((1, ROWS, COLS), lambda i, h=h: (h, 0, 0)) for h in (0, 1)]
    return pl.pallas_call(
        kernel,
        grid=(1,),
        in_specs=block + [block[0]] * 2 + [ANY] * len(after),
        out_specs=block,
        out_shape=[jax.ShapeDtypeStruct(right.shape, BF16)] * 2,
        input_output_aliases={0: 0, 1: 1},
        compiler_params=pltpu.CompilerParams(vmem_limit_bytes=VMEM),
        cost_estimate=SMALL,
        name="add_far",
    )(right, left, up, down, *after)


def turn_far(core, below, above, after):
    count = below.shape[0]

    def kernel(core_ref, below_ref, above_ref, after_ref, o_ref, both_ref, sem):
        copies = [
            pltpu.make_async_copy(below_ref, both_ref.at[pl.ds(0, count)], sem.at[0]),
            pltpu.make_async_copy(above_ref, both_ref.at[pl.ds(count, count)], sem.at[1]),
        ]
        for c in copies:
            c.start()
        for c in copies:
            c.wait()
        o_ref[...] = both_ref[pl.ds(pl.multiple_of(core_ref[0] * count, count), count)]

    return pl.pallas_call(
        kernel,
        in_specs=[IN_SMEM, ANY, ANY, ANY],
        out_specs=[IN_VMEM] * 2,
        out_shape=[
            jax.ShapeDtypeStruct(below.shape, BF16),
            jax.ShapeDtypeStruct((2 * count,) + below.shape[1:], BF16),
        ],
        scratch_shapes=[pltpu.SemaphoreType.DMA((2,))],
        compiler_params=pltpu.CompilerParams(vmem_limit_bytes=VMEM),
        cost_estimate=SMALL,
        name="turn_far",
    )(core, below, above, after)


def hold(array, after):
    def kernel(*refs):
        pass

    return pl.pallas_call(
        kernel,
        in_specs=[ANY] * 2,
        out_specs=ANY,
        out_shape=jax.ShapeDtypeStruct(array.shape, array.dtype),
        input_output_aliases={0: 0},
        cost_estimate=SMALL,
        name="hold",
    )(array, after)


def prefix_copies(refs, buf, sem):
    sources = []
    for own, both, far in (refs[:3], refs[3:6]):
        sources += [own, both.at[pl.ds(0, 4)], both.at[pl.ds(4, 4)], far]
    return [
        pltpu.make_async_copy(sources[g], buf.at[pl.ds(4 * g, 4), pl.ds(0, 512)], sem.at[g]) for g in range(8)
    ]


def sum_x(own, from_left, from_right):
    def kernel(a, b, c, keep, send):
        for i, out in enumerate((keep, send)):
            out[...] = (a[i].astype(F32) + b[i].astype(F32) + c[i].astype(F32)).astype(out.dtype)

    return pl.pallas_call(
        kernel,
        in_specs=[IN_VMEM] * 3,
        out_specs=[IN_VMEM] * 2,
        out_shape=[jax.ShapeDtypeStruct((ROWS, COLS), F32), jax.ShapeDtypeStruct((ROWS, COLS), BF16)],
        compiler_params=pltpu.CompilerParams(vmem_limit_bytes=VMEM),
        cost_estimate=SMALL,
        name="sum_x",
    )(own, from_left, from_right)


def rotated(keep_ref, more_ref, bias_ref, cos_ref, sin_ref, first, q_buf):
    cos, sin = cos_ref[first : first + ROWS, :], sin_ref[first : first + ROWS, :]

    def turn(v):
        return v * cos + pltpu.roll(v, HD // 2, 1) * sin

    for h in range(HEADS):
        low, high = h * HD, h * HD + HD
        v = turn(keep_ref[:, low:high] + more_ref[:, low:high].astype(F32) + bias_ref[:, low:high])
        for p in range(32):
            q_buf[32 * p + 4 * h : 32 * p + 4 * h + 4, :] = v[4 * p : 4 * p + 4]
    u = keep_ref[:, QW:] + more_ref[:, QW:].astype(F32) + bias_ref[:, QW:]
    return jnp.concatenate([turn(u[:, :HD]), u[:, HD:]], 1)


def masked_scores(q, keys, valid):
    return jnp.where(valid, dot(q, keys, ((1,), (1,))) * LOG2_SCALE, NEG)


def weigh(s_buf, w_buf, top_buf, sum_buf):
    for g in range(8):
        rows = slice(128 * g, 128 * g + 128)
        s = s_buf[rows, :]
        top = jnp.max(s, -1, keepdims=True)
        w = jnp.exp2(s - top)
        w_buf[rows, :] = w.astype(BF16)
        top_buf[rows, :] = top
        sum_buf[rows, :] = jnp.sum(w, -1, keepdims=True)


def new_block(new_ref_rows):
    return jnp.concatenate([new_ref_rows, jnp.zeros((12, PW), F32)], 0).astype(BF16)


def buffers(keys):
    return [
        pltpu.VMEM((32, keys, PW), BF16),
        pltpu.VMEM((1024, keys), F32),
        pltpu.VMEM((1024, keys), BF16),
        pltpu.VMEM((1024, 1), F32),
        pltpu.VMEM((1024, 1), F32),
    ]


def pack_logs(top_buf, sum_buf):
    lane = lax.broadcasted_iota(jnp.int32, (32, 128), 1)
    packed = jnp.zeros((32, 128), F32)
    for p in range(32):
        rows = slice(32 * p, 32 * p + 32)
        packed = jnp.where(lane == 4 * p, top_buf[rows, :] + jnp.log2(sum_buf[rows, :]), packed)
    return packed


def attend(limits, lengths, order, keep, more, bias, cosine, sine, cache, kvs):
    keys = 512 + 64 + 16

    def kernel(limit_ref, length_ref, at_ref, keep_ref, more_ref, bias_ref, cos_ref, sin_ref, cache_ref, *refs):
        o_ref, buf, s_buf, w_buf, top_buf, sum_buf, qbuf, sem, csem = refs[6:]
        copies = prefix_copies(refs, buf, sem) + [
            pltpu.make_async_copy(cache_ref.at[at_ref[32 + p]], buf.at[p, pl.ds(512, 64)], csem.at[p])
            for p in range(32)
        ]
        for c in copies:
            c.start()
        new_all = rotated(keep_ref, more_ref, bias_ref, cos_ref, sin_ref, ROWS, qbuf)
        for p in range(32):
            o_ref[p, :, QW:] = new_all[4 * p : 4 * p + 4].astype(BF16)
            buf[p, 576:592, :] = new_block(new_all[4 * p : 4 * p + 4])
        row = lax.broadcasted_iota(jnp.int32, (32, keys), 0)
        col = lax.broadcasted_iota(jnp.int32, (32, keys), 1)
        fresh = (col >= 576) & (col - 576 <= row & 3)
        for c in copies:
            c.wait()
        for p in range(32):
            valid = (col < limit_ref[p]) | ((col >= 512) & (col < 512 + length_ref[32 + p])) | fresh
            rows = slice(32 * p, 32 * p + 32)
            s_buf[rows, :] = masked_scores(qbuf[rows, :].astype(BF16), buf[p, :, :HD], valid)
        weigh(s_buf, w_buf, top_buf, sum_buf)
        for p in range(32):
            rows = slice(32 * p, 32 * p + 32)
            o = dot(w_buf[rows, :], buf[p, :, HD:]) / sum_buf[rows, :]
            for h in range(HEADS):
                o_ref[p, :, h * HD : h * HD + HD] = o[4 * h : 4 * h + 4].astype(BF16)

    return pl.pallas_call(
        kernel,
        in_specs=[IN_SMEM] * 3 + [IN_VMEM] * 5 + [ANY] * 7,
        out_specs=IN_VMEM,
        out_shape=jax.ShapeDtypeStruct((32, 4, COLS), BF16),
        scratch_shapes=buffers(keys)
        + [pltpu.VMEM((1024, HD), F32), pltpu.SemaphoreType.DMA((8,)), pltpu.SemaphoreType.DMA((32,))],
        compiler_params=pltpu.CompilerParams(vmem_limit_bytes=VMEM),
        cost_estimate=SMALL,
        name="attend",
    )(limits, lengths, order, keep, more, bias, cosine, sine, cache, *kvs)


def make_queries(keep, more, bias, cosine, sine, after):
    def kernel(keep_ref, more_ref, bias_ref, cos_ref, sin_ref, after_ref, q_ref, new_ref, qbuf):
        new_ref[...] = rotated(keep_ref, more_ref, bias_ref, cos_ref, sin_ref, 0, qbuf).astype(BF16)
        q_ref[...] = qbuf[...].astype(BF16).reshape(32, 32, HD)

    return pl.pallas_call(
        kernel,
        in_specs=[IN_VMEM] * 5 + [ANY],
        out_specs=[IN_VMEM] * 2,
        out_shape=[jax.ShapeDtypeStruct((32, 32, HD), BF16), jax.ShapeDtypeStruct((ROWS, PW), BF16)],
        scratch_shapes=[pltpu.VMEM((1024, HD), F32)],
        compiler_params=pltpu.CompilerParams(vmem_limit_bytes=VMEM),
        cost_estimate=SMALL,
        name="make_queries",
    )(keep, more, bias, cosine, sine, after)


def attend_prefix(limits, q, kvs):
    keys = 512

    def kernel(limit_ref, q_ref, *refs):
        o_ref, buf, s_buf, w_buf, top_buf, sum_buf, sem = refs[6:]
        copies = prefix_copies(refs, buf, sem)
        for c in copies:
            c.start()
        col = lax.broadcasted_iota(jnp.int32, (32, keys), 1)
        for g in range(8):
            copies[g].wait()
            for p in range(4 * g, 4 * g + 4):
                s_buf[32 * p : 32 * p + 32, :] = masked_scores(q_ref[p], buf[p, :, :HD], col < limit_ref[p])
        weigh(s_buf, w_buf, top_buf, sum_buf)
        for p in range(32):
            rows = slice(32 * p, 32 * p + 32)
            o_ref[p] = (dot(w_buf[rows, :], buf[p, :, HD:]) / sum_buf[rows, :]).astype(BF16)
        rest = pack_logs(top_buf, sum_buf)
        lane = lax.broadcasted_iota(jnp.int32, (32, 128), 1)
        packed = jnp.zeros((32, 128), F32)
        for part in range(3):
            piece = rest.astype(BF16).astype(F32)
            packed = jnp.where(lane % 4 == part, pltpu.roll(piece, part, 1), packed)
            rest = rest - piece
        o_ref[32] = packed.astype(BF16)

    return pl.pallas_call(
        kernel,
        in_specs=[IN_SMEM, IN_VMEM] + [ANY] * 6,
        out_specs=IN_VMEM,
        out_shape=jax.ShapeDtypeStruct((33, 32, HD), BF16),
        scratch_shapes=buffers(keys) + [pltpu.SemaphoreType.DMA((8,))],
        compiler_params=pltpu.CompilerParams(vmem_limit_bytes=VMEM),
        cost_estimate=SMALL,
        name="attend_prefix",
    )(limits, q, *kvs)


def attend_near(lengths, order, q, new, cache, after):
    keys = 64 + 16

    def kernel(
        length_ref, at_ref, q_ref, new_ref, cache_ref, after_ref, o_ref, buf, s_buf, w_buf, top_buf, sum_buf, sem
    ):
        copies = [
            pltpu.make_async_copy(cache_ref.at[at_ref[p]], buf.at[p, pl.ds(0, 64)], sem.at[p])
            for p in range(32)
        ]
        for c in copies:
            c.start()
        for p in range(32):
            buf[p, 64:80, :] = new_block(new_ref[4 * p : 4 * p + 4].astype(F32))
        row = lax.broadcasted_iota(jnp.int32, (32, keys), 0)
        col = lax.broadcasted_iota(jnp.int32, (32, keys), 1)
        fresh = (col >= 64) & (col - 64 <= row & 3)
        for c in copies:
            c.wait()
        for p in range(32):
            valid = (col < length_ref[p]) | fresh
            s_buf[32 * p : 32 * p + 32, :] = masked_scores(q_ref[p], buf[p, :, :HD], valid)
        weigh(s_buf, w_buf, top_buf, sum_buf)
        for p in range(32):
            rows = slice(32 * p, 32 * p + 32)
            o_ref[p] = dot(w_buf[rows, :], buf[p, :, HD:]) / sum_buf[rows, :]
        o_ref[32] = pack_logs(top_buf, sum_buf)

    return pl.pallas_call(
        kernel,
        in_specs=[IN_SMEM] * 2 + [IN_VMEM] * 2 + [ANY] * 2,
        out_specs=IN_VMEM,
        out_shape=jax.ShapeDtypeStruct((33, 32, HD), F32),
        scratch_shapes=buffers(keys) + [pltpu.SemaphoreType.DMA((32,))],
        compiler_params=pltpu.CompilerParams(vmem_limit_bytes=VMEM),
        cost_estimate=SMALL,
        name="attend_near",
    )(lengths, order, q, new, cache, after)


def merge_rows(order, far, near, new, done):
    def kernel(order_ref, far_ref, near_ref, new_ref, done_ref, out_ref, pair_ref):
        parts = far_ref[32].astype(F32)
        theirs = parts + pltpu.roll(parts, 127, 1) + pltpu.roll(parts, 126, 1)
        ours = near_ref[32]
        top = jnp.maximum(theirs, ours)
        wt, wo = jnp.exp2(theirs - top), jnp.exp2(ours - top)
        share = wt / (wt + wo)
        for p in range(32):
            at = order_ref[p]
            mine = near_ref[p]
            o = mine + (far_ref[p].astype(F32) - mine) * share[:, 4 * p : 4 * p + 1]
            for h in range(HEADS):
                out_ref[at, :, h * HD : h * HD + HD] = o[4 * h : 4 * h + 4].astype(BF16)
            pair_ref[at] = new_ref[p]
            at = order_ref[32 + p]
            out_ref[at] = done_ref[p, :, :QW]
            pair_ref[at] = done_ref[p, :, QW:]

    return pl.pallas_call(
        kernel,
        in_specs=[IN_SMEM] + [IN_VMEM] * 4,
        out_specs=[IN_VMEM] * 2,
        out_shape=[jax.ShapeDtypeStruct((64, 4, QW), BF16), jax.ShapeDtypeStruct((64, 4, PW), BF16)],
        compiler_params=pltpu.CompilerParams(vmem_limit_bytes=VMEM),
        cost_estimate=SMALL,
        name="merge_rows",
    )(order, far, near, new, done)


def on_device(
    tokens,
    query_weight,
    query_bias,
    pair_weight,
    pair_bias,
    cache_pairs,
    prefix_pairs,
    owner_slot,
    prefix_blocks,
    positions,
):
    prompts, _, new, width = tokens.shape
    me = lax.axis_index("roll")
    my_y, my_z, my_c = me // 8, me // 2 % 4, me % 2
    tp = lax.axis_index("tp")
    tp_y, tp_x = tp // 4, tp % 4
    pos = positions.reshape(prompts)

    own = prefix_pairs.reshape(-1, 512, 2 * HD)
    below, above, own_c = over_roll(own, 0, 1, 0), over_roll(own, 0, 3, 0), over_roll(own, 0, 0, 1)

    x_o, x_m = sort_rows(
        jnp.stack([my_y, my_z, my_c]).astype(jnp.int32),
        jnp.broadcast_to(owner_slot[:, None], (prompts, new)).reshape(1, prompts * new),
        tokens.reshape(prompts * new, width),
    )

    def heads(*pairs):
        return jnp.stack([(tp_y + dy) % 2 * 4 + (tp_x + dx) % 4 for dy, dx in pairs]).astype(jnp.int32)

    weights = (query_weight, pair_weight)
    up_o, down_o, up_m, down_m = project(heads((0, 2), (1, 2)), [x_o, x_m], *weights, [[0], [1]])
    right_o, left_o, right_m, left_m = project(
        heads((0, 1), (1, 1), (0, 3), (1, 3)), [x_o, x_m], *weights, [[0, 1], [2, 3]], after=(own_c,)
    )
    right_o, left_o = add_far(right_o, left_o, over_tp(up_o, 0, 1), over_tp(down_o, 0, 3), ())
    right_m, left_m = add_far(right_m, left_m, over_tp(up_m, 0, 1), over_tp(down_m, 0, 3), (right_o,))
    own_o, own_m = project(heads((0, 0), (1, 0)), [x_o, x_m], *weights, [[0, 1]], after=(right_o, left_o))

    def reduce(right, left, own_part):
        keep, send = sum_x(own_part, over_tp(right, 0, 1), over_tp(left, 0, 3))
        return keep, over_tp(send, 1, 0)

    full_o = reduce(right_o, left_o, own_o)
    full_m = reduce(right_m, left_m, own_m)

    far, both = turn_far(jnp.stack([my_c]).astype(jnp.int32), below, above, full_o[0])
    far = lax.ppermute(
        far,
        "roll",
        [
            ((y * 4 + z) * 2 + c, (y * 4 + (z + 1 + 2 * c) % 4) * 2 + c)
            for y in range(2)
            for z in range(4)
            for c in range(2)
        ],
    )

    index = jnp.arange(prompts, dtype=jnp.int32)
    half, quarter = jnp.arange(2, dtype=jnp.int32), jnp.arange(4, dtype=jnp.int32)
    y_of, c_of = (1 - half + my_y) % 2, (half + my_c) % 2
    z_of = (jnp.array([0, 3, 1, 2], jnp.int32) + my_z) % 4
    slot = (
        ((y_of[:, None, None, None] * 4 + z_of[None, None, :, None]) * 2 + c_of[None, :, None, None]) * 4
        + quarter[None, None, None, :]
    ).reshape(prompts)
    hit = owner_slot[None, :] == slot[:, None]
    order = jnp.sum(jnp.where(hit, index[None, :], 0), 1)
    limits = BLOCK * jnp.sum(jnp.where(hit, prefix_blocks[None, :], 0), 1)
    lengths = jnp.sum(jnp.where(hit, pos[None, :], 0), 1)
    my_limits = limits[32:]
    at = (limits[:, None] + lengths[:, None] + quarter[None, :]).reshape(prompts * new)
    frequency = jnp.exp(jnp.arange(HD // 2, dtype=F32) * (-2.0 * math.log(ROPE_BASE) / HD))
    angles = at.astype(F32)[:, None] * frequency[None, :]
    cosine, sine = jnp.cos(angles), jnp.sin(angles)
    tables = (
        jnp.concatenate([query_bias, pair_bias]).astype(F32)[None],
        jnp.concatenate([cosine, cosine], 1),
        jnp.concatenate([-sine, sine], 1),
    )
    cache = cache_pairs.reshape(prompts, 64, 2 * HD)

    q_o, new_o = make_queries(*full_o, *tables, right_m)
    far = hold(far, q_o)
    kvs = [own, both, far, own_c, over_roll(both, 0, 0, 1), over_roll(far, 0, 0, 1)]
    values = attend_prefix(my_limits, over_roll(q_o, 1, 0, 0), kvs)
    far = over_roll(values, 1, 0, 0)
    near = attend_near(lengths, order, q_o, new_o, cache, values)
    done = attend(my_limits, lengths, order, *full_m, *tables, cache, kvs)
    attended, new_pairs = merge_rows(order, far, near, new_o.reshape(32, new, PW), done)
    return (
        attended.reshape(prompts, 1, new, QW),
        new_pairs.reshape(prompts, 1, new, 1, PW),
    )


def solution(mesh):
    return jax.shard_map(
        on_device,
        mesh=mesh,
        in_specs=(
            P(None, "roll", None, "tp"),
            P("tp", None),
            P("tp"),
            P("tp", None),
            P("tp"),
            P(None, "roll", None, "tp", None),
            P("roll", None, "tp", None),
            P(),
            P(),
            P(None, "roll"),
        ),
        out_specs=(P(None, "roll", None, "tp"), P(None, "roll", None, "tp", None)),
        check_vma=False,
    )
```

```python
import math

import jax
import jax.numpy as jnp
from jax import lax
from jax.experimental import pallas as pl
from jax.experimental.pallas import tpu as pltpu
from jax.sharding import PartitionSpec as P

BLOCK = 128
HD = 128
HEADS = 8
QW = HEADS * HD
PW = 2 * HD
COLS = QW + PW
ROWS = 128
ROPE_BASE = 1000000.0
NEG = -1e30
LOG2_SCALE = HD ** -0.5 / math.log(2.0)
F32 = jnp.float32
BF16 = jnp.bfloat16
VMEM = 20 * 1024 * 1024
VMEM_PROJECT = 50 * 1024 * 1024


def tp_shift(dy, dx):
    return [(y * 4 + x, (y + dy) % 2 * 4 + (x + dx) % 4) for y in range(2) for x in range(4)]


def roll_shift(dy, dz, dc):
    return [
        ((y * 4 + z) * 2 + c, ((y + dy) % 2 * 4 + (z + dz) % 4) * 2 + (c + dc) % 2)
        for y in range(2)
        for z in range(4)
        for c in range(2)
    ]


def over_tp(a, dy, dx):
    return lax.ppermute(a, "tp", tp_shift(dy, dx))


def over_roll(a, dy, dz, dc):
    return lax.ppermute(a, "roll", roll_shift(dy, dz, dc))


def dot(a, b, dims=((1,), (0,))):
    return lax.dot_general(a, b, (dims, ((), ())), preferred_element_type=F32)


ANY = pl.BlockSpec(memory_space=pl.ANY)
IN_HBM = pl.BlockSpec(memory_space=pltpu.HBM)
IN_VMEM = pl.BlockSpec(memory_space=pltpu.VMEM)


def cost(us):
    return pl.CostEstimate(flops=10**6, bytes_accessed=int(us * 2_500_000), transcendentals=0)


SMALL = cost(0.04)
IN_SMEM = pl.BlockSpec(memory_space=pltpu.SMEM)


def project(heads, xs, wq, wp, groups, after=()):
    count = sum(len(g) for g in groups)
    depth = wq.shape[0]

    def kernel(heads_ref, *refs):
        x_refs, (wq_ref, wp_ref) = refs[: len(xs)], refs[len(xs) : len(xs) + 2]
        rest = refs[len(xs) + 2 + len(after) :]
        outs, (q_buf, p_buf, q_sem, p_sem) = rest[:-4], rest[-4:]
        copies = []
        for d in range(count):
            k = heads_ref[d]
            copies.append(
                (
                    pltpu.make_async_copy(
                        wq_ref.at[:, pl.ds(pl.multiple_of(k * QW, QW), QW)], q_buf.at[d], q_sem.at[d]
                    ),
                    pltpu.make_async_copy(
                        wp_ref.at[:, pl.ds(pl.multiple_of(k * PW, PW), PW)], p_buf.at[d], p_sem.at[d]
                    ),
                )
            )
        for pair in copies:
            for c in pair:
                c.start()
        x = jnp.concatenate([r[...] for r in x_refs], 0)
        d = 0
        for g, group in enumerate(groups):
            for i in range(len(group)):
                for c in copies[d]:
                    c.wait()
                for buf, low, high in ((q_buf, 0, QW), (p_buf, QW, COLS)):
                    y = dot(x, buf[d]).astype(BF16)
                    for b in range(len(xs)):
                        outs[b * len(groups) + g][i, :, low:high] = y[b * ROWS : (b + 1) * ROWS]
                d += 1

    return pl.pallas_call(
        kernel,
        in_specs=[IN_SMEM] + [IN_VMEM] * len(xs) + [IN_HBM, IN_HBM] + [ANY] * len(after),
        out_specs=[IN_VMEM] * (len(xs) * len(groups)),
        out_shape=[jax.ShapeDtypeStruct((len(g), ROWS, COLS), BF16) for _ in xs for g in groups],
        scratch_shapes=[
            pltpu.VMEM((count, depth, QW), BF16),
            pltpu.VMEM((count, depth, PW), BF16),
            pltpu.SemaphoreType.DMA((count,)),
            pltpu.SemaphoreType.DMA((count,)),
        ],
        compiler_params=pltpu.CompilerParams(vmem_limit_bytes=VMEM_PROJECT),
        cost_estimate=SMALL,
        name="project",
    )(heads, *xs, wq, wp, *after)


def sort_rows(place, owner, tokens):
    rows, width = tokens.shape

    def kernel(place_ref, owner_ref, x_ref, *outs):
        x = x_ref[...]
        for b, out in enumerate(outs):
            row = lax.broadcasted_iota(jnp.int32, (ROWS, rows), 0)
            col = lax.broadcasted_iota(jnp.int32, (ROWS, rows), 1)
            i = row // 4
            y, c, step, j = (1 - b + place_ref[0]) % 2, i // 16, i // 4 % 4, i % 4
            c = jnp.where(c == 0, place_ref[2], 1 - place_ref[2])
            z = (jnp.where(step == 1, 3, jnp.where(step == 0, 0, step - 1)) + place_ref[1]) % 4
            slot = ((y * 4 + z) * 2 + c) * 4 + j
            hit = (owner_ref[...] == slot) & (col % 4 == row % 4)
            out[...] = dot(jnp.where(hit, 1.0, 0.0).astype(BF16), x).astype(BF16)

    return pl.pallas_call(
        kernel,
        in_specs=[IN_SMEM, IN_VMEM, IN_VMEM],
        out_specs=[IN_VMEM] * 2,
        out_shape=[jax.ShapeDtypeStruct((ROWS, width), BF16)] * 2,
        compiler_params=pltpu.CompilerParams(vmem_limit_bytes=VMEM),
        cost_estimate=SMALL,
        name="sort_rows",
    )(place, owner, tokens)


def add_far(right, left, up, down, after):
    def kernel(r, l, u, d, *refs):
        r_out, l_out = refs[len(after) :]
        r_out[...] = (r[...].astype(F32) + u[...].astype(F32)).astype(BF16)
        l_out[...] = (l[...].astype(F32) + d[...].astype(F32)).astype(BF16)

    block = [pl.BlockSpec((1, ROWS, COLS), lambda i, h=h: (h, 0, 0)) for h in (0, 1)]
    return pl.pallas_call(
        kernel,
        grid=(1,),
        in_specs=block + [block[0]] * 2 + [ANY] * len(after),
        out_specs=block,
        out_shape=[jax.ShapeDtypeStruct(right.shape, BF16)] * 2,
        input_output_aliases={0: 0, 1: 1},
        compiler_params=pltpu.CompilerParams(vmem_limit_bytes=VMEM),
        cost_estimate=SMALL,
        name="add_far",
    )(right, left, up, down, *after)


def hold(arrays, after):
    def kernel(*refs):
        pass

    count = len(arrays)
    return pl.pallas_call(
        kernel,
        in_specs=[ANY] * (count + 1),
        out_specs=[ANY] * count,
        out_shape=[jax.ShapeDtypeStruct(a.shape, a.dtype) for a in arrays],
        input_output_aliases={i: i for i in range(count)},
        cost_estimate=SMALL,
        name="hold",
    )(*arrays, after)


def prefix_copies(refs, buf, sem):
    return [
        pltpu.make_async_copy(refs[g], buf.at[pl.ds(4 * g, 4), pl.ds(0, 512)], sem.at[g]) for g in range(8)
    ]


def sum_x(own, from_left, from_right, after):
    def kernel(a, b, c, after_ref, keep, send):
        for i, out in enumerate((keep, send)):
            out[...] = (a[i].astype(F32) + b[i].astype(F32) + c[i].astype(F32)).astype(out.dtype)

    return pl.pallas_call(
        kernel,
        in_specs=[IN_VMEM] * 3 + [ANY],
        out_specs=[IN_VMEM] * 2,
        out_shape=[jax.ShapeDtypeStruct((ROWS, COLS), F32), jax.ShapeDtypeStruct((ROWS, COLS), BF16)],
        compiler_params=pltpu.CompilerParams(vmem_limit_bytes=VMEM),
        cost_estimate=SMALL,
        name="sum_x",
    )(own, from_left, from_right, after)


def rotated(keep_ref, more_ref, bias_ref, cos_ref, sin_ref, first, q_buf):
    cos, sin = cos_ref[first : first + ROWS, :], sin_ref[first : first + ROWS, :]

    def turn(v):
        return v * cos + pltpu.roll(v, HD // 2, 1) * sin

    for h in range(HEADS):
        low, high = h * HD, h * HD + HD
        v = turn(keep_ref[:, low:high] + more_ref[:, low:high].astype(F32) + bias_ref[:, low:high])
        for p in range(32):
            q_buf[32 * p + 4 * h : 32 * p + 4 * h + 4, :] = v[4 * p : 4 * p + 4]
    u = keep_ref[:, QW:] + more_ref[:, QW:].astype(F32) + bias_ref[:, QW:]
    return jnp.concatenate([turn(u[:, :HD]), u[:, HD:]], 1)


def masked_scores(q, keys, valid):
    return jnp.where(valid, dot(q, keys, ((1,), (1,))) * LOG2_SCALE, NEG)


def weigh(s_buf, w_buf, top_buf, sum_buf):
    for g in range(8):
        rows = slice(128 * g, 128 * g + 128)
        s = s_buf[rows, :]
        top = jnp.max(s, -1, keepdims=True)
        w = jnp.exp2(s - top)
        w_buf[rows, :] = w.astype(BF16)
        top_buf[rows, :] = top
        sum_buf[rows, :] = jnp.sum(w, -1, keepdims=True)


def new_block(new_ref_rows):
    return jnp.concatenate([new_ref_rows, jnp.zeros((12, PW), F32)], 0).astype(BF16)


def buffers(keys):
    return [
        pltpu.VMEM((32, keys, PW), BF16),
        pltpu.VMEM((1024, keys), F32),
        pltpu.VMEM((1024, keys), BF16),
        pltpu.VMEM((1024, 1), F32),
        pltpu.VMEM((1024, 1), F32),
    ]


def pack_logs(top_buf, sum_buf):
    lane = lax.broadcasted_iota(jnp.int32, (32, 128), 1)
    packed = jnp.zeros((32, 128), F32)
    for p in range(32):
        rows = slice(32 * p, 32 * p + 32)
        packed = jnp.where(lane == 4 * p, top_buf[rows, :] + jnp.log2(sum_buf[rows, :]), packed)
    return packed


def attend(limits, lengths, order, keep, more, bias, cosine, sine, cache, kvs):
    keys = 512 + 64 + 16

    def kernel(limit_ref, length_ref, at_ref, keep_ref, more_ref, bias_ref, cos_ref, sin_ref, cache_ref, *refs):
        o_ref, buf, s_buf, w_buf, top_buf, sum_buf, qbuf, sem, csem = refs[8:]
        copies = prefix_copies(refs, buf, sem) + [
            pltpu.make_async_copy(cache_ref.at[at_ref[32 + p]], buf.at[p, pl.ds(512, 64)], csem.at[p])
            for p in range(32)
        ]
        for c in copies:
            c.start()
        new_all = rotated(keep_ref, more_ref, bias_ref, cos_ref, sin_ref, ROWS, qbuf)
        for p in range(32):
            o_ref[p, :, QW:] = new_all[4 * p : 4 * p + 4].astype(BF16)
            buf[p, 576:592, :] = new_block(new_all[4 * p : 4 * p + 4])
        row = lax.broadcasted_iota(jnp.int32, (32, keys), 0)
        col = lax.broadcasted_iota(jnp.int32, (32, keys), 1)
        fresh = (col >= 576) & (col - 576 <= row & 3)
        for c in copies:
            c.wait()
        for p in range(32):
            valid = (col < limit_ref[p]) | ((col >= 512) & (col < 512 + length_ref[32 + p])) | fresh
            rows = slice(32 * p, 32 * p + 32)
            s_buf[rows, :] = masked_scores(qbuf[rows, :].astype(BF16), buf[p, :, :HD], valid)
        weigh(s_buf, w_buf, top_buf, sum_buf)
        for p in range(32):
            rows = slice(32 * p, 32 * p + 32)
            o = dot(w_buf[rows, :], buf[p, :, HD:]) / sum_buf[rows, :]
            for h in range(HEADS):
                o_ref[p, :, h * HD : h * HD + HD] = o[4 * h : 4 * h + 4].astype(BF16)

    return pl.pallas_call(
        kernel,
        in_specs=[IN_SMEM] * 3 + [IN_VMEM] * 5 + [ANY] * 9,
        out_specs=IN_VMEM,
        out_shape=jax.ShapeDtypeStruct((32, 4, COLS), BF16),
        scratch_shapes=buffers(keys)
        + [pltpu.VMEM((1024, HD), F32), pltpu.SemaphoreType.DMA((8,)), pltpu.SemaphoreType.DMA((32,))],
        compiler_params=pltpu.CompilerParams(vmem_limit_bytes=VMEM),
        cost_estimate=SMALL,
        name="attend",
    )(limits, lengths, order, keep, more, bias, cosine, sine, cache, *kvs)


def make_queries(keep, more, bias, cosine, sine, after):
    def kernel(keep_ref, more_ref, bias_ref, cos_ref, sin_ref, after_ref, q_ref, new_ref, qbuf):
        new_ref[...] = rotated(keep_ref, more_ref, bias_ref, cos_ref, sin_ref, 0, qbuf).astype(BF16)
        q_ref[...] = qbuf[...].astype(BF16).reshape(32, 32, HD)

    return pl.pallas_call(
        kernel,
        in_specs=[IN_VMEM] * 5 + [ANY],
        out_specs=[IN_VMEM] * 2,
        out_shape=[jax.ShapeDtypeStruct((32, 32, HD), BF16), jax.ShapeDtypeStruct((ROWS, PW), BF16)],
        scratch_shapes=[pltpu.VMEM((1024, HD), F32)],
        compiler_params=pltpu.CompilerParams(vmem_limit_bytes=VMEM),
        cost_estimate=SMALL,
        name="make_queries",
    )(keep, more, bias, cosine, sine, after)


def attend_prefix(limits, q, kvs, after):
    keys = 512

    def kernel(limit_ref, q_ref, *refs):
        o_ref, buf, s_buf, w_buf, top_buf, sum_buf, sem = refs[9:]
        copies = prefix_copies(refs, buf, sem)
        for c in copies:
            c.start()
        col = lax.broadcasted_iota(jnp.int32, (32, keys), 1)
        for g in range(8):
            copies[g].wait()
            for p in range(4 * g, 4 * g + 4):
                s_buf[32 * p : 32 * p + 32, :] = masked_scores(q_ref[p], buf[p, :, :HD], col < limit_ref[p])
        weigh(s_buf, w_buf, top_buf, sum_buf)
        for p in range(32):
            rows = slice(32 * p, 32 * p + 32)
            o_ref[p] = (dot(w_buf[rows, :], buf[p, :, HD:]) / sum_buf[rows, :]).astype(BF16)
        rest = pack_logs(top_buf, sum_buf)
        lane = lax.broadcasted_iota(jnp.int32, (32, 128), 1)
        packed = jnp.zeros((32, 128), F32)
        for part in range(3):
            piece = rest.astype(BF16).astype(F32)
            packed = jnp.where(lane % 4 == part, pltpu.roll(piece, part, 1), packed)
            rest = rest - piece
        o_ref[32] = packed.astype(BF16)

    return pl.pallas_call(
        kernel,
        in_specs=[IN_SMEM, IN_VMEM] + [ANY] * 9,
        out_specs=IN_VMEM,
        out_shape=jax.ShapeDtypeStruct((33, 32, HD), BF16),
        scratch_shapes=buffers(keys) + [pltpu.SemaphoreType.DMA((8,))],
        compiler_params=pltpu.CompilerParams(vmem_limit_bytes=VMEM),
        cost_estimate=SMALL,
        name="attend_prefix",
    )(limits, q, *kvs, after)


def attend_near(lengths, order, q, new, cache, after):
    keys = 64 + 16

    def kernel(
        length_ref, at_ref, q_ref, new_ref, cache_ref, after_ref, o_ref, buf, s_buf, w_buf, top_buf, sum_buf, sem
    ):
        copies = [
            pltpu.make_async_copy(cache_ref.at[at_ref[p]], buf.at[p, pl.ds(0, 64)], sem.at[p])
            for p in range(32)
        ]
        for c in copies:
            c.start()
        for p in range(32):
            buf[p, 64:80, :] = new_block(new_ref[4 * p : 4 * p + 4].astype(F32))
        row = lax.broadcasted_iota(jnp.int32, (32, keys), 0)
        col = lax.broadcasted_iota(jnp.int32, (32, keys), 1)
        fresh = (col >= 64) & (col - 64 <= row & 3)
        for c in copies:
            c.wait()
        for p in range(32):
            valid = (col < length_ref[p]) | fresh
            s_buf[32 * p : 32 * p + 32, :] = masked_scores(q_ref[p], buf[p, :, :HD], valid)
        weigh(s_buf, w_buf, top_buf, sum_buf)
        for p in range(32):
            rows = slice(32 * p, 32 * p + 32)
            o_ref[p] = dot(w_buf[rows, :], buf[p, :, HD:]) / sum_buf[rows, :]
        o_ref[32] = pack_logs(top_buf, sum_buf)

    return pl.pallas_call(
        kernel,
        in_specs=[IN_SMEM] * 2 + [IN_VMEM] * 2 + [ANY] * 2,
        out_specs=IN_VMEM,
        out_shape=jax.ShapeDtypeStruct((33, 32, HD), F32),
        scratch_shapes=buffers(keys) + [pltpu.SemaphoreType.DMA((32,))],
        compiler_params=pltpu.CompilerParams(vmem_limit_bytes=VMEM),
        cost_estimate=SMALL,
        name="attend_near",
    )(lengths, order, q, new, cache, after)


def merge_rows(order, far, near, new, done):
    def kernel(order_ref, far_ref, near_ref, new_ref, done_ref, out_ref, pair_ref):
        parts = far_ref[32].astype(F32)
        theirs = parts + pltpu.roll(parts, 127, 1) + pltpu.roll(parts, 126, 1)
        ours = near_ref[32]
        top = jnp.maximum(theirs, ours)
        wt, wo = jnp.exp2(theirs - top), jnp.exp2(ours - top)
        share = wt / (wt + wo)
        for p in range(32):
            at = order_ref[p]
            mine = near_ref[p]
            o = mine + (far_ref[p].astype(F32) - mine) * share[:, 4 * p : 4 * p + 1]
            for h in range(HEADS):
                out_ref[at, :, h * HD : h * HD + HD] = o[4 * h : 4 * h + 4].astype(BF16)
            pair_ref[at] = new_ref[p]
            at = order_ref[32 + p]
            out_ref[at] = done_ref[p, :, :QW]
            pair_ref[at] = done_ref[p, :, QW:]

    return pl.pallas_call(
        kernel,
        in_specs=[IN_SMEM] + [IN_VMEM] * 4,
        out_specs=[IN_VMEM] * 2,
        out_shape=[jax.ShapeDtypeStruct((64, 4, QW), BF16), jax.ShapeDtypeStruct((64, 4, PW), BF16)],
        compiler_params=pltpu.CompilerParams(vmem_limit_bytes=VMEM),
        cost_estimate=SMALL,
        name="merge_rows",
    )(order, far, near, new, done)


def on_device(
    tokens,
    query_weight,
    query_bias,
    pair_weight,
    pair_bias,
    cache_pairs,
    prefix_pairs,
    owner_slot,
    prefix_blocks,
    positions,
):
    prompts, _, new, width = tokens.shape
    me = lax.axis_index("roll")
    my_y, my_z, my_c = me // 8, me // 2 % 4, me % 2
    tp = lax.axis_index("tp")
    tp_y, tp_x = tp // 4, tp % 4
    pos = positions.reshape(prompts)

    own = prefix_pairs.reshape(-1, 512, 2 * HD)
    below, above, own_c = over_roll(own, 0, 1, 0), over_roll(own, 0, 3, 0), over_roll(own, 0, 0, 1)
    far = over_roll(below, 0, 1, 0)

    x_o, x_m = sort_rows(
        jnp.stack([my_y, my_z, my_c]).astype(jnp.int32),
        jnp.broadcast_to(owner_slot[:, None], (prompts, new)).reshape(1, prompts * new),
        tokens.reshape(prompts * new, width),
    )

    def heads(*pairs):
        return jnp.stack([(tp_y + dy) % 2 * 4 + (tp_x + dx) % 4 for dy, dx in pairs]).astype(jnp.int32)

    weights = (query_weight, pair_weight)
    up_o, down_o, up_m, down_m = project(heads((0, 2), (1, 2)), [x_o, x_m], *weights, [[0], [1]])
    right_o, left_o, right_m, left_m = project(
        heads((0, 1), (1, 1), (0, 3), (1, 3)), [x_o, x_m], *weights, [[0, 1], [2, 3]], after=(own_c,)
    )
    right_o, left_o = add_far(right_o, left_o, over_tp(up_o, 0, 1), over_tp(down_o, 0, 3), ())
    right_m, left_m = add_far(right_m, left_m, over_tp(up_m, 0, 1), over_tp(down_m, 0, 3), (right_o,))
    own_o, own_m = project(heads((0, 0), (1, 0)), [x_o, x_m], *weights, [[0, 1]], after=(right_o, left_o))

    def reduce(right, left, own_part, after):
        keep, send = sum_x(own_part, over_tp(right, 0, 1), over_tp(left, 0, 3), after)
        return keep, over_tp(send, 1, 0)

    full_o = reduce(right_o, left_o, own_o, right_m)
    full_m = reduce(right_m, left_m, own_m, full_o[0])

    index = jnp.arange(prompts, dtype=jnp.int32)
    half, quarter = jnp.arange(2, dtype=jnp.int32), jnp.arange(4, dtype=jnp.int32)
    y_of, c_of = (1 - half + my_y) % 2, (half + my_c) % 2
    z_of = (jnp.array([0, 3, 1, 2], jnp.int32) + my_z) % 4
    slot = (
        ((y_of[:, None, None, None] * 4 + z_of[None, None, :, None]) * 2 + c_of[None, :, None, None]) * 4
        + quarter[None, None, None, :]
    ).reshape(prompts)
    hit = owner_slot[None, :] == slot[:, None]
    order = jnp.sum(jnp.where(hit, index[None, :], 0), 1)
    limits = BLOCK * jnp.sum(jnp.where(hit, prefix_blocks[None, :], 0), 1)
    lengths = jnp.sum(jnp.where(hit, pos[None, :], 0), 1)
    my_limits = limits[32:]
    at = (limits[:, None] + lengths[:, None] + quarter[None, :]).reshape(prompts * new)
    frequency = jnp.exp(jnp.arange(HD // 2, dtype=F32) * (-2.0 * math.log(ROPE_BASE) / HD))
    angles = at.astype(F32)[:, None] * frequency[None, :]
    cosine, sine = jnp.cos(angles), jnp.sin(angles)
    tables = (
        jnp.concatenate([query_bias, pair_bias]).astype(F32)[None],
        jnp.concatenate([cosine, cosine], 1),
        jnp.concatenate([-sine, sine], 1),
    )
    cache = cache_pairs.reshape(prompts, 64, 2 * HD)

    q_o, new_o = make_queries(*full_o, *tables, full_m[0])
    near = attend_near(lengths, order, q_o, new_o, cache, full_m[1])
    gathered = hold((below, above, far), q_o)
    kvs = [own, *gathered, own_c] + [over_roll(a, 0, 0, 1) for a in gathered]
    far = over_roll(attend_prefix(my_limits, over_roll(q_o, 1, 0, 0), kvs, near), 1, 0, 0)
    done = attend(my_limits, lengths, order, *full_m, *tables, cache, kvs)
    attended, new_pairs = merge_rows(order, far, near, new_o.reshape(32, new, PW), done)
    return (
        attended.reshape(prompts, 1, new, QW),
        new_pairs.reshape(prompts, 1, new, 1, PW),
    )


def solution(mesh):
    return jax.shard_map(
        on_device,
        mesh=mesh,
        in_specs=(
            P(None, "roll", None, "tp"),
            P("tp", None),
            P("tp"),
            P("tp", None),
            P("tp"),
            P(None, "roll", None, "tp", None),
            P("roll", None, "tp", None),
            P(),
            P(),
            P(None, "roll"),
        ),
        out_specs=(P(None, "roll", None, "tp"), P(None, "roll", None, "tp", None)),
        check_vma=False,
    )
```

```python
import math

import jax
import jax.numpy as jnp
from jax import lax
from jax.experimental import pallas as pl
from jax.experimental.pallas import tpu as pltpu
from jax.sharding import PartitionSpec as P

BLOCK = 128
HD = 128
HEADS = 8
QW = HEADS * HD
PW = 2 * HD
COLS = QW + PW
ROWS = 128
ROPE_BASE = 1000000.0
NEG = -1e30
LOG2_SCALE = HD ** -0.5 / math.log(2.0)
F32 = jnp.float32
BF16 = jnp.bfloat16
VMEM = 20 * 1024 * 1024
VMEM_PROJECT = 28 * 1024 * 1024


def tp_shift(dy, dx):
    return [(y * 4 + x, (y + dy) % 2 * 4 + (x + dx) % 4) for y in range(2) for x in range(4)]


def roll_shift(dy, dz, dc):
    return [
        ((y * 4 + z) * 2 + c, ((y + dy) % 2 * 4 + (z + dz) % 4) * 2 + (c + dc) % 2)
        for y in range(2)
        for z in range(4)
        for c in range(2)
    ]


def over_tp(a, dy, dx):
    return lax.ppermute(a, "tp", tp_shift(dy, dx))


def over_roll(a, dy, dz, dc):
    return lax.ppermute(a, "roll", roll_shift(dy, dz, dc))


def dot(a, b, dims=((1,), (0,))):
    return lax.dot_general(a, b, (dims, ((), ())), preferred_element_type=F32)


ANY = pl.BlockSpec(memory_space=pl.ANY)
IN_HBM = pl.BlockSpec(memory_space=pltpu.HBM)
IN_VMEM = pl.BlockSpec(memory_space=pltpu.VMEM)


def cost(us):
    return pl.CostEstimate(flops=10**6, bytes_accessed=int(us * 2_500_000), transcendentals=0)


SMALL = cost(0.04)
IN_SMEM = pl.BlockSpec(memory_space=pltpu.SMEM)


def in_hbm(*arrays):
    return [pltpu.with_memory_space_constraint(a, pltpu.HBM) for a in arrays]


def project(heads, xs, wq, wp, groups, after=()):
    count = sum(len(g) for g in groups)
    depth = wq.shape[0]

    def kernel(heads_ref, *refs):
        x_refs, (wq_ref, wp_ref) = refs[: len(xs)], refs[len(xs) : len(xs) + 2]
        rest = refs[len(xs) + 2 + len(after) :]
        outs, (q_buf, p_buf, q_sem, p_sem) = rest[:-4], rest[-4:]
        copies = []
        for d in range(count):
            k = heads_ref[d]
            copies.append(
                (
                    pltpu.make_async_copy(
                        wq_ref.at[:, pl.ds(pl.multiple_of(k * QW, QW), QW)], q_buf.at[d], q_sem.at[d]
                    ),
                    pltpu.make_async_copy(
                        wp_ref.at[:, pl.ds(pl.multiple_of(k * PW, PW), PW)], p_buf.at[d], p_sem.at[d]
                    ),
                )
            )
        for pair in copies:
            for c in pair:
                c.start()
        x = jnp.concatenate([r[...] for r in x_refs], 0)
        d = 0
        for g, group in enumerate(groups):
            for i in range(len(group)):
                for c in copies[d]:
                    c.wait()
                for buf, low, high in ((q_buf, 0, QW), (p_buf, QW, COLS)):
                    y = dot(x, buf[d]).astype(BF16)
                    for b in range(len(xs)):
                        outs[b * len(groups) + g][i, :, low:high] = y[b * ROWS : (b + 1) * ROWS]
                d += 1

    return pl.pallas_call(
        kernel,
        in_specs=[IN_SMEM] + [IN_VMEM] * len(xs) + [IN_HBM, IN_HBM] + [ANY] * len(after),
        out_specs=[IN_VMEM] * (len(xs) * len(groups)),
        out_shape=[jax.ShapeDtypeStruct((len(g), ROWS, COLS), BF16) for _ in xs for g in groups],
        scratch_shapes=[
            pltpu.VMEM((count, depth, QW), BF16),
            pltpu.VMEM((count, depth, PW), BF16),
            pltpu.SemaphoreType.DMA((count,)),
            pltpu.SemaphoreType.DMA((count,)),
        ],
        compiler_params=pltpu.CompilerParams(vmem_limit_bytes=VMEM_PROJECT),
        cost_estimate=SMALL,
        name="project",
    )(heads, *xs, *in_hbm(wq, wp), *after)


def sort_rows(place, owner, tokens):
    rows, width = tokens.shape

    def kernel(place_ref, owner_ref, x_ref, *outs):
        x = x_ref[...]
        for b, out in enumerate(outs):
            row = lax.broadcasted_iota(jnp.int32, (ROWS, rows), 0)
            col = lax.broadcasted_iota(jnp.int32, (ROWS, rows), 1)
            i = row // 4
            y, c, step, j = (1 - b + place_ref[0]) % 2, i // 16, i // 4 % 4, i % 4
            c = jnp.where(c == 0, place_ref[2], 1 - place_ref[2])
            z = (jnp.where(step == 1, 3, jnp.where(step == 0, 0, step - 1)) + place_ref[1]) % 4
            slot = ((y * 4 + z) * 2 + c) * 4 + j
            hit = (owner_ref[...] == slot) & (col % 4 == row % 4)
            out[...] = dot(jnp.where(hit, 1.0, 0.0).astype(BF16), x).astype(BF16)

    return pl.pallas_call(
        kernel,
        in_specs=[IN_SMEM, IN_VMEM, IN_VMEM],
        out_specs=[IN_VMEM] * 2,
        out_shape=[jax.ShapeDtypeStruct((ROWS, width), BF16)] * 2,
        compiler_params=pltpu.CompilerParams(vmem_limit_bytes=VMEM),
        cost_estimate=SMALL,
        name="sort_rows",
    )(place, owner, *in_hbm(tokens))


def add_far(right, left, up, down, after):
    def kernel(r, l, u, d, *refs):
        r_out, l_out = refs[len(after) :]
        r_out[...] = (r[...].astype(F32) + u[...].astype(F32)).astype(BF16)
        l_out[...] = (l[...].astype(F32) + d[...].astype(F32)).astype(BF16)

    block = [pl.BlockSpec((1, ROWS, COLS), lambda i, h=h: (h, 0, 0)) for h in (0, 1)]
    return pl.pallas_call(
        kernel,
        grid=(1,),
        in_specs=block + [block[0]] * 2 + [ANY] * len(after),
        out_specs=block,
        out_shape=[jax.ShapeDtypeStruct(right.shape, BF16)] * 2,
        input_output_aliases={0: 0, 1: 1},
        compiler_params=pltpu.CompilerParams(vmem_limit_bytes=VMEM),
        cost_estimate=SMALL,
        name="add_far",
    )(right, left, up, down, *after)


def hold(arrays, after):
    def kernel(*refs):
        pass

    count = len(arrays)
    return pl.pallas_call(
        kernel,
        in_specs=[ANY] * (count + 1),
        out_specs=[ANY] * count,
        out_shape=[pltpu.HBM(a.shape, a.dtype) for a in arrays],
        input_output_aliases={i: i for i in range(count)},
        compiler_params=pltpu.CompilerParams(vmem_limit_bytes=1024 * 1024),
        cost_estimate=SMALL,
        name="hold",
    )(*arrays, after)


def prefix_copies(refs, buf, sem):
    return [
        pltpu.make_async_copy(refs[g], buf.at[pl.ds(4 * g, 4), pl.ds(0, 512)], sem.at[g]) for g in range(8)
    ]


def sum_x(own, from_left, from_right, after):
    def kernel(a, b, c, after_ref, keep, send):
        for i, out in enumerate((keep, send)):
            out[...] = (a[i].astype(F32) + b[i].astype(F32) + c[i].astype(F32)).astype(out.dtype)

    return pl.pallas_call(
        kernel,
        in_specs=[IN_VMEM] * 3 + [ANY],
        out_specs=[IN_VMEM] * 2,
        out_shape=[jax.ShapeDtypeStruct((ROWS, COLS), F32), jax.ShapeDtypeStruct((ROWS, COLS), BF16)],
        compiler_params=pltpu.CompilerParams(vmem_limit_bytes=VMEM),
        cost_estimate=SMALL,
        name="sum_x",
    )(own, from_left, from_right, after)


def rotated(keep_ref, more_ref, bias_ref, cos_ref, sin_ref, first, q_buf):
    cos, sin = cos_ref[first : first + ROWS, :], sin_ref[first : first + ROWS, :]

    def turn(v):
        return v * cos + pltpu.roll(v, HD // 2, 1) * sin

    for h in range(HEADS):
        low, high = h * HD, h * HD + HD
        v = turn(keep_ref[:, low:high] + more_ref[:, low:high].astype(F32) + bias_ref[:, low:high])
        for p in range(32):
            q_buf[32 * p + 4 * h : 32 * p + 4 * h + 4, :] = v[4 * p : 4 * p + 4]
    u = keep_ref[:, QW:] + more_ref[:, QW:].astype(F32) + bias_ref[:, QW:]
    return jnp.concatenate([turn(u[:, :HD]), u[:, HD:]], 1)


def masked_scores(q, keys, valid):
    return jnp.where(valid, dot(q, keys, ((1,), (1,))) * LOG2_SCALE, NEG)


def weigh(s_buf, w_buf, top_buf, sum_buf):
    for g in range(8):
        rows = slice(128 * g, 128 * g + 128)
        s = s_buf[rows, :]
        top = jnp.max(s, -1, keepdims=True)
        w = jnp.exp2(s - top)
        w_buf[rows, :] = w.astype(BF16)
        top_buf[rows, :] = top
        sum_buf[rows, :] = jnp.sum(w, -1, keepdims=True)


def new_block(new_ref_rows):
    return jnp.concatenate([new_ref_rows, jnp.zeros((12, PW), F32)], 0).astype(BF16)


def buffers(keys):
    return [
        pltpu.VMEM((32, keys, PW), BF16),
        pltpu.VMEM((1024, keys), F32),
        pltpu.VMEM((1024, keys), BF16),
        pltpu.VMEM((1024, 1), F32),
        pltpu.VMEM((1024, 1), F32),
    ]


def pack_logs(top_buf, sum_buf):
    lane = lax.broadcasted_iota(jnp.int32, (32, 128), 1)
    packed = jnp.zeros((32, 128), F32)
    for p in range(32):
        rows = slice(32 * p, 32 * p + 32)
        packed = jnp.where(lane == 4 * p, top_buf[rows, :] + jnp.log2(sum_buf[rows, :]), packed)
    return packed


def attend(limits, lengths, order, keep, more, bias, cosine, sine, cache, kvs):
    keys = 512 + 64 + 16

    def kernel(limit_ref, length_ref, at_ref, keep_ref, more_ref, bias_ref, cos_ref, sin_ref, cache_ref, *refs):
        o_ref, buf, s_buf, w_buf, top_buf, sum_buf, qbuf, sem, csem = refs[8:]
        copies = prefix_copies(refs, buf, sem) + [
            pltpu.make_async_copy(cache_ref.at[at_ref[32 + p]], buf.at[p, pl.ds(512, 64)], csem.at[p])
            for p in range(32)
        ]
        for c in copies:
            c.start()
        new_all = rotated(keep_ref, more_ref, bias_ref, cos_ref, sin_ref, ROWS, qbuf)
        for p in range(32):
            o_ref[p, :, QW:] = new_all[4 * p : 4 * p + 4].astype(BF16)
            buf[p, 576:592, :] = new_block(new_all[4 * p : 4 * p + 4])
        row = lax.broadcasted_iota(jnp.int32, (32, keys), 0)
        col = lax.broadcasted_iota(jnp.int32, (32, keys), 1)
        fresh = (col >= 576) & (col - 576 <= row & 3)
        for c in copies:
            c.wait()
        for p in range(32):
            valid = (col < limit_ref[p]) | ((col >= 512) & (col < 512 + length_ref[32 + p])) | fresh
            rows = slice(32 * p, 32 * p + 32)
            s_buf[rows, :] = masked_scores(qbuf[rows, :].astype(BF16), buf[p, :, :HD], valid)
        weigh(s_buf, w_buf, top_buf, sum_buf)
        for p in range(32):
            rows = slice(32 * p, 32 * p + 32)
            o = dot(w_buf[rows, :], buf[p, :, HD:]) / sum_buf[rows, :]
            for h in range(HEADS):
                o_ref[p, :, h * HD : h * HD + HD] = o[4 * h : 4 * h + 4].astype(BF16)

    return pl.pallas_call(
        kernel,
        in_specs=[IN_SMEM] * 3 + [IN_VMEM] * 5 + [ANY] * 9,
        out_specs=IN_VMEM,
        out_shape=jax.ShapeDtypeStruct((32, 4, COLS), BF16),
        scratch_shapes=buffers(keys)
        + [pltpu.VMEM((1024, HD), F32), pltpu.SemaphoreType.DMA((8,)), pltpu.SemaphoreType.DMA((32,))],
        compiler_params=pltpu.CompilerParams(vmem_limit_bytes=VMEM),
        cost_estimate=SMALL,
        name="attend",
    )(limits, lengths, order, keep, more, bias, cosine, sine, *in_hbm(cache, *kvs))


def make_queries(keep, more, bias, cosine, sine, after):
    def kernel(keep_ref, more_ref, bias_ref, cos_ref, sin_ref, after_ref, q_ref, new_ref, qbuf):
        new_ref[...] = rotated(keep_ref, more_ref, bias_ref, cos_ref, sin_ref, 0, qbuf).astype(BF16)
        q_ref[...] = qbuf[...].astype(BF16).reshape(32, 32, HD)

    return pl.pallas_call(
        kernel,
        in_specs=[IN_VMEM] * 5 + [ANY],
        out_specs=[IN_VMEM] * 2,
        out_shape=[jax.ShapeDtypeStruct((32, 32, HD), BF16), jax.ShapeDtypeStruct((ROWS, PW), BF16)],
        scratch_shapes=[pltpu.VMEM((1024, HD), F32)],
        compiler_params=pltpu.CompilerParams(vmem_limit_bytes=VMEM),
        cost_estimate=SMALL,
        name="make_queries",
    )(keep, more, bias, cosine, sine, after)


def attend_prefix(limits, q, kvs, after):
    keys = 512

    def kernel(limit_ref, q_ref, *refs):
        o_ref, buf, s_buf, w_buf, top_buf, sum_buf, sem = refs[9:]
        copies = prefix_copies(refs, buf, sem)
        for c in copies:
            c.start()
        col = lax.broadcasted_iota(jnp.int32, (32, keys), 1)
        for g in range(8):
            copies[g].wait()
            for p in range(4 * g, 4 * g + 4):
                s_buf[32 * p : 32 * p + 32, :] = masked_scores(q_ref[p], buf[p, :, :HD], col < limit_ref[p])
        weigh(s_buf, w_buf, top_buf, sum_buf)
        for p in range(32):
            rows = slice(32 * p, 32 * p + 32)
            o_ref[p] = (dot(w_buf[rows, :], buf[p, :, HD:]) / sum_buf[rows, :]).astype(BF16)
        rest = pack_logs(top_buf, sum_buf)
        lane = lax.broadcasted_iota(jnp.int32, (32, 128), 1)
        packed = jnp.zeros((32, 128), F32)
        for part in range(3):
            piece = rest.astype(BF16).astype(F32)
            packed = jnp.where(lane % 4 == part, pltpu.roll(piece, part, 1), packed)
            rest = rest - piece
        o_ref[32] = packed.astype(BF16)

    return pl.pallas_call(
        kernel,
        in_specs=[IN_SMEM, IN_VMEM] + [ANY] * 9,
        out_specs=IN_VMEM,
        out_shape=jax.ShapeDtypeStruct((33, 32, HD), BF16),
        scratch_shapes=buffers(keys) + [pltpu.SemaphoreType.DMA((8,))],
        compiler_params=pltpu.CompilerParams(vmem_limit_bytes=VMEM),
        cost_estimate=SMALL,
        name="attend_prefix",
    )(limits, q, *in_hbm(*kvs, after))


def attend_near(lengths, order, q, new, cache, after):
    keys = 64 + 16

    def kernel(
        length_ref, at_ref, q_ref, new_ref, cache_ref, after_ref, o_ref, buf, s_buf, w_buf, top_buf, sum_buf, sem
    ):
        copies = [
            pltpu.make_async_copy(cache_ref.at[at_ref[p]], buf.at[p, pl.ds(0, 64)], sem.at[p])
            for p in range(32)
        ]
        for c in copies:
            c.start()
        for p in range(32):
            buf[p, 64:80, :] = new_block(new_ref[4 * p : 4 * p + 4].astype(F32))
        row = lax.broadcasted_iota(jnp.int32, (32, keys), 0)
        col = lax.broadcasted_iota(jnp.int32, (32, keys), 1)
        fresh = (col >= 64) & (col - 64 <= row & 3)
        for c in copies:
            c.wait()
        for p in range(32):
            valid = (col < length_ref[p]) | fresh
            s_buf[32 * p : 32 * p + 32, :] = masked_scores(q_ref[p], buf[p, :, :HD], valid)
        weigh(s_buf, w_buf, top_buf, sum_buf)
        for p in range(32):
            rows = slice(32 * p, 32 * p + 32)
            o_ref[p] = dot(w_buf[rows, :], buf[p, :, HD:]) / sum_buf[rows, :]
        o_ref[32] = pack_logs(top_buf, sum_buf)

    return pl.pallas_call(
        kernel,
        in_specs=[IN_SMEM] * 2 + [IN_VMEM] * 2 + [ANY] * 2,
        out_specs=IN_VMEM,
        out_shape=pltpu.HBM((33, 32, HD), F32),
        scratch_shapes=buffers(keys) + [pltpu.SemaphoreType.DMA((32,))],
        compiler_params=pltpu.CompilerParams(vmem_limit_bytes=VMEM),
        cost_estimate=SMALL,
        name="attend_near",
    )(lengths, order, q, new, *in_hbm(cache, after))


def merge_rows(order, far, near, new, done):
    def kernel(order_ref, far_ref, near_ref, new_ref, done_ref, out_ref, pair_ref):
        parts = far_ref[32].astype(F32)
        theirs = parts + pltpu.roll(parts, 127, 1) + pltpu.roll(parts, 126, 1)
        ours = near_ref[32]
        top = jnp.maximum(theirs, ours)
        wt, wo = jnp.exp2(theirs - top), jnp.exp2(ours - top)
        share = wt / (wt + wo)
        for p in range(32):
            at = order_ref[p]
            mine = near_ref[p]
            o = mine + (far_ref[p].astype(F32) - mine) * share[:, 4 * p : 4 * p + 1]
            for h in range(HEADS):
                out_ref[at, :, h * HD : h * HD + HD] = o[4 * h : 4 * h + 4].astype(BF16)
            pair_ref[at] = new_ref[p]
            at = order_ref[32 + p]
            out_ref[at] = done_ref[p, :, :QW]
            pair_ref[at] = done_ref[p, :, QW:]

    return pl.pallas_call(
        kernel,
        in_specs=[IN_SMEM] + [IN_VMEM] * 4,
        out_specs=[IN_VMEM] * 2,
        out_shape=[jax.ShapeDtypeStruct((64, 4, QW), BF16), jax.ShapeDtypeStruct((64, 4, PW), BF16)],
        compiler_params=pltpu.CompilerParams(vmem_limit_bytes=VMEM),
        cost_estimate=SMALL,
        name="merge_rows",
    )(order, far, *in_hbm(near), new, done)


def on_device(
    tokens,
    query_weight,
    query_bias,
    pair_weight,
    pair_bias,
    cache_pairs,
    prefix_pairs,
    owner_slot,
    prefix_blocks,
    positions,
):
    prompts, _, new, width = tokens.shape
    me = lax.axis_index("roll")
    my_y, my_z, my_c = me // 8, me // 2 % 4, me % 2
    tp = lax.axis_index("tp")
    tp_y, tp_x = tp // 4, tp % 4
    pos = positions.reshape(prompts)

    own = prefix_pairs.reshape(-1, 512, 2 * HD)
    below, above, own_c = over_roll(own, 0, 1, 0), over_roll(own, 0, 3, 0), over_roll(own, 0, 0, 1)
    far = over_roll(below, 0, 1, 0)

    x_o, x_m = sort_rows(
        jnp.stack([my_y, my_z, my_c]).astype(jnp.int32),
        jnp.broadcast_to(owner_slot[:, None], (prompts, new)).reshape(1, prompts * new),
        tokens.reshape(prompts * new, width),
    )

    def heads(*pairs):
        return jnp.stack([(tp_y + dy) % 2 * 4 + (tp_x + dx) % 4 for dy, dx in pairs]).astype(jnp.int32)

    weights = (query_weight, pair_weight)
    up_o, down_o, up_m, down_m = project(heads((0, 2), (1, 2)), [x_o, x_m], *weights, [[0], [1]])
    right_o, left_o, right_m, left_m = project(
        heads((0, 1), (1, 1), (0, 3), (1, 3)), [x_o, x_m], *weights, [[0, 1], [2, 3]], after=(own_c,)
    )
    right_o, left_o = add_far(right_o, left_o, over_tp(up_o, 0, 1), over_tp(down_o, 0, 3), ())
    right_m, left_m = add_far(right_m, left_m, over_tp(up_m, 0, 1), over_tp(down_m, 0, 3), (right_o,))
    own_o, own_m = project(heads((0, 0), (1, 0)), [x_o, x_m], *weights, [[0, 1]], after=(right_o, left_o))

    def reduce(right, left, own_part, after):
        keep, send = sum_x(own_part, over_tp(right, 0, 1), over_tp(left, 0, 3), after)
        return keep, over_tp(send, 1, 0)

    full_o = reduce(right_o, left_o, own_o, right_m)
    full_m = reduce(right_m, left_m, own_m, full_o[0])

    index = jnp.arange(prompts, dtype=jnp.int32)
    half, quarter = jnp.arange(2, dtype=jnp.int32), jnp.arange(4, dtype=jnp.int32)
    y_of, c_of = (1 - half + my_y) % 2, (half + my_c) % 2
    z_of = (jnp.array([0, 3, 1, 2], jnp.int32) + my_z) % 4
    slot = (
        ((y_of[:, None, None, None] * 4 + z_of[None, None, :, None]) * 2 + c_of[None, :, None, None]) * 4
        + quarter[None, None, None, :]
    ).reshape(prompts)
    hit = owner_slot[None, :] == slot[:, None]
    order = jnp.sum(jnp.where(hit, index[None, :], 0), 1)
    limits = BLOCK * jnp.sum(jnp.where(hit, prefix_blocks[None, :], 0), 1)
    lengths = jnp.sum(jnp.where(hit, pos[None, :], 0), 1)
    my_limits = limits[32:]
    at = (limits[:, None] + lengths[:, None] + quarter[None, :]).reshape(prompts * new)
    frequency = jnp.exp(jnp.arange(HD // 2, dtype=F32) * (-2.0 * math.log(ROPE_BASE) / HD))
    angles = at.astype(F32)[:, None] * frequency[None, :]
    cosine, sine = jnp.cos(angles), jnp.sin(angles)
    tables = (
        jnp.concatenate([query_bias, pair_bias]).astype(F32)[None],
        jnp.concatenate([cosine, cosine], 1),
        jnp.concatenate([-sine, sine], 1),
    )
    cache = cache_pairs.reshape(prompts, 64, 2 * HD)

    q_o, new_o = make_queries(*full_o, *tables, full_m[0])
    gathered = hold((below, above, far), q_o)
    kvs = [own, *gathered, own_c] + [over_roll(a, 0, 0, 1) for a in gathered]
    near = attend_near(lengths, order, q_o, new_o, cache, kvs[-1])
    far = over_roll(attend_prefix(my_limits, over_roll(q_o, 1, 0, 0), kvs, near), 1, 0, 0)
    done = attend(my_limits, lengths, order, *full_m, *tables, cache, kvs)
    attended, new_pairs = merge_rows(order, far, near, new_o.reshape(32, new, PW), done)
    return (
        attended.reshape(prompts, 1, new, QW),
        new_pairs.reshape(prompts, 1, new, 1, PW),
    )


def solution(mesh):
    return jax.shard_map(
        on_device,
        mesh=mesh,
        in_specs=(
            P(None, "roll", None, "tp"),
            P("tp", None),
            P("tp"),
            P("tp", None),
            P("tp"),
            P(None, "roll", None, "tp", None),
            P("roll", None, "tp", None),
            P(),
            P(),
            P(None, "roll"),
        ),
        out_specs=(P(None, "roll", None, "tp"), P(None, "roll", None, "tp", None)),
        check_vma=False,
    )
```

```python
import math

import jax
import jax.numpy as jnp
from jax import lax
from jax.experimental import pallas as pl
from jax.experimental.pallas import tpu as pltpu
from jax.sharding import PartitionSpec as P

BLOCK = 128
HD = 128
HEADS = 8
QW = HEADS * HD
PW = 2 * HD
COLS = QW + PW
ROWS = 128
ROPE_BASE = 1000000.0
NEG = -1e30
LOG2_SCALE = HD ** -0.5 / math.log(2.0)
F32 = jnp.float32
BF16 = jnp.bfloat16
VMEM = 18 * 1024 * 1024
VMEM_PROJECT = 18 * 1024 * 1024


def tp_shift(dy, dx):
    return [(y * 4 + x, (y + dy) % 2 * 4 + (x + dx) % 4) for y in range(2) for x in range(4)]


def roll_shift(dy, dz, dc):
    return [
        ((y * 4 + z) * 2 + c, ((y + dy) % 2 * 4 + (z + dz) % 4) * 2 + (c + dc) % 2)
        for y in range(2)
        for z in range(4)
        for c in range(2)
    ]


def over_tp(a, dy, dx):
    return lax.ppermute(a, "tp", tp_shift(dy, dx))


def over_roll(a, dy, dz, dc):
    return lax.ppermute(a, "roll", roll_shift(dy, dz, dc))


def dot(a, b, dims=((1,), (0,))):
    return lax.dot_general(a, b, (dims, ((), ())), preferred_element_type=F32)


ANY = pl.BlockSpec(memory_space=pl.ANY)
IN_HBM = pl.BlockSpec(memory_space=pltpu.HBM)
IN_VMEM = pl.BlockSpec(memory_space=pltpu.VMEM)


def cost(us):
    return pl.CostEstimate(flops=10**6, bytes_accessed=int(us * 2_500_000), transcendentals=0)


SMALL = cost(0.04)
IN_SMEM = pl.BlockSpec(memory_space=pltpu.SMEM)


def in_hbm(*arrays):
    return [pltpu.with_memory_space_constraint(a, pltpu.HBM) for a in arrays]


def project(heads, xs, wq, wp, groups, after=()):
    count = sum(len(g) for g in groups)
    depth = wq.shape[0]

    def kernel(heads_ref, *refs):
        x_refs, (wq_ref, wp_ref) = refs[: len(xs)], refs[len(xs) : len(xs) + 2]
        rest = refs[len(xs) + 2 + len(after) :]
        outs, (q_buf, p_buf, q_sem, p_sem) = rest[:-4], rest[-4:]
        copies = []
        for d in range(count):
            k = heads_ref[d]
            copies.append(
                (
                    pltpu.make_async_copy(
                        wq_ref.at[:, pl.ds(pl.multiple_of(k * QW, QW), QW)], q_buf.at[d], q_sem.at[d]
                    ),
                    pltpu.make_async_copy(
                        wp_ref.at[:, pl.ds(pl.multiple_of(k * PW, PW), PW)], p_buf.at[d], p_sem.at[d]
                    ),
                )
            )
        for pair in copies:
            for c in pair:
                c.start()
        x = jnp.concatenate([r[...] for r in x_refs], 0)
        d = 0
        for g, group in enumerate(groups):
            for i in range(len(group)):
                for c in copies[d]:
                    c.wait()
                for buf, low, high in ((q_buf, 0, QW), (p_buf, QW, COLS)):
                    y = dot(x, buf[d]).astype(BF16)
                    for b in range(len(xs)):
                        outs[b * len(groups) + g][i, :, low:high] = y[b * ROWS : (b + 1) * ROWS]
                d += 1

    return pl.pallas_call(
        kernel,
        in_specs=[IN_SMEM] + [IN_VMEM] * len(xs) + [IN_HBM, IN_HBM] + [ANY] * len(after),
        out_specs=[IN_VMEM] * (len(xs) * len(groups)),
        out_shape=[jax.ShapeDtypeStruct((len(g), ROWS, COLS), BF16) for _ in xs for g in groups],
        scratch_shapes=[
            pltpu.VMEM((count, depth, QW), BF16),
            pltpu.VMEM((count, depth, PW), BF16),
            pltpu.SemaphoreType.DMA((count,)),
            pltpu.SemaphoreType.DMA((count,)),
        ],
        compiler_params=pltpu.CompilerParams(vmem_limit_bytes=VMEM_PROJECT),
        cost_estimate=SMALL,
        name="project",
    )(heads, *xs, *in_hbm(wq, wp), *after)


def project_far(heads, place, owner, tokens, wq, wp):
    rows, depth = tokens.shape

    def kernel(heads_ref, place_ref, owner_ref, t_ref, wq_ref, wp_ref, *refs):
        xs, outs, (q_buf, p_buf, q_sem, p_sem) = refs[:2], refs[2:6], refs[6:]
        copies = []
        for d in range(2):
            k = heads_ref[d]
            copies.append(
                (
                    pltpu.make_async_copy(
                        wq_ref.at[:, pl.ds(pl.multiple_of(k * QW, QW), QW)], q_buf.at[d], q_sem.at[d]
                    ),
                    pltpu.make_async_copy(
                        wp_ref.at[:, pl.ds(pl.multiple_of(k * PW, PW), PW)], p_buf.at[d], p_sem.at[d]
                    ),
                )
            )
        for pair in copies:
            for c in pair:
                c.start()
        t = t_ref[...]
        for b, out in enumerate(xs):
            row = lax.broadcasted_iota(jnp.int32, (ROWS, rows), 0)
            col = lax.broadcasted_iota(jnp.int32, (ROWS, rows), 1)
            i = row // 4
            y, c, step, j = (1 - b + place_ref[0]) % 2, i // 16, i // 4 % 4, i % 4
            c = jnp.where(c == 0, place_ref[2], 1 - place_ref[2])
            z = (jnp.where(step == 1, 3, jnp.where(step == 0, 0, step - 1)) + place_ref[1]) % 4
            slot = ((y * 4 + z) * 2 + c) * 4 + j
            hit = (owner_ref[...] == slot) & (col % 4 == row % 4)
            out[...] = dot(jnp.where(hit, 1.0, 0.0).astype(BF16), t).astype(BF16)
        x = jnp.concatenate([r[...] for r in xs], 0)
        for d in range(2):
            for c in copies[d]:
                c.wait()
            for buf, low, high in ((q_buf, 0, QW), (p_buf, QW, COLS)):
                y = dot(x, buf[d]).astype(BF16)
                for b in range(2):
                    outs[2 * b + d][0, :, low:high] = y[b * ROWS : (b + 1) * ROWS]

    return pl.pallas_call(
        kernel,
        in_specs=[IN_SMEM, IN_SMEM, IN_VMEM, IN_VMEM, IN_HBM, IN_HBM],
        out_specs=[IN_VMEM] * 6,
        out_shape=[jax.ShapeDtypeStruct((ROWS, depth), BF16)] * 2
        + [jax.ShapeDtypeStruct((1, ROWS, COLS), BF16)] * 4,
        scratch_shapes=[
            pltpu.VMEM((2, depth, QW), BF16),
            pltpu.VMEM((2, depth, PW), BF16),
            pltpu.SemaphoreType.DMA((2,)),
            pltpu.SemaphoreType.DMA((2,)),
        ],
        compiler_params=pltpu.CompilerParams(vmem_limit_bytes=VMEM_PROJECT),
        cost_estimate=SMALL,
        name="project_far",
    )(heads, place, owner, *in_hbm(tokens, wq, wp))


def add_far(right, left, up, down, after):
    def kernel(r, l, u, d, *refs):
        r_out, l_out = refs[len(after) :]
        r_out[...] = (r[...].astype(F32) + u[...].astype(F32)).astype(BF16)
        l_out[...] = (l[...].astype(F32) + d[...].astype(F32)).astype(BF16)

    block = [pl.BlockSpec((1, ROWS, COLS), lambda i, h=h: (h, 0, 0)) for h in (0, 1)]
    return pl.pallas_call(
        kernel,
        grid=(1,),
        in_specs=block + [block[0]] * 2 + [ANY] * len(after),
        out_specs=block,
        out_shape=[jax.ShapeDtypeStruct(right.shape, BF16)] * 2,
        input_output_aliases={0: 0, 1: 1},
        compiler_params=pltpu.CompilerParams(vmem_limit_bytes=VMEM),
        cost_estimate=SMALL,
        name="add_far",
    )(right, left, up, down, *after)


def hold(arrays, after):
    def kernel(*refs):
        pass

    count = len(arrays)
    return pl.pallas_call(
        kernel,
        in_specs=[ANY] * (count + 1),
        out_specs=[ANY] * count,
        out_shape=[pltpu.HBM(a.shape, a.dtype) for a in arrays],
        input_output_aliases={i: i for i in range(count)},
        compiler_params=pltpu.CompilerParams(vmem_limit_bytes=1024 * 1024),
        cost_estimate=SMALL,
        name="hold",
    )(*arrays, after)


def prefix_copies(refs, buf, sem):
    return [
        pltpu.make_async_copy(refs[g], buf.at[pl.ds(4 * g, 4), pl.ds(0, 512)], sem.at[g]) for g in range(8)
    ]


def sum_x(own, from_left, from_right, after):
    def kernel(a, b, c, after_ref, keep, send):
        for i, out in enumerate((keep, send)):
            out[...] = (a[i].astype(F32) + b[i].astype(F32) + c[i].astype(F32)).astype(out.dtype)

    return pl.pallas_call(
        kernel,
        in_specs=[IN_VMEM] * 3 + [ANY],
        out_specs=[IN_VMEM] * 2,
        out_shape=[jax.ShapeDtypeStruct((ROWS, COLS), F32), jax.ShapeDtypeStruct((ROWS, COLS), BF16)],
        compiler_params=pltpu.CompilerParams(vmem_limit_bytes=VMEM),
        cost_estimate=SMALL,
        name="sum_x",
    )(own, from_left, from_right, after)


def rotated(keep_ref, more_ref, bias_ref, cos_ref, sin_ref, first, q_buf):
    cos, sin = cos_ref[first : first + ROWS, :], sin_ref[first : first + ROWS, :]

    def turn(v):
        return v * cos + pltpu.roll(v, HD // 2, 1) * sin

    for h in range(HEADS):
        low, high = h * HD, h * HD + HD
        v = turn(keep_ref[:, low:high] + more_ref[:, low:high].astype(F32) + bias_ref[:, low:high])
        for p in range(32):
            q_buf[32 * p + 4 * h : 32 * p + 4 * h + 4, :] = v[4 * p : 4 * p + 4]
    u = keep_ref[:, QW:] + more_ref[:, QW:].astype(F32) + bias_ref[:, QW:]
    return jnp.concatenate([turn(u[:, :HD]), u[:, HD:]], 1)


def masked_scores(q, keys, valid):
    return jnp.where(valid, dot(q, keys, ((1,), (1,))) * LOG2_SCALE, NEG)


def weigh(s_buf, w_buf, top_buf, sum_buf):
    for g in range(8):
        rows = slice(128 * g, 128 * g + 128)
        s = s_buf[rows, :]
        top = jnp.max(s, -1, keepdims=True)
        w = jnp.exp2(s - top)
        w_buf[rows, :] = w.astype(BF16)
        top_buf[rows, :] = top
        sum_buf[rows, :] = jnp.sum(w, -1, keepdims=True)


def new_block(new_ref_rows):
    return jnp.concatenate([new_ref_rows, jnp.zeros((12, PW), F32)], 0).astype(BF16)


def buffers(keys):
    return [
        pltpu.VMEM((32, keys, PW), BF16),
        pltpu.VMEM((1024, keys), F32),
        pltpu.VMEM((1024, keys), BF16),
        pltpu.VMEM((1024, 1), F32),
        pltpu.VMEM((1024, 1), F32),
    ]


def pack_logs(top_buf, sum_buf):
    lane = lax.broadcasted_iota(jnp.int32, (32, 128), 1)
    packed = jnp.zeros((32, 128), F32)
    for p in range(32):
        rows = slice(32 * p, 32 * p + 32)
        packed = jnp.where(lane == 4 * p, top_buf[rows, :] + jnp.log2(sum_buf[rows, :]), packed)
    return packed


def attend(limits, lengths, order, keep, more, bias, cosine, sine, cache, kvs):
    keys = 512 + 64 + 16

    def kernel(limit_ref, length_ref, at_ref, keep_ref, more_ref, bias_ref, cos_ref, sin_ref, cache_ref, *refs):
        o_ref, buf, s_buf, w_buf, top_buf, sum_buf, qbuf, sem, csem = refs[8:]
        copies = prefix_copies(refs, buf, sem) + [
            pltpu.make_async_copy(cache_ref.at[at_ref[32 + p]], buf.at[p, pl.ds(512, 64)], csem.at[p])
            for p in range(32)
        ]
        for c in copies:
            c.start()
        new_all = rotated(keep_ref, more_ref, bias_ref, cos_ref, sin_ref, ROWS, qbuf)
        for p in range(32):
            o_ref[p, :, QW:] = new_all[4 * p : 4 * p + 4].astype(BF16)
            buf[p, 576:592, :] = new_block(new_all[4 * p : 4 * p + 4])
        row = lax.broadcasted_iota(jnp.int32, (32, keys), 0)
        col = lax.broadcasted_iota(jnp.int32, (32, keys), 1)
        fresh = (col >= 576) & (col - 576 <= row & 3)
        for c in copies:
            c.wait()
        for p in range(32):
            valid = (col < limit_ref[p]) | ((col >= 512) & (col < 512 + length_ref[32 + p])) | fresh
            rows = slice(32 * p, 32 * p + 32)
            s_buf[rows, :] = masked_scores(qbuf[rows, :].astype(BF16), buf[p, :, :HD], valid)
        weigh(s_buf, w_buf, top_buf, sum_buf)
        for p in range(32):
            rows = slice(32 * p, 32 * p + 32)
            o = dot(w_buf[rows, :], buf[p, :, HD:]) / sum_buf[rows, :]
            for h in range(HEADS):
                o_ref[p, :, h * HD : h * HD + HD] = o[4 * h : 4 * h + 4].astype(BF16)

    return pl.pallas_call(
        kernel,
        in_specs=[IN_SMEM] * 3 + [IN_VMEM] * 5 + [ANY] * 9,
        out_specs=IN_VMEM,
        out_shape=jax.ShapeDtypeStruct((32, 4, COLS), BF16),
        scratch_shapes=buffers(keys)
        + [pltpu.VMEM((1024, HD), F32), pltpu.SemaphoreType.DMA((8,)), pltpu.SemaphoreType.DMA((32,))],
        compiler_params=pltpu.CompilerParams(vmem_limit_bytes=VMEM),
        cost_estimate=SMALL,
        name="attend",
    )(limits, lengths, order, keep, more, bias, cosine, sine, *in_hbm(cache, *kvs))


def make_queries(keep, more, bias, cosine, sine, after):
    def kernel(keep_ref, more_ref, bias_ref, cos_ref, sin_ref, after_ref, q_ref, new_ref, qbuf):
        new_ref[...] = rotated(keep_ref, more_ref, bias_ref, cos_ref, sin_ref, 0, qbuf).astype(BF16)
        q_ref[...] = qbuf[...].astype(BF16).reshape(32, 32, HD)

    return pl.pallas_call(
        kernel,
        in_specs=[IN_VMEM] * 5 + [ANY],
        out_specs=[IN_VMEM] * 2,
        out_shape=[jax.ShapeDtypeStruct((32, 32, HD), BF16), jax.ShapeDtypeStruct((ROWS, PW), BF16)],
        scratch_shapes=[pltpu.VMEM((1024, HD), F32)],
        compiler_params=pltpu.CompilerParams(vmem_limit_bytes=VMEM),
        cost_estimate=SMALL,
        name="make_queries",
    )(keep, more, bias, cosine, sine, after)


def attend_prefix(limits, q, kvs, after):
    keys = 512

    def kernel(limit_ref, q_ref, *refs):
        o_ref, buf, s_buf, w_buf, top_buf, sum_buf, sem = refs[9:]
        copies = prefix_copies(refs, buf, sem)
        for c in copies:
            c.start()
        col = lax.broadcasted_iota(jnp.int32, (32, keys), 1)
        for g in range(8):
            copies[g].wait()
            for p in range(4 * g, 4 * g + 4):
                s_buf[32 * p : 32 * p + 32, :] = masked_scores(q_ref[p], buf[p, :, :HD], col < limit_ref[p])
        weigh(s_buf, w_buf, top_buf, sum_buf)
        for p in range(32):
            rows = slice(32 * p, 32 * p + 32)
            o_ref[p] = (dot(w_buf[rows, :], buf[p, :, HD:]) / sum_buf[rows, :]).astype(BF16)
        rest = pack_logs(top_buf, sum_buf)
        lane = lax.broadcasted_iota(jnp.int32, (32, 128), 1)
        packed = jnp.zeros((32, 128), F32)
        for part in range(3):
            piece = rest.astype(BF16).astype(F32)
            packed = jnp.where(lane % 4 == part, pltpu.roll(piece, part, 1), packed)
            rest = rest - piece
        o_ref[32] = packed.astype(BF16)

    return pl.pallas_call(
        kernel,
        in_specs=[IN_SMEM, IN_VMEM] + [ANY] * 9,
        out_specs=IN_VMEM,
        out_shape=jax.ShapeDtypeStruct((33, 32, HD), BF16),
        scratch_shapes=buffers(keys) + [pltpu.SemaphoreType.DMA((8,))],
        compiler_params=pltpu.CompilerParams(vmem_limit_bytes=VMEM),
        cost_estimate=SMALL,
        name="attend_prefix",
    )(limits, q, *in_hbm(*kvs, after))


def attend_near(lengths, order, q, new, cache, after):
    keys = 64 + 16

    def kernel(
        length_ref, at_ref, q_ref, new_ref, cache_ref, after_ref, o_ref, buf, s_buf, w_buf, top_buf, sum_buf, sem
    ):
        copies = [
            pltpu.make_async_copy(cache_ref.at[at_ref[p]], buf.at[p, pl.ds(0, 64)], sem.at[p])
            for p in range(32)
        ]
        for c in copies:
            c.start()
        for p in range(32):
            buf[p, 64:80, :] = new_block(new_ref[4 * p : 4 * p + 4].astype(F32))
        row = lax.broadcasted_iota(jnp.int32, (32, keys), 0)
        col = lax.broadcasted_iota(jnp.int32, (32, keys), 1)
        fresh = (col >= 64) & (col - 64 <= row & 3)
        for c in copies:
            c.wait()
        for p in range(32):
            valid = (col < length_ref[p]) | fresh
            s_buf[32 * p : 32 * p + 32, :] = masked_scores(q_ref[p], buf[p, :, :HD], valid)
        weigh(s_buf, w_buf, top_buf, sum_buf)
        for p in range(32):
            rows = slice(32 * p, 32 * p + 32)
            o_ref[p] = dot(w_buf[rows, :], buf[p, :, HD:]) / sum_buf[rows, :]
        o_ref[32] = pack_logs(top_buf, sum_buf)

    return pl.pallas_call(
        kernel,
        in_specs=[IN_SMEM] * 2 + [IN_VMEM] * 2 + [ANY] * 2,
        out_specs=IN_VMEM,
        out_shape=pltpu.HBM((33, 32, HD), F32),
        scratch_shapes=buffers(keys) + [pltpu.SemaphoreType.DMA((32,))],
        compiler_params=pltpu.CompilerParams(vmem_limit_bytes=VMEM),
        cost_estimate=SMALL,
        name="attend_near",
    )(lengths, order, q, new, *in_hbm(cache, after))


def merge_rows(order, far, near, new, done):
    def kernel(order_ref, far_ref, near_ref, new_ref, done_ref, out_ref, pair_ref):
        parts = far_ref[32].astype(F32)
        theirs = parts + pltpu.roll(parts, 127, 1) + pltpu.roll(parts, 126, 1)
        ours = near_ref[32]
        top = jnp.maximum(theirs, ours)
        wt, wo = jnp.exp2(theirs - top), jnp.exp2(ours - top)
        share = wt / (wt + wo)
        for p in range(32):
            at = order_ref[p]
            mine = near_ref[p]
            o = mine + (far_ref[p].astype(F32) - mine) * share[:, 4 * p : 4 * p + 1]
            for h in range(HEADS):
                out_ref[at, :, h * HD : h * HD + HD] = o[4 * h : 4 * h + 4].astype(BF16)
            pair_ref[at] = new_ref[p]
            at = order_ref[32 + p]
            out_ref[at] = done_ref[p, :, :QW]
            pair_ref[at] = done_ref[p, :, QW:]

    return pl.pallas_call(
        kernel,
        in_specs=[IN_SMEM] + [IN_VMEM] * 4,
        out_specs=[IN_VMEM] * 2,
        out_shape=[jax.ShapeDtypeStruct((64, 4, QW), BF16), jax.ShapeDtypeStruct((64, 4, PW), BF16)],
        compiler_params=pltpu.CompilerParams(vmem_limit_bytes=VMEM),
        cost_estimate=SMALL,
        name="merge_rows",
    )(order, far, *in_hbm(near), new, done)


def on_device(
    tokens,
    query_weight,
    query_bias,
    pair_weight,
    pair_bias,
    cache_pairs,
    prefix_pairs,
    owner_slot,
    prefix_blocks,
    positions,
):
    prompts, _, new, width = tokens.shape
    me = lax.axis_index("roll")
    my_y, my_z, my_c = me // 8, me // 2 % 4, me % 2
    tp = lax.axis_index("tp")
    tp_y, tp_x = tp // 4, tp % 4
    pos = positions.reshape(prompts)

    own = prefix_pairs.reshape(-1, 512, 2 * HD)
    below, above, own_c = over_roll(own, 0, 1, 0), over_roll(own, 0, 3, 0), over_roll(own, 0, 0, 1)
    far = over_roll(below, 0, 1, 0)

    def heads(*pairs):
        return jnp.stack([(tp_y + dy) % 2 * 4 + (tp_x + dx) % 4 for dy, dx in pairs]).astype(jnp.int32)

    weights = (query_weight, pair_weight)
    x_o, x_m, up_o, down_o, up_m, down_m = project_far(
        heads((0, 2), (1, 2)),
        jnp.stack([my_y, my_z, my_c]).astype(jnp.int32),
        jnp.broadcast_to(owner_slot[:, None], (prompts, new)).reshape(1, prompts * new),
        tokens.reshape(prompts * new, width),
        *weights,
    )
    right_o, left_o, right_m, left_m = project(
        heads((0, 1), (1, 1), (0, 3), (1, 3)), [x_o, x_m], *weights, [[0, 1], [2, 3]], after=(own_c,)
    )
    right_o, left_o = add_far(right_o, left_o, over_tp(up_o, 0, 1), over_tp(down_o, 0, 3), ())
    own_o, own_m = project(heads((0, 0), (1, 0)), [x_o, x_m], *weights, [[0, 1]], after=(right_o, left_o))
    right_m, left_m = add_far(right_m, left_m, over_tp(up_m, 0, 1), over_tp(down_m, 0, 3), (right_o, own_m))

    def reduce(right, left, own_part, after):
        keep, send = sum_x(own_part, over_tp(right, 0, 1), over_tp(left, 0, 3), after)
        return keep, over_tp(send, 1, 0)

    full_o = reduce(right_o, left_o, own_o, right_m)
    full_m = reduce(right_m, left_m, own_m, full_o[0])

    index = jnp.arange(prompts, dtype=jnp.int32)
    half, quarter = jnp.arange(2, dtype=jnp.int32), jnp.arange(4, dtype=jnp.int32)
    y_of, c_of = (1 - half + my_y) % 2, (half + my_c) % 2
    z_of = (jnp.array([0, 3, 1, 2], jnp.int32) + my_z) % 4
    slot = (
        ((y_of[:, None, None, None] * 4 + z_of[None, None, :, None]) * 2 + c_of[None, :, None, None]) * 4
        + quarter[None, None, None, :]
    ).reshape(prompts)
    hit = owner_slot[None, :] == slot[:, None]
    order = jnp.sum(jnp.where(hit, index[None, :], 0), 1)
    limits = BLOCK * jnp.sum(jnp.where(hit, prefix_blocks[None, :], 0), 1)
    lengths = jnp.sum(jnp.where(hit, pos[None, :], 0), 1)
    my_limits = limits[32:]
    at = (limits[:, None] + lengths[:, None] + quarter[None, :]).reshape(prompts * new)
    frequency = jnp.exp(jnp.arange(HD // 2, dtype=F32) * (-2.0 * math.log(ROPE_BASE) / HD))
    angles = at.astype(F32)[:, None] * frequency[None, :]
    cosine, sine = jnp.cos(angles), jnp.sin(angles)
    tables = (
        jnp.concatenate([query_bias, pair_bias]).astype(F32)[None],
        jnp.concatenate([cosine, cosine], 1),
        jnp.concatenate([-sine, sine], 1),
    )
    cache = cache_pairs.reshape(prompts, 64, 2 * HD)

    q_o, new_o = make_queries(*full_o, *tables, full_m[0])
    gathered = hold((below, above, far), q_o)
    kvs = [own, *gathered, own_c] + [over_roll(a, 0, 0, 1) for a in gathered]
    near = attend_near(lengths, order, q_o, new_o, cache, kvs[-1])
    far = over_roll(attend_prefix(my_limits, over_roll(q_o, 1, 0, 0), kvs, near), 1, 0, 0)
    done = attend(my_limits, lengths, order, *full_m, *tables, cache, kvs)
    attended, new_pairs = merge_rows(order, far, near, new_o.reshape(32, new, PW), done)
    return (
        attended.reshape(prompts, 1, new, QW),
        new_pairs.reshape(prompts, 1, new, 1, PW),
    )


def solution(mesh):
    return jax.shard_map(
        on_device,
        mesh=mesh,
        in_specs=(
            P(None, "roll", None, "tp"),
            P("tp", None),
            P("tp"),
            P("tp", None),
            P("tp"),
            P(None, "roll", None, "tp", None),
            P("roll", None, "tp", None),
            P(),
            P(),
            P(None, "roll"),
        ),
        out_specs=(P(None, "roll", None, "tp"), P(None, "roll", None, "tp", None)),
        check_vma=False,
    )
```

```python
import math

import jax
import jax.numpy as jnp
from jax import lax
from jax.experimental import pallas as pl
from jax.experimental.pallas import tpu as pltpu
from jax.sharding import PartitionSpec as P

BLOCK = 128
HD = 128
HEADS = 8
QW = HEADS * HD
PW = 2 * HD
COLS = QW + PW
ROWS = 128
ROPE_BASE = 1000000.0
NEG = -1e30
LOG2_SCALE = HD ** -0.5 / math.log(2.0)
F32 = jnp.float32
BF16 = jnp.bfloat16
VMEM = 18 * 1024 * 1024
VMEM_PROJECT = 18 * 1024 * 1024


def tp_shift(dy, dx):
    return [(y * 4 + x, (y + dy) % 2 * 4 + (x + dx) % 4) for y in range(2) for x in range(4)]


def roll_shift(dy, dz, dc):
    return [
        ((y * 4 + z) * 2 + c, ((y + dy) % 2 * 4 + (z + dz) % 4) * 2 + (c + dc) % 2)
        for y in range(2)
        for z in range(4)
        for c in range(2)
    ]


def over_tp(a, dy, dx):
    return lax.ppermute(a, "tp", tp_shift(dy, dx))


def over_roll(a, dy, dz, dc):
    return lax.ppermute(a, "roll", roll_shift(dy, dz, dc))


def dot(a, b, dims=((1,), (0,))):
    return lax.dot_general(a, b, (dims, ((), ())), preferred_element_type=F32)


ANY = pl.BlockSpec(memory_space=pl.ANY)
IN_HBM = pl.BlockSpec(memory_space=pltpu.HBM)
IN_VMEM = pl.BlockSpec(memory_space=pltpu.VMEM)


def cost(us):
    return pl.CostEstimate(flops=10**6, bytes_accessed=int(us * 2_500_000), transcendentals=0)


SMALL = cost(0.04)
IN_SMEM = pl.BlockSpec(memory_space=pltpu.SMEM)


def in_hbm(*arrays):
    return [pltpu.with_memory_space_constraint(a, pltpu.HBM) for a in arrays]


def project(heads, xs, wq, wp, groups, after=()):
    count = sum(len(g) for g in groups)
    depth = wq.shape[0]

    def kernel(heads_ref, *refs):
        x_refs, (wq_ref, wp_ref) = refs[: len(xs)], refs[len(xs) : len(xs) + 2]
        rest = refs[len(xs) + 2 + len(after) :]
        outs, (q_buf, p_buf, q_sem, p_sem) = rest[:-4], rest[-4:]
        copies = []
        for d in range(count):
            k = heads_ref[d]
            copies.append(
                (
                    pltpu.make_async_copy(
                        wq_ref.at[:, pl.ds(pl.multiple_of(k * QW, QW), QW)], q_buf.at[d], q_sem.at[d]
                    ),
                    pltpu.make_async_copy(
                        wp_ref.at[:, pl.ds(pl.multiple_of(k * PW, PW), PW)], p_buf.at[d], p_sem.at[d]
                    ),
                )
            )
        for pair in copies:
            for c in pair:
                c.start()
        x = jnp.concatenate([r[...] for r in x_refs], 0)
        d = 0
        for g, group in enumerate(groups):
            for i in range(len(group)):
                for c in copies[d]:
                    c.wait()
                for buf, low, high in ((q_buf, 0, QW), (p_buf, QW, COLS)):
                    y = dot(x, buf[d]).astype(BF16)
                    for b in range(len(xs)):
                        outs[b * len(groups) + g][i, :, low:high] = y[b * ROWS : (b + 1) * ROWS]
                d += 1

    return pl.pallas_call(
        kernel,
        in_specs=[IN_SMEM] + [IN_VMEM] * len(xs) + [IN_HBM, IN_HBM] + [ANY] * len(after),
        out_specs=[IN_VMEM] * (len(xs) * len(groups)),
        out_shape=[jax.ShapeDtypeStruct((len(g), ROWS, COLS), BF16) for _ in xs for g in groups],
        scratch_shapes=[
            pltpu.VMEM((count, depth, QW), BF16),
            pltpu.VMEM((count, depth, PW), BF16),
            pltpu.SemaphoreType.DMA((count,)),
            pltpu.SemaphoreType.DMA((count,)),
        ],
        compiler_params=pltpu.CompilerParams(vmem_limit_bytes=VMEM_PROJECT),
        cost_estimate=SMALL,
        name="project",
    )(heads, *xs, *in_hbm(wq, wp), *after)


def project_far(heads, place, owner, tokens, wq, wp):
    rows, depth = tokens.shape

    def kernel(heads_ref, place_ref, owner_ref, t_ref, wq_ref, wp_ref, *refs):
        xs, outs, (q_buf, p_buf, q_sem, p_sem) = refs[:2], refs[2:6], refs[6:]
        copies = []
        for d in range(2):
            k = heads_ref[d]
            copies.append(
                (
                    pltpu.make_async_copy(
                        wq_ref.at[:, pl.ds(pl.multiple_of(k * QW, QW), QW)], q_buf.at[d], q_sem.at[d]
                    ),
                    pltpu.make_async_copy(
                        wp_ref.at[:, pl.ds(pl.multiple_of(k * PW, PW), PW)], p_buf.at[d], p_sem.at[d]
                    ),
                )
            )
        for pair in copies:
            for c in pair:
                c.start()
        t = t_ref[...]
        for b, out in enumerate(xs):
            row = lax.broadcasted_iota(jnp.int32, (ROWS, rows), 0)
            col = lax.broadcasted_iota(jnp.int32, (ROWS, rows), 1)
            i = row // 4
            y, c, step, j = (1 - b + place_ref[0]) % 2, i // 16, i // 4 % 4, i % 4
            c = jnp.where(c == 0, place_ref[2], 1 - place_ref[2])
            z = (jnp.where(step == 1, 3, jnp.where(step == 0, 0, step - 1)) + place_ref[1]) % 4
            slot = ((y * 4 + z) * 2 + c) * 4 + j
            hit = (owner_ref[...] == slot) & (col % 4 == row % 4)
            out[...] = dot(jnp.where(hit, 1.0, 0.0).astype(BF16), t).astype(BF16)
        x = jnp.concatenate([r[...] for r in xs], 0)
        for d in range(2):
            for c in copies[d]:
                c.wait()
            for buf, low, high in ((q_buf, 0, QW), (p_buf, QW, COLS)):
                y = dot(x, buf[d]).astype(BF16)
                for b in range(2):
                    outs[2 * b + d][0, :, low:high] = y[b * ROWS : (b + 1) * ROWS]

    return pl.pallas_call(
        kernel,
        in_specs=[IN_SMEM, IN_SMEM, IN_VMEM, IN_VMEM, IN_HBM, IN_HBM],
        out_specs=[IN_VMEM] * 6,
        out_shape=[jax.ShapeDtypeStruct((ROWS, depth), BF16)] * 2
        + [jax.ShapeDtypeStruct((1, ROWS, COLS), BF16)] * 4,
        scratch_shapes=[
            pltpu.VMEM((2, depth, QW), BF16),
            pltpu.VMEM((2, depth, PW), BF16),
            pltpu.SemaphoreType.DMA((2,)),
            pltpu.SemaphoreType.DMA((2,)),
        ],
        compiler_params=pltpu.CompilerParams(vmem_limit_bytes=VMEM_PROJECT),
        cost_estimate=SMALL,
        name="project_far",
    )(heads, place, owner, *in_hbm(tokens, wq, wp))


def add_far(right, left, up, down, after):
    def kernel(r, l, u, d, *refs):
        r_out, l_out = refs[len(after) :]
        r_out[...] = (r[...].astype(F32) + u[...].astype(F32)).astype(BF16)
        l_out[...] = (l[...].astype(F32) + d[...].astype(F32)).astype(BF16)

    block = [pl.BlockSpec((1, ROWS, COLS), lambda i, h=h: (h, 0, 0)) for h in (0, 1)]
    return pl.pallas_call(
        kernel,
        grid=(1,),
        in_specs=block + [block[0]] * 2 + [ANY] * len(after),
        out_specs=block,
        out_shape=[jax.ShapeDtypeStruct(right.shape, BF16)] * 2,
        input_output_aliases={0: 0, 1: 1},
        compiler_params=pltpu.CompilerParams(vmem_limit_bytes=VMEM),
        cost_estimate=SMALL,
        name="add_far",
    )(right, left, up, down, *after)


def hold(arrays, after):
    def kernel(*refs):
        pass

    count = len(arrays)
    return pl.pallas_call(
        kernel,
        in_specs=[ANY] * (count + 1),
        out_specs=[ANY] * count,
        out_shape=[pltpu.HBM(a.shape, a.dtype) for a in arrays],
        input_output_aliases={i: i for i in range(count)},
        compiler_params=pltpu.CompilerParams(vmem_limit_bytes=1024 * 1024),
        cost_estimate=SMALL,
        name="hold",
    )(*arrays, after)


def prefix_copies(refs, buf, sem):
    return [
        pltpu.make_async_copy(refs[g], buf.at[pl.ds(4 * g, 4), pl.ds(0, 512)], sem.at[g]) for g in range(8)
    ]


def sum_x(own, from_left, from_right, after):
    def kernel(a, b, c, after_ref, keep, send):
        for i, out in enumerate((keep, send)):
            out[...] = (a[i].astype(F32) + b[i].astype(F32) + c[i].astype(F32)).astype(out.dtype)

    return pl.pallas_call(
        kernel,
        in_specs=[IN_VMEM] * 3 + [ANY],
        out_specs=[IN_VMEM] * 2,
        out_shape=[jax.ShapeDtypeStruct((ROWS, COLS), F32), jax.ShapeDtypeStruct((ROWS, COLS), BF16)],
        compiler_params=pltpu.CompilerParams(vmem_limit_bytes=VMEM),
        cost_estimate=SMALL,
        name="sum_x",
    )(own, from_left, from_right, after)


def rotated(keep_ref, more_ref, bias_ref, cos_ref, sin_ref, first, q_buf):
    cos, sin = cos_ref[first : first + ROWS, :], sin_ref[first : first + ROWS, :]

    def turn(v):
        return v * cos + pltpu.roll(v, HD // 2, 1) * sin

    for h in range(HEADS):
        low, high = h * HD, h * HD + HD
        v = turn(keep_ref[:, low:high] + more_ref[:, low:high].astype(F32) + bias_ref[:, low:high])
        for p in range(32):
            q_buf[32 * p + 4 * h : 32 * p + 4 * h + 4, :] = v[4 * p : 4 * p + 4]
    u = keep_ref[:, QW:] + more_ref[:, QW:].astype(F32) + bias_ref[:, QW:]
    return jnp.concatenate([turn(u[:, :HD]), u[:, HD:]], 1)


def masked_scores(q, keys, valid):
    return jnp.where(valid, dot(q, keys, ((1,), (1,))) * LOG2_SCALE, NEG)


def weigh(s_buf, w_buf, top_buf, sum_buf):
    for g in range(8):
        rows = slice(128 * g, 128 * g + 128)
        s = s_buf[rows, :]
        top = jnp.max(s, -1, keepdims=True)
        w = jnp.exp2(s - top)
        w_buf[rows, :] = w.astype(BF16)
        top_buf[rows, :] = top
        sum_buf[rows, :] = jnp.sum(w, -1, keepdims=True)


def new_block(new_ref_rows):
    return jnp.concatenate([new_ref_rows, jnp.zeros((12, PW), F32)], 0).astype(BF16)


def buffers(keys):
    return [
        pltpu.VMEM((32, keys, PW), BF16),
        pltpu.VMEM((1024, keys), F32),
        pltpu.VMEM((1024, keys), BF16),
        pltpu.VMEM((1024, 1), F32),
        pltpu.VMEM((1024, 1), F32),
    ]


def pack_logs(top_buf, sum_buf):
    lane = lax.broadcasted_iota(jnp.int32, (32, 128), 1)
    packed = jnp.zeros((32, 128), F32)
    for p in range(32):
        rows = slice(32 * p, 32 * p + 32)
        packed = jnp.where(lane == 4 * p, top_buf[rows, :] + jnp.log2(sum_buf[rows, :]), packed)
    return packed


def attend(limits, lengths, order, keep, more, bias, cosine, sine, cache, kvs):
    keys = 512 + 64 + 16

    def kernel(limit_ref, length_ref, at_ref, keep_ref, more_ref, bias_ref, cos_ref, sin_ref, cache_ref, *refs):
        o_ref, buf, s_buf, w_buf, top_buf, sum_buf, qbuf, sem, csem = refs[8:]
        copies = prefix_copies(refs, buf, sem) + [
            pltpu.make_async_copy(cache_ref.at[at_ref[32 + p]], buf.at[p, pl.ds(512, 64)], csem.at[p])
            for p in range(32)
        ]
        for g in range(8):
            for c in [copies[g]] + copies[8 + 4 * g : 12 + 4 * g]:
                c.start()
        new_all = rotated(keep_ref, more_ref, bias_ref, cos_ref, sin_ref, ROWS, qbuf)
        for p in range(32):
            o_ref[p, :, QW:] = new_all[4 * p : 4 * p + 4].astype(BF16)
            buf[p, 576:592, :] = new_block(new_all[4 * p : 4 * p + 4])
        row = lax.broadcasted_iota(jnp.int32, (32, keys), 0)
        col = lax.broadcasted_iota(jnp.int32, (32, keys), 1)
        fresh = (col >= 576) & (col - 576 <= row & 3)
        for p in range(32):
            if p % 4 == 0:
                for c in [copies[p // 4]] + copies[8 + p : 12 + p]:
                    c.wait()
            valid = (col < limit_ref[p]) | ((col >= 512) & (col < 512 + length_ref[32 + p])) | fresh
            rows = slice(32 * p, 32 * p + 32)
            s_buf[rows, :] = masked_scores(qbuf[rows, :].astype(BF16), buf[p, :, :HD], valid)
        weigh(s_buf, w_buf, top_buf, sum_buf)
        for p in range(32):
            rows = slice(32 * p, 32 * p + 32)
            o = dot(w_buf[rows, :], buf[p, :, HD:]) / sum_buf[rows, :]
            for h in range(HEADS):
                o_ref[p, :, h * HD : h * HD + HD] = o[4 * h : 4 * h + 4].astype(BF16)

    return pl.pallas_call(
        kernel,
        in_specs=[IN_SMEM] * 3 + [IN_VMEM] * 5 + [ANY] * 9,
        out_specs=IN_VMEM,
        out_shape=jax.ShapeDtypeStruct((32, 4, COLS), BF16),
        scratch_shapes=buffers(keys)
        + [pltpu.VMEM((1024, HD), F32), pltpu.SemaphoreType.DMA((8,)), pltpu.SemaphoreType.DMA((32,))],
        compiler_params=pltpu.CompilerParams(vmem_limit_bytes=VMEM),
        cost_estimate=SMALL,
        name="attend",
    )(limits, lengths, order, keep, more, bias, cosine, sine, *in_hbm(cache, *kvs))


def make_queries(keep, more, bias, cosine, sine, after):
    def kernel(keep_ref, more_ref, bias_ref, cos_ref, sin_ref, after_ref, q_ref, new_ref, qbuf):
        new_ref[...] = rotated(keep_ref, more_ref, bias_ref, cos_ref, sin_ref, 0, qbuf).astype(BF16)
        q_ref[...] = qbuf[...].astype(BF16).reshape(32, 32, HD)

    return pl.pallas_call(
        kernel,
        in_specs=[IN_VMEM] * 5 + [ANY],
        out_specs=[IN_VMEM] * 2,
        out_shape=[jax.ShapeDtypeStruct((32, 32, HD), BF16), jax.ShapeDtypeStruct((ROWS, PW), BF16)],
        scratch_shapes=[pltpu.VMEM((1024, HD), F32)],
        compiler_params=pltpu.CompilerParams(vmem_limit_bytes=VMEM),
        cost_estimate=SMALL,
        name="make_queries",
    )(keep, more, bias, cosine, sine, after)


def attend_prefix(limits, q, kvs, after):
    keys = 512

    def kernel(limit_ref, q_ref, *refs):
        o_ref, buf, s_buf, w_buf, top_buf, sum_buf, sem = refs[9:]
        copies = prefix_copies(refs, buf, sem)
        for c in copies:
            c.start()
        col = lax.broadcasted_iota(jnp.int32, (32, keys), 1)
        for g in range(8):
            copies[g].wait()
            for p in range(4 * g, 4 * g + 4):
                s_buf[32 * p : 32 * p + 32, :] = masked_scores(q_ref[p], buf[p, :, :HD], col < limit_ref[p])
        weigh(s_buf, w_buf, top_buf, sum_buf)
        for p in range(32):
            rows = slice(32 * p, 32 * p + 32)
            o_ref[p] = (dot(w_buf[rows, :], buf[p, :, HD:]) / sum_buf[rows, :]).astype(BF16)
        rest = pack_logs(top_buf, sum_buf)
        lane = lax.broadcasted_iota(jnp.int32, (32, 128), 1)
        packed = jnp.zeros((32, 128), F32)
        for part in range(3):
            piece = rest.astype(BF16).astype(F32)
            packed = jnp.where(lane % 4 == part, pltpu.roll(piece, part, 1), packed)
            rest = rest - piece
        o_ref[32] = packed.astype(BF16)

    return pl.pallas_call(
        kernel,
        in_specs=[IN_SMEM, IN_VMEM] + [ANY] * 9,
        out_specs=IN_VMEM,
        out_shape=jax.ShapeDtypeStruct((33, 32, HD), BF16),
        scratch_shapes=buffers(keys) + [pltpu.SemaphoreType.DMA((8,))],
        compiler_params=pltpu.CompilerParams(vmem_limit_bytes=VMEM),
        cost_estimate=SMALL,
        name="attend_prefix",
    )(limits, q, *in_hbm(*kvs, after))


def attend_near(lengths, order, q, new, cache, after):
    keys = 64 + 16

    def kernel(
        length_ref, at_ref, q_ref, new_ref, cache_ref, after_ref, o_ref, buf, s_buf, w_buf, top_buf, sum_buf, sem
    ):
        copies = [
            pltpu.make_async_copy(cache_ref.at[at_ref[p]], buf.at[p, pl.ds(0, 64)], sem.at[p])
            for p in range(32)
        ]
        for c in copies:
            c.start()
        for p in range(32):
            buf[p, 64:80, :] = new_block(new_ref[4 * p : 4 * p + 4].astype(F32))
        row = lax.broadcasted_iota(jnp.int32, (32, keys), 0)
        col = lax.broadcasted_iota(jnp.int32, (32, keys), 1)
        fresh = (col >= 64) & (col - 64 <= row & 3)
        for c in copies:
            c.wait()
        for p in range(32):
            valid = (col < length_ref[p]) | fresh
            s_buf[32 * p : 32 * p + 32, :] = masked_scores(q_ref[p], buf[p, :, :HD], valid)
        weigh(s_buf, w_buf, top_buf, sum_buf)
        for p in range(32):
            rows = slice(32 * p, 32 * p + 32)
            o_ref[p] = dot(w_buf[rows, :], buf[p, :, HD:]) / sum_buf[rows, :]
        o_ref[32] = pack_logs(top_buf, sum_buf)

    return pl.pallas_call(
        kernel,
        in_specs=[IN_SMEM] * 2 + [IN_VMEM] * 2 + [ANY] * 2,
        out_specs=IN_VMEM,
        out_shape=pltpu.HBM((33, 32, HD), F32),
        scratch_shapes=buffers(keys) + [pltpu.SemaphoreType.DMA((32,))],
        compiler_params=pltpu.CompilerParams(vmem_limit_bytes=VMEM),
        cost_estimate=SMALL,
        name="attend_near",
    )(lengths, order, q, new, *in_hbm(cache, after))


def merge_rows(order, far, near, new, done):
    def kernel(order_ref, far_ref, near_ref, new_ref, done_ref, out_ref, pair_ref):
        parts = far_ref[32].astype(F32)
        theirs = parts + pltpu.roll(parts, 127, 1) + pltpu.roll(parts, 126, 1)
        ours = near_ref[32]
        top = jnp.maximum(theirs, ours)
        wt, wo = jnp.exp2(theirs - top), jnp.exp2(ours - top)
        share = wt / (wt + wo)
        for p in range(32):
            at = order_ref[p]
            mine = near_ref[p]
            o = mine + (far_ref[p].astype(F32) - mine) * share[:, 4 * p : 4 * p + 1]
            for h in range(HEADS):
                out_ref[at, :, h * HD : h * HD + HD] = o[4 * h : 4 * h + 4].astype(BF16)
            pair_ref[at] = new_ref[p]
            at = order_ref[32 + p]
            out_ref[at] = done_ref[p, :, :QW]
            pair_ref[at] = done_ref[p, :, QW:]

    return pl.pallas_call(
        kernel,
        in_specs=[IN_SMEM] + [IN_VMEM] * 4,
        out_specs=[IN_VMEM] * 2,
        out_shape=[jax.ShapeDtypeStruct((64, 4, QW), BF16), jax.ShapeDtypeStruct((64, 4, PW), BF16)],
        compiler_params=pltpu.CompilerParams(vmem_limit_bytes=VMEM),
        cost_estimate=SMALL,
        name="merge_rows",
    )(order, far, *in_hbm(near), new, done)


def on_device(
    tokens,
    query_weight,
    query_bias,
    pair_weight,
    pair_bias,
    cache_pairs,
    prefix_pairs,
    owner_slot,
    prefix_blocks,
    positions,
):
    prompts, _, new, width = tokens.shape
    me = lax.axis_index("roll")
    my_y, my_z, my_c = me // 8, me // 2 % 4, me % 2
    tp = lax.axis_index("tp")
    tp_y, tp_x = tp // 4, tp % 4
    pos = positions.reshape(prompts)

    own = prefix_pairs.reshape(-1, 512, 2 * HD)
    below, above, own_c = over_roll(own, 0, 1, 0), over_roll(own, 0, 3, 0), over_roll(own, 0, 0, 1)
    far = over_roll(below, 0, 1, 0)

    def heads(*pairs):
        return jnp.stack([(tp_y + dy) % 2 * 4 + (tp_x + dx) % 4 for dy, dx in pairs]).astype(jnp.int32)

    weights = (query_weight, pair_weight)
    x_o, x_m, up_o, down_o, up_m, down_m = project_far(
        heads((0, 2), (1, 2)),
        jnp.stack([my_y, my_z, my_c]).astype(jnp.int32),
        jnp.broadcast_to(owner_slot[:, None], (prompts, new)).reshape(1, prompts * new),
        tokens.reshape(prompts * new, width),
        *weights,
    )
    right_o, left_o, right_m, left_m = project(
        heads((0, 1), (1, 1), (0, 3), (1, 3)), [x_o, x_m], *weights, [[0, 1], [2, 3]], after=(own_c,)
    )
    right_o, left_o = add_far(right_o, left_o, over_tp(up_o, 0, 1), over_tp(down_o, 0, 3), ())
    own_o, own_m = project(heads((0, 0), (1, 0)), [x_o, x_m], *weights, [[0, 1]], after=(right_o, left_o))
    right_m, left_m = add_far(right_m, left_m, over_tp(up_m, 0, 1), over_tp(down_m, 0, 3), (right_o, own_m))

    def reduce(right, left, own_part, after):
        keep, send = sum_x(own_part, over_tp(right, 0, 1), over_tp(left, 0, 3), after)
        return keep, over_tp(send, 1, 0)

    full_o = reduce(right_o, left_o, own_o, right_m)
    full_m = reduce(right_m, left_m, own_m, full_o[0])

    index = jnp.arange(prompts, dtype=jnp.int32)
    half, quarter = jnp.arange(2, dtype=jnp.int32), jnp.arange(4, dtype=jnp.int32)
    y_of, c_of = (1 - half + my_y) % 2, (half + my_c) % 2
    z_of = (jnp.array([0, 3, 1, 2], jnp.int32) + my_z) % 4
    slot = (
        ((y_of[:, None, None, None] * 4 + z_of[None, None, :, None]) * 2 + c_of[None, :, None, None]) * 4
        + quarter[None, None, None, :]
    ).reshape(prompts)
    hit = owner_slot[None, :] == slot[:, None]
    order = jnp.sum(jnp.where(hit, index[None, :], 0), 1)
    limits = BLOCK * jnp.sum(jnp.where(hit, prefix_blocks[None, :], 0), 1)
    lengths = jnp.sum(jnp.where(hit, pos[None, :], 0), 1)
    my_limits = limits[32:]
    at = (limits[:, None] + lengths[:, None] + quarter[None, :]).reshape(prompts * new)
    frequency = jnp.exp(jnp.arange(HD // 2, dtype=F32) * (-2.0 * math.log(ROPE_BASE) / HD))
    angles = at.astype(F32)[:, None] * frequency[None, :]
    cosine, sine = jnp.cos(angles), jnp.sin(angles)
    tables = (
        jnp.concatenate([query_bias, pair_bias]).astype(F32)[None],
        jnp.concatenate([cosine, cosine], 1),
        jnp.concatenate([-sine, sine], 1),
    )
    cache = cache_pairs.reshape(prompts, 64, 2 * HD)

    q_o, new_o = make_queries(*full_o, *tables, full_m[0])
    gathered = hold((below, above, far), q_o)
    kvs = [own, *gathered, own_c] + [over_roll(a, 0, 0, 1) for a in gathered]
    near = attend_near(lengths, order, q_o, new_o, cache, kvs[-1])
    far = over_roll(attend_prefix(my_limits, over_roll(q_o, 1, 0, 0), kvs, near), 1, 0, 0)
    done = attend(my_limits, lengths, order, *full_m, *tables, cache, kvs)
    attended, new_pairs = merge_rows(order, far, near, new_o.reshape(32, new, PW), done)
    return (
        attended.reshape(prompts, 1, new, QW),
        new_pairs.reshape(prompts, 1, new, 1, PW),
    )


def solution(mesh):
    return jax.shard_map(
        on_device,
        mesh=mesh,
        in_specs=(
            P(None, "roll", None, "tp"),
            P("tp", None),
            P("tp"),
            P("tp", None),
            P("tp"),
            P(None, "roll", None, "tp", None),
            P("roll", None, "tp", None),
            P(),
            P(),
            P(None, "roll"),
        ),
        out_specs=(P(None, "roll", None, "tp"), P(None, "roll", None, "tp", None)),
        check_vma=False,
    )
```
